128 devices in a mesh: tm: 32 (over y, z, core), chan: 4 (over x).
Axes of the slice: x: 4, y: 4, z: 4, core: 2. Of those that a mesh axis runs over, the one named last changes fastest.
Arguments:
- latent: bfloat16 [32, 384, 8, 128], P('tm', 'chan'), may hold values from -33 to 33
- clip_ids: int32 [32], replicated, may hold values from 0 to 7, never falling along the last dimension, each value on 1 to 8 neighbouring positions
- gamma_one: float32 [384], P('chan'), may hold values from 0.1 to 1.9
- beta_one: float32 [384], P('chan'), may hold values from -3 to 3
- weight_one: bfloat16 [3, 3, 3, 384, 384], P(None, None, None, 'chan'), may hold values from -0.0625 to 0.0625
- bias_one: float32 [384], P('chan'), may hold values from -2 to 2
- gamma_two: float32 [384], P('chan'), may hold values from 0.1 to 1.9
- beta_two: float32 [384], P('chan'), may hold values from -3 to 3
- weight_two: bfloat16 [3, 3, 3, 384, 384], P(None, None, None, 'chan'), may hold values from -0.0625 to 0.0625
- bias_two: float32 [384], P('chan'), may hold values from -2 to 2
- weight_three: bfloat16 [3, 3, 3, 384, 384], replicated, may hold values from -0.0625 to 0.0625
- bias_three: float32 [384], P('chan'), may hold values from -2 to 2
Outputs:
- decoded: bfloat16 [32, 384, 16, 256], P('tm', 'chan')
The draws below stay inside these ranges and needn't reach their ends.
Inputs may be any that keep to these rules, and one draw needn't show every extreme that they name: `clip_ids`: clip ids never fall along the frames; each clip holds 1 to 8 frames and some clip exactly 8.
All inputs are finite; a program needn't handle non-finite values.
Results may differ from the reference program's by a relative error of at most 0.015.
Values may be sent and summed in bfloat16 or wider, within the bound.
A program may use at most 128 MiB of HBM per device.

```python
import math
import jax
import jax.numpy as jnp
import numpy as np
from jax import lax

C = 384
GROUPS = 32
H = 8
W = 128
MOST_FRAMES = 8
FRAMES = 32
CLIPS = 8
N_CHAN = 4


def draw_latent(key, part):
    key = jax.random.fold_in(key, 11)
    key_base, key_frame, key_chan, key_cell = jax.random.split(key, 4)
    position = jnp.arange(FRAMES, dtype=jnp.float32) / float(max(FRAMES - 1, 1))
    rising = jnp.exp(position * math.log(3.0)) * jax.random.uniform(key_frame, (FRAMES,), jnp.float32, 0.6, 1.6)
    base = jnp.clip(jax.random.normal(key_base, (FRAMES, C, H, W), jnp.float32), -5.0, 5.0)
    chan_scale = jnp.exp(jax.random.uniform(key_chan, (C,), jnp.float32, math.log(0.3), math.log(3.0)))
    cell_scale = jax.random.uniform(key_cell, (H, W), jnp.float32, 0.5, 1.5)
    return (0.3 * base * chan_scale[None, :, None, None] * rising[:, None, None, None] * cell_scale[None, None, :, :]).astype(jnp.bfloat16)


def steps_of(rng, dims, shards, low, top_value):
    level = 1.0
    for axis_at, shards_of in shards:
        heights = jax.random.uniform(jax.random.fold_in(jax.random.fold_in(rng, 6), axis_at), (shards_of,), jnp.float32, low / len(shards), top_value / len(shards))
        level = level * jnp.repeat(jnp.exp(heights), dims[axis_at] // shards_of).reshape((-1,) + (1,) * (len(dims) - 1 - axis_at))
    return level


def profile(number_of, total, reach, slope):
    loads = [(1 << 20) // math.isqrt(rank ** slope) + 1 for rank in range(2, number_of + 1)]
    surplus, given = total - reach - (number_of - 1), [1] * (number_of - 1)
    while surplus > 0:
        candidates = [i for i in range(number_of - 1) if given[i] < reach]
        whole, remaining = sum([loads[i] for i in candidates]), surplus
        for i in candidates:
            more = min(reach - given[i], max(1, remaining * loads[i] // whole), surplus)
            given[i] = given[i] + more
            surplus = surplus - more
    return np.array([reach] + given)


def uneven_parts(key, number_of, total, bound, skew):
    if number_of == 2:
        one = jax.random.randint(key, (), max(1, total - bound), min(bound, total - 1) + 1)
        return jnp.stack([one, total - one])
    tallies = jnp.asarray(profile(number_of, total, bound, skew), jnp.int32)
    twos = (number_of - 1) // 2
    source_of, receiver = tallies[1:1 + 2 * twos:2], tallies[2:2 + 2 * twos:2]
    margin = jnp.minimum(source_of - 1, bound - receiver)
    moved = jax.random.randint(jax.random.fold_in(key, 1), (twos,), 0, 1 << 20) % (margin + 1)
    tallies = tallies.at[1:1 + 2 * twos:2].set(source_of - moved).at[2:2 + 2 * twos:2].set(receiver + moved)
    return tallies[jax.random.permutation(jax.random.fold_in(key, 2), number_of)]


def gaussian(stream_key, extent, deviation, most, cuts=(), held_as=jnp.bfloat16):
    loudness = steps_of(stream_key, extent, cuts, -0.22, 0.18) if cuts else 1.0
    values = jax.random.normal(stream_key, extent, jnp.float32) * deviation * loudness
    return jnp.minimum(jnp.maximum(values, -most), most).astype(held_as)


def setup_inputs(seed: int = 0) -> dict:
    keys = jax.random.split(jax.random.key(seed), 13)
    return {
        "latent": draw_latent(jax.random.fold_in(keys[12], 71), 0),
        "clip_ids": jnp.searchsorted(jnp.cumsum(uneven_parts(keys[1], CLIPS, FRAMES, MOST_FRAMES, 1)), jnp.arange(FRAMES), side="right").astype(jnp.int32),
        "gamma_one": jnp.clip(1.0 + 0.18 * jax.random.normal(keys[2], (C,), jnp.float32), 0.1, 1.9),
        "beta_one": gaussian(keys[3], (C,), 0.5, 3.0, ((0, 4),), jnp.float32),
        "weight_one": gaussian(keys[4], (3, 3, 3, C, C), (27 * C) ** -0.5, 0.0625, ((3, 4),)),
        "bias_one": gaussian(keys[5], (C,), 0.3, 2.0, ((0, 4),), jnp.float32),
        "gamma_two": jnp.clip(1.0 + 0.18 * jax.random.normal(keys[6], (C,), jnp.float32), 0.1, 1.9),
        "beta_two": gaussian(keys[7], (C,), 0.5, 3.0, ((0, 4),), jnp.float32),
        "weight_two": gaussian(keys[8], (3, 3, 3, C, C), (27 * C) ** -0.5, 0.0625, ((3, 4),)),
        "bias_two": gaussian(keys[9], (C,), 0.3, 2.0, ((0, 4),), jnp.float32),
        "weight_three": gaussian(keys[10], (3, 3, 3, C, C), (27 * C) ** -0.5, 0.0625),
        "bias_three": gaussian(keys[11], (C,), 0.3, 2.0, ((0, 4),), jnp.float32),
    }


EPSILON = 1e-06

def window_mask(clip_ids, frame_idx):
    offsets = jnp.array([2, 1, 0], dtype=jnp.int32)
    source = frame_idx - offsets
    clamped = jnp.maximum(source, 0)
    matches = clip_ids[clamped] == clip_ids[frame_idx]
    return ((source >= 0) & matches).astype(jnp.bfloat16)

def spatial_conv(window, weights):
    frames_in, inputs, height, breadth = window.shape
    outputs = weights.shape[4]
    padded = jnp.pad(window, ((0, 0), (0, 0), (1, 1), (1, 1)))
    summed = jnp.zeros((outputs, height * breadth), jnp.float32)
    for row_tap in range(3):
        for col_tap in range(3):
            patches = padded[:, :, row_tap:row_tap + height, col_tap:col_tap + breadth].reshape(frames_in * inputs, height * breadth)
            matrix = weights[:, row_tap, col_tap].reshape(frames_in * inputs, outputs)
            summed = summed + jnp.dot(matrix.T, patches, preferred_element_type=jnp.float32)
    return summed

def enlarge(window):
    return jnp.repeat(jnp.repeat(window, 2, axis=2), 2, axis=3)

def group_norm_silu(values, clip_ids, gain, offset):
    frames, channels, height, breadth = values.shape
    per_group = channels // GROUPS
    grouped = values.reshape(frames, GROUPS, per_group * height * breadth)
    firsts = lax.optimization_barrier(jnp.sum(grouped, 2))
    seconds = lax.optimization_barrier(jnp.sum(grouped * grouped, 2))
    onehot = (clip_ids[:, None] == jnp.arange(CLIPS, dtype=jnp.int32)[None, :]).astype(jnp.float32)
    highest = lax.Precision.HIGHEST
    frame_first = jnp.dot(onehot, jnp.dot(onehot.T, firsts, precision=highest), precision=highest)
    frame_second = jnp.dot(onehot, jnp.dot(onehot.T, seconds, precision=highest), precision=highest)
    frame_count = jnp.dot(onehot, lax.optimization_barrier(jnp.sum(onehot, 0)), precision=highest) * float(per_group * height * breadth)
    average = frame_first / frame_count[:, None]
    variance = frame_second / frame_count[:, None] - average * average
    normed = (grouped - average[:, :, None]) * lax.rsqrt(variance + EPSILON)[:, :, None]
    normed = normed.reshape(values.shape) * gain[None, :, None, None] + offset[None, :, None, None]
    return jax.nn.silu(normed).astype(jnp.bfloat16)

def reference(latent, clip_ids, gamma_one, beta_one, weight_one, bias_one, gamma_two, beta_two, weight_two, bias_two, weight_three, bias_three):
    frames, channels, height, breadth = latent.shape
    portion = channels // N_CHAN

    def causal_conv(activation, weights, split):
        padded = jnp.concatenate([jnp.zeros((2,) + activation.shape[1:], activation.dtype), activation], 0)

        def per_frame(frame_idx):
            window = lax.dynamic_slice_in_dim(padded, frame_idx, 3, 0) * window_mask(clip_ids, frame_idx)[:, None, None, None]
            if split:
                summed = jnp.zeros((channels, height * breadth), jnp.float32)
                for part_idx in range(N_CHAN):
                    lower = part_idx * portion
                    partial_term = spatial_conv(window[:, lower:lower + portion], weights[:, :, :, lower:lower + portion])
                    rounded = lax.optimization_barrier(partial_term.astype(jnp.bfloat16))
                    summed = summed + rounded.astype(jnp.float32)
                return summed
            return spatial_conv(enlarge(window), weights)
        return lax.map(per_frame, jnp.arange(frames, dtype=jnp.int32))
    act_one = group_norm_silu(latent.astype(jnp.float32), clip_ids, gamma_one, beta_one)
    sums_one = causal_conv(act_one, weight_one, True)
    hidden_one = (sums_one + bias_one[None, :, None]).reshape(latent.shape).astype(jnp.bfloat16)
    act_two = group_norm_silu(hidden_one.astype(jnp.float32), clip_ids, gamma_two, beta_two)
    sums_two = causal_conv(act_two, weight_two, True)
    residual = (latent.astype(jnp.float32) + (sums_two + bias_two[None, :, None]).reshape(latent.shape)).astype(jnp.bfloat16)
    sums_three = causal_conv(residual, weight_three, False)
    decoded = (sums_three + bias_three[None, :, None]).reshape(frames, channels, 2 * height, 2 * breadth)
    return decoded.astype(jnp.bfloat16)
```

```python
import functools

import jax
import jax.numpy as jnp
from jax import lax
from jax.experimental import pallas as pl
from jax.experimental.pallas import tpu as pltpu
from jax.sharding import PartitionSpec as P

C = 384
GROUPS = 32
PER_GROUP = C // GROUPS
Q = 96
H = 8
W = 128
CELLS = H * W
NCH = 4
CW = CELLS // NCH
REACH = 7
KP = 896
EPSILON = 1e-06
MESH = pl.DeviceIdType.MESH
BF = jnp.bfloat16
F32 = jnp.float32
OFFSETS = [d for d in range(-REACH, REACH + 1) if d != 0]


def kernel(
    nt,
    nc,
    lat_hbm,
    clip,
    gamma1,
    beta1,
    w1,
    bias1,
    gamma2,
    beta2,
    w2,
    bias2,
    w3,
    bias3,
    out,
    lat_raw,
    lat32,
    flat,
    halo,
    prm,
    tmp,
    colp,
    st_send,
    st_recv,
    wv1,
    wv2,
    wt1,
    wt2,
    w3v,
    t3,
    wf,
    act,
    yb,
    sb,
    rb,
    x3,
    oscr,
    loc_sem,
    w_sem,
    hs_sem,
    hr_sem,
    ss_sem,
    sr_sem,
    rs_sem,
    rr_sem,
    as_sem,
    ar_sem,
    zs_sem,
    zr_sem,
    xs_sem,
    xr_sem,
    bs_sem,
    br_sem,
):
    t = lax.axis_index("tm")
    c = lax.axis_index("chan")
    core = lax.rem(t, 2)

    def tm(d):
        return (lax.rem(t + d + nt, nt), c)

    def xp(d):
        return (t, lax.rem(c + d, nc))

    def quarter(d):
        return pl.ds(pl.multiple_of(lax.rem(c + d, nc) * Q, Q), Q)

    def remote(src, dst, ssem, rsem, dev):
        return pltpu.make_async_remote_copy(
            src_ref=src, dst_ref=dst, send_sem=ssem, recv_sem=rsem, device_id=dev, device_id_type=MESH
        )

    def arrived(dst, ssem, rsem):
        remote(dst, dst, ssem, rsem, xp(1)).wait_recv()

    loads = [pltpu.make_async_copy(lat_hbm.at[0], lat_raw, loc_sem.at[0])]
    for cp in loads:
        cp.start()
    wloads = [[], []]
    for s, (src, dst) in enumerate(((w1, wv1), (w2, wv2))):
        for f in range(3):
            for a in range(3):
                wloads[s].append(
                    pltpu.make_async_copy(
                        src.at[f, a], dst.at[:, pl.ds((a * 3 + f) * Q, Q), :], w_sem.at[s * 9 + f * 3 + a]
                    )
                )
    for cp in wloads[0] + wloads[1]:
        cp.start()
    half = c // 2
    w3load = pltpu.make_async_copy(
        w3.at[:, :, :, :, pl.ds(pl.multiple_of(half * 128, 128), 256)], w3v, w_sem.at[18]
    )
    w3load.start()

    prm[...] = jnp.zeros_like(prm)
    for r, ref in enumerate((gamma1, beta1, bias1, gamma2, beta2, bias2, bias3)):
        prm[r : r + 1, 0:Q] = ref[...]

    zero = jnp.zeros((3, C, W), BF)
    x3[:, :, 0:W] = zero
    x3[:, :, W + CELLS : 2 * W + CELLS] = zero
    act[...] = jnp.zeros_like(act)
    for dst in (wv1, wv2):
        dst[:, 9 * Q : KP, :] = jnp.zeros((3, KP - 9 * Q, C), BF)
    tmp[...] = jnp.zeros_like(tmp)

    barrier = pltpu.get_barrier_semaphore()
    for d in OFFSETS:
        pl.semaphore_signal(barrier, inc=1, device_id=tm(d), device_id_type=MESH)
    for d in range(1, nc):
        pl.semaphore_signal(barrier, inc=1, device_id=xp(d), device_id_type=MESH)

    for cp in loads:
        cp.wait()
    lat32[...] = lat_raw[...].astype(F32).reshape(Q * H, W)

    def frame_sums(slot, p1, p2):
        tmp[0:Q, :] = p1
        s1 = jnp.sum(tmp[...].T, axis=0, keepdims=True)
        tmp[0:Q, :] = p2
        s2 = jnp.sum(tmp[...].T, axis=0, keepdims=True)
        st_send[slot] = jnp.concatenate([s1, s2, jnp.zeros((6, 128), F32)], 0)

    p1 = jnp.zeros((Q, W), F32)
    p2 = jnp.zeros((Q, W), F32)
    for i in range(H):
        row = lat32[pl.ds(i, Q, stride=H), :]
        p1 = p1 + row
        p2 = p2 + row * row
        flat[0, :, i * W : (i + 1) * W] = row.astype(BF)
    frame_sums(0, p1, p2)
    colp[...] = prm[...].T

    pl.semaphore_wait(barrier, len(OFFSETS) + nc - 1)

    def stats_copies(s):
        return [
            remote(st_send.at[s], st_recv.at[s, k], ss_sem.at[s, k], sr_sem.at[s, k], tm(d))
            for k, d in enumerate(OFFSETS)
        ]

    def halo_copy(s, k, ch):
        lanes = pl.ds(pl.multiple_of(ch * CW, CW), CW)
        return remote(
            flat.at[s, :, lanes], halo.at[s, k, :, lanes], hs_sem.at[s, k, ch], hr_sem.at[s, k, ch], tm(2 - k)
        )

    own_clip = clip[t]
    valid = []
    for d in (2, 1):
        src = lax.rem(t - d + nt, nt)
        valid.append(jnp.where((t - d >= 0) & (clip[src] == own_clip), 1.0, 0.0).astype(F32))
    valid.append(jnp.float32(1.0))

    lane = lax.broadcasted_iota(jnp.int32, (128, 128), 1)
    subl = lax.broadcasted_iota(jnp.int32, (128, 128), 0)
    ga = jnp.floor((subl.astype(F32) + 0.5) * (1.0 / PER_GROUP))
    gb = jnp.floor((lane.astype(F32) + 0.5) * (1.0 / PER_GROUP))
    gmat = jnp.where(ga == gb, 1.0, 0.0).astype(F32)

    def norm_params(s):
        total = st_send[s]
        frames = jnp.float32(1.0)
        for k, d in enumerate(OFFSETS):
            arrived(st_recv.at[s, k], ss_sem.at[s, k], sr_sem.at[s, k])
            src = lax.rem(t - d + nt, nt)
            inside = (t - d >= 0) & (t - d < nt)
            m = jnp.where(inside & (clip[src] == own_clip), 1.0, 0.0).astype(F32)
            total = total + m * st_recv[s, k]
            frames = frames + m
        grouped = jnp.dot(total, gmat, precision=lax.Precision.HIGHEST, preferred_element_type=F32)
        tmp[0:8, :] = grouped
        cols = tmp[...].T
        count = frames * float(PER_GROUP * CELLS)
        mean = cols[0:Q, 0:1] / count
        var = cols[0:Q, 1:2] / count - mean * mean
        inv = lax.rsqrt(var + EPSILON)
        return mean, inv * colp[0:Q, 3 * s : 3 * s + 1], colp[0:Q, 3 * s + 1 : 3 * s + 2]

    def fill_act(s, mean, scale, shift):
        mean = jnp.broadcast_to(mean, (Q, W))
        scale = jnp.broadcast_to(scale, (Q, W))
        shift = jnp.broadcast_to(shift, (Q, W))
        for f in (2, 1, 0):
            for i in range(H):
                cells = slice(i * W, (i + 1) * W)
                v = (flat[s, :, cells] if f == 2 else halo[s, f, :, cells]).astype(F32)
                u = (v - mean) * scale + shift
                u = u / (1.0 + jnp.exp(-u))
                if f < 2:
                    u = u * valid[f]
                u = u.astype(BF)
                for a in range(3):
                    o = i + 1 - a
                    if 0 <= o < H:
                        k = (a * 3 + f) * Q
                        act[o // 2, k : k + Q, (o % 2) * W : (o % 2 + 1) * W] = u

    first = lax.broadcasted_iota(jnp.int32, (C, W), 1) == 0
    last = lax.broadcasted_iota(jnp.int32, (C, W), 1) == W - 1

    def sums_copy(s, d, ch):
        return remote(
            sb.at[s, ch, quarter(d), :], rb.at[s, ch, d - 1], rs_sem.at[s, d - 1, ch], rr_sem.at[s, d - 1, ch], xp(d)
        )

    def conv(s, wt):
        def chunk(ch, carry):
            yb[...] = jnp.dot(wt[...], act[ch], preferred_element_type=F32)
            for h in range(2):
                cells = slice(h * W, (h + 1) * W)
                left = jnp.where(first, 0.0, pltpu.roll(yb[0:C, cells], 1, 1))
                right = jnp.where(last, 0.0, pltpu.roll(yb[2 * C : 3 * C, cells], W - 1, 1))
                sb[s, ch, :, cells] = (yb[C : 2 * C, cells] + left + right).astype(BF)
            for d in (2, 1, 3):
                sums_copy(s, d, ch).start()
            return carry

        lax.fori_loop(0, NCH, chunk, 0)

    def gathered(s, ch):
        for d in (1, 2, 3):
            arrived(rb.at[s, ch, d - 1], rs_sem.at[s, d - 1, ch], rr_sem.at[s, d - 1, ch])
        total = sb[s, ch, quarter(0), :].astype(F32)
        for d in (1, 2, 3):
            total = total + rb[s, ch, d - 1].astype(F32)
        return total + colp[0:Q, 3 * s + 2 : 3 * s + 3]

    def prep_conv(src, dst):
        for b in range(3):
            dst[b * C : (b + 1) * C, :] = src[b].T

    offset = pl.multiple_of(c * Q - half * 128, 32)

    def prep_three(f):
        taps = {}
        for a in range(3):
            for b in range(3):
                t3[a * 3 + b] = w3v[f, a, b].T
        m = valid[f]

        def tap(a, b):
            return t3[a * 3 + b, pl.ds(offset, Q), :].astype(F32)

        for pi in range(2):
            for block, di in enumerate((0, 1) if pi else (0, -1)):
                rows = ((0, 1), (2,))[block] if pi else ((1, 2), (0,))[block]
                sums = []
                for b in range(3):
                    v = tap(rows[0], b)
                    for a in rows[1:]:
                        v = v + tap(a, b)
                    sums.append(v * m if f < 2 else v)
                parts = (sums[0], sums[1] + sums[2], sums[0] + sums[1], sums[2])
                for k, part in enumerate(parts):
                    base = ((pi * 2 + block) * 4 + k) * Q
                    wf[base : base + Q, f * C : (f + 1) * C] = part.astype(BF)

    for cp in stats_copies(0):
        cp.start()
    for ch in range(NCH):
        for k in range(2):
            halo_copy(0, k, ch).start()
    for cp in wloads[0]:
        cp.wait()
    prep_conv(wv1, wt1)
    params = norm_params(0)
    for ch in range(NCH):
        for k in range(2):
            arrived(halo.at[0, k, :, pl.ds(ch * CW, CW)], hs_sem.at[0, k, ch], hr_sem.at[0, k, ch])
    fill_act(0, *params)
    conv(0, wt1)
    for cp in wloads[1]:
        cp.wait()
    prep_conv(wv2, wt2)
    w3load.wait()

    p1 = jnp.zeros((Q, W), F32)
    p2 = jnp.zeros((Q, W), F32)
    for ch in range(NCH):
        if ch < 3:
            prep_three(ch)
        hidden = gathered(0, ch).astype(BF)
        flat[1, :, ch * CW : (ch + 1) * CW] = hidden
        for k in range(2):
            halo_copy(1, k, ch).start()
        hidden = hidden.astype(F32)
        for h in range(2):
            row = hidden[:, h * W : (h + 1) * W]
            p1 = p1 + row
            p2 = p2 + row * row
    frame_sums(1, p1, p2)
    for cp in stats_copies(1):
        cp.start()

    params = norm_params(1)
    for ch in range(NCH):
        for k in range(2):
            arrived(halo.at[1, k, :, pl.ds(ch * CW, CW)], hs_sem.at[1, k, ch], hr_sem.at[1, k, ch])
    fill_act(1, *params)
    conv(1, wt2)

    def lanes_of(ch):
        return pl.ds(W + ch * CW, CW)

    def own_x(d, ch):
        spot = x3.at[2, quarter(0), lanes_of(ch)]
        return remote(spot, spot, as_sem.at[d - 1, ch], ar_sem.at[d - 1, ch], xp(d))

    def own_z(k, ch):
        return remote(
            x3.at[2, quarter(2 * k), lanes_of(ch)],
            x3.at[0, quarter(2 * k), lanes_of(ch)],
            zs_sem.at[k, ch],
            zr_sem.at[k, ch],
            tm(2),
        )

    def back_x(d, ch):
        spot = x3.at[0, quarter(0), lanes_of(ch)]
        return remote(spot, spot, xs_sem.at[d // 2, ch], xr_sem.at[d // 2, ch], xp(d))

    def across(ch):
        return remote(
            x3.at[2 - 2 * core, :, lanes_of(ch)],
            x3.at[1, :, lanes_of(ch)],
            bs_sem.at[ch],
            br_sem.at[ch],
            (t + 1 - 2 * core, c),
        )

    for ch in range(NCH):
        cells = slice(ch * CW, (ch + 1) * CW)
        residual = flat[0, :, cells].astype(F32) + gathered(1, ch)
        x3[2, quarter(0), W + ch * CW : W + (ch + 1) * CW] = residual.astype(BF)
        own_z(0, ch).start()
        for d in (2, 1, 3):
            own_x(d, ch).start()
    for ch in range(NCH):
        arrived(x3.at[2, quarter(2), lanes_of(ch)], as_sem.at[1, ch], ar_sem.at[1, ch])
        own_z(1, ch).start()
        arrived(x3.at[0, quarter(0), lanes_of(ch)], zs_sem.at[0, ch], zr_sem.at[0, ch])
        for d in (1, 3):
            back_x(d, ch).start()
    for ch in range(NCH):
        for d in (1, 3):
            arrived(x3.at[2, quarter(4 - d), lanes_of(ch)], as_sem.at[d - 1, ch], ar_sem.at[d - 1, ch])
        arrived(x3.at[0, quarter(2), lanes_of(ch)], zs_sem.at[1, ch], zr_sem.at[1, ch])
        for d in (1, 3):
            arrived(x3.at[0, quarter(4 - d), lanes_of(ch)], xs_sem.at[d // 2, ch], xr_sem.at[d // 2, ch])
        across(ch).start()
    for ch in range(NCH):
        arrived(x3.at[1, :, lanes_of(ch)], bs_sem.at[ch], br_sem.at[ch])

    er = lax.broadcasted_iota(jnp.int32, (256, 256), 0)
    ec = lax.broadcasted_iota(jnp.int32, (256, 256), 1)
    perm = jnp.where(jnp.where(er < 128, 2 * er, 2 * er - 255) == ec, 1.0, 0.0).astype(BF)
    bias = colp[0:Q, 6:7]
    first = first[0:Q]
    last = last[0:Q]

    def last_chunk(ch, carry):
        def window(di):
            return x3[:, :, pl.ds(pl.multiple_of((1 + di) * W + ch * CW, W), CW)].reshape(3 * C, CW)

        mid = window(0)
        for pi in range(2):
            edge = window(1 if pi else -1)
            base = pi * 8 * Q
            y = jnp.dot(wf[base : base + C, :], mid, preferred_element_type=F32)
            y = y + jnp.dot(wf[base + C : base + 2 * C, :], edge, preferred_element_type=F32)
            for h in range(2):
                cells = slice(h * W, (h + 1) * W)
                left = jnp.where(first, 0.0, pltpu.roll(y[0:Q, cells], 1, 1))
                right = jnp.where(last, 0.0, pltpu.roll(y[3 * Q : 4 * Q, cells], W - 1, 1))
                even = y[Q : 2 * Q, cells] + left + bias
                odd = y[2 * Q : 3 * Q, cells] + right + bias
                both = jnp.concatenate([even, odd], 1).astype(BF)
                spread = jnp.dot(both, perm, preferred_element_type=F32)
                line = ch * 4 + 2 * h + pi
                for g in range(2):
                    oscr[g, pl.ds(line, Q, stride=2 * H), :] = spread[:, g * 128 : (g + 1) * 128]
        return carry

    lax.fori_loop(0, NCH, last_chunk, 0)
    for g in range(2):
        out[0, :, :, g * 128 : (g + 1) * 128] = oscr[g].reshape(Q, 2 * H, 128).astype(BF)

    for s in range(2):
        for cp in stats_copies(s):
            cp.wait_send()
        for ch in range(NCH):
            for k in range(2):
                halo_copy(s, k, ch).wait_send()
            for d in (1, 2, 3):
                sums_copy(s, d, ch).wait_send()
    for ch in range(NCH):
        for d in (1, 2, 3):
            own_x(d, ch).wait_send()
        for k in range(2):
            own_z(k, ch).wait_send()
        for d in (1, 3):
            back_x(d, ch).wait_send()
        across(ch).wait_send()


def on_device(nt, nc, *args):
    args = [a.reshape(1, Q) if a.ndim == 1 and a.dtype == F32 else a for a in args]
    anywhere = pl.BlockSpec(memory_space=pl.ANY)
    specs = [pl.BlockSpec(memory_space=pltpu.VMEM) if a.ndim == 2 else anywhere for a in args]
    specs[1] = pl.BlockSpec(memory_space=pltpu.SMEM)
    dma = pltpu.SemaphoreType.DMA
    scratch = [
        pltpu.VMEM((Q, H, W), BF),
        pltpu.VMEM((Q * H, W), F32),
        pltpu.VMEM((2, Q, CELLS), BF),
        pltpu.VMEM((2, 2, Q, CELLS), BF),
        pltpu.VMEM((128, 128), F32),
        pltpu.VMEM((128, 128), F32),
        pltpu.VMEM((128, 128), F32),
        pltpu.VMEM((2, 8, 128), F32),
        pltpu.VMEM((2, len(OFFSETS), 8, 128), F32),
        pltpu.VMEM((3, KP, C), BF),
        pltpu.VMEM((3, KP, C), BF),
        pltpu.VMEM((3 * C, KP), BF),
        pltpu.VMEM((3 * C, KP), BF),
        pltpu.VMEM((3, 3, 3, C, 256), BF),
        pltpu.VMEM((9, 256, C), BF),
        pltpu.VMEM((16 * Q, 3 * C), BF),
        pltpu.VMEM((NCH, KP, CW), BF),
        pltpu.VMEM((3 * C, CW), F32),
        pltpu.VMEM((2, NCH, C, CW), BF),
        pltpu.VMEM((2, NCH, 3, Q, CW), BF),
        pltpu.VMEM((3, C, CELLS + 2 * W), BF),
        pltpu.VMEM((2, Q * 2 * H, 128), F32),
        dma((1,)),
        dma((19,)),
        dma((2, 2, NCH)),
        dma((2, 2, NCH)),
        dma((2, len(OFFSETS))),
        dma((2, len(OFFSETS))),
        dma((2, 3, NCH)),
        dma((2, 3, NCH)),
        dma((3, NCH)),
        dma((3, NCH)),
        dma((2, NCH)),
        dma((2, NCH)),
        dma((2, NCH)),
        dma((2, NCH)),
        dma((NCH,)),
        dma((NCH,)),
    ]
    return pl.pallas_call(
        functools.partial(kernel, nt, nc),
        out_shape=jax.ShapeDtypeStruct((1, Q, 2 * H, 2 * W), BF),
        in_specs=specs,
        out_specs=pl.BlockSpec(memory_space=pltpu.VMEM),
        scratch_shapes=scratch,
        compiler_params=pltpu.CompilerParams(
            collective_id=0, has_side_effects=True, vmem_limit_bytes=60 * 1024 * 1024
        ),
    )(*args)


def solution(mesh):
    in_specs = (
        P("tm", "chan", None, None),
        P(),
        P("chan"),
        P("chan"),
        P(None, None, None, "chan", None),
        P("chan"),
        P("chan"),
        P("chan"),
        P(None, None, None, "chan", None),
        P("chan"),
        P(),
        P("chan"),
    )
    return jax.shard_map(
        functools.partial(on_device, mesh.shape["tm"], mesh.shape["chan"]),
        mesh=mesh,
        in_specs=in_specs,
        out_specs=P("tm", "chan", None, None),
        check_vma=False,
    )
```

```python
import functools

import jax
import jax.numpy as jnp
from jax import lax
from jax.experimental import pallas as pl
from jax.experimental.pallas import tpu as pltpu
from jax.sharding import PartitionSpec as P

C = 384
GROUPS = 32
PER_GROUP = C // GROUPS
Q = 96
H = 8
W = 128
CELLS = H * W
NCH = 4
CW = CELLS // NCH
REACH = 7
KP = 896
EPSILON = 1e-06
MESH = pl.DeviceIdType.MESH
BF = jnp.bfloat16
F32 = jnp.float32
OFFSETS = [d for d in range(-REACH, REACH + 1) if d != 0]


def kernel(
    nt,
    nc,
    lat_hbm,
    clip,
    gamma1,
    beta1,
    w1,
    bias1,
    gamma2,
    beta2,
    w2,
    bias2,
    w3,
    bias3,
    out,
    lat_raw,
    lat32,
    flat,
    halo,
    prm,
    tmp,
    colp,
    st_send,
    st_recv,
    wv1,
    wv2,
    wt1,
    wt2,
    w3v,
    t3,
    wf,
    act,
    yb,
    sb,
    rb,
    x3,
    y3,
    both,
    perm,
    oscr,
    loc_sem,
    w_sem,
    hs_sem,
    hr_sem,
    ss_sem,
    sr_sem,
    rs_sem,
    rr_sem,
    as_sem,
    ar_sem,
    zs_sem,
    zr_sem,
    xs_sem,
    xr_sem,
    bs_sem,
    br_sem,
):
    t = lax.axis_index("tm")
    c = lax.axis_index("chan")
    core = lax.rem(t, 2)

    def tm(d):
        return (lax.rem(t + d + nt, nt), c)

    def xp(d):
        return (t, lax.rem(c + d, nc))

    def quarter(d):
        return pl.ds(pl.multiple_of(lax.rem(c + d, nc) * Q, Q), Q)

    def remote(src, dst, ssem, rsem, dev):
        return pltpu.make_async_remote_copy(
            src_ref=src, dst_ref=dst, send_sem=ssem, recv_sem=rsem, device_id=dev, device_id_type=MESH
        )

    def arrived(dst, ssem, rsem):
        remote(dst, dst, ssem, rsem, xp(1)).wait_recv()

    loads = [pltpu.make_async_copy(lat_hbm.at[0], lat_raw, loc_sem.at[0])]
    for cp in loads:
        cp.start()
    wloads = [[], []]
    for s, (src, dst) in enumerate(((w1, wv1), (w2, wv2))):
        for f in range(3):
            for a in range(3):
                wloads[s].append(
                    pltpu.make_async_copy(
                        src.at[f, a], dst.at[:, pl.ds((a * 3 + f) * Q, Q), :], w_sem.at[s * 9 + f * 3 + a]
                    )
                )
    for cp in wloads[0] + wloads[1]:
        cp.start()
    half = c // 2
    w3load = pltpu.make_async_copy(
        w3.at[:, :, :, :, pl.ds(pl.multiple_of(half * 128, 128), 256)], w3v, w_sem.at[18]
    )
    w3load.start()

    prm[...] = jnp.zeros_like(prm)
    for r, ref in enumerate((gamma1, beta1, bias1, gamma2, beta2, bias2, bias3)):
        prm[r : r + 1, 0:Q] = ref[...]

    zero = jnp.zeros((3, C, W), BF)
    x3[:, :, 0:W] = zero
    x3[:, :, W + CELLS : 2 * W + CELLS] = zero
    act[...] = jnp.zeros_like(act)
    for dst in (wv1, wv2):
        dst[:, 9 * Q : KP, :] = jnp.zeros((3, KP - 9 * Q, C), BF)
    tmp[...] = jnp.zeros_like(tmp)
    er = lax.broadcasted_iota(jnp.int32, (2 * W, 2 * W), 0)
    ec = lax.broadcasted_iota(jnp.int32, (2 * W, 2 * W), 1)
    perm[...] = jnp.where(jnp.where(er < W, 2 * er, 2 * er - 2 * W + 1) == ec, 1.0, 0.0).astype(BF)

    barrier = pltpu.get_barrier_semaphore()
    for d in OFFSETS:
        pl.semaphore_signal(barrier, inc=1, device_id=tm(d), device_id_type=MESH)
    for d in range(1, nc):
        pl.semaphore_signal(barrier, inc=1, device_id=xp(d), device_id_type=MESH)

    for cp in loads:
        cp.wait()
    lat32[...] = lat_raw[...].astype(F32).reshape(Q * H, W)

    def frame_sums(slot, p1, p2):
        tmp[0:Q, :] = p1
        s1 = jnp.sum(tmp[...].T, axis=0, keepdims=True)
        tmp[0:Q, :] = p2
        s2 = jnp.sum(tmp[...].T, axis=0, keepdims=True)
        st_send[slot] = jnp.concatenate([s1, s2, jnp.zeros((6, 128), F32)], 0)

    p1 = jnp.zeros((Q, W), F32)
    p2 = jnp.zeros((Q, W), F32)
    for i in range(H):
        row = lat32[pl.ds(i, Q, stride=H), :]
        p1 = p1 + row
        p2 = p2 + row * row
        flat[0, :, i * W : (i + 1) * W] = row.astype(BF)
    frame_sums(0, p1, p2)
    colp[...] = prm[...].T

    pl.semaphore_wait(barrier, len(OFFSETS) + nc - 1)

    def stats_copies(s):
        return [
            remote(st_send.at[s], st_recv.at[s, k], ss_sem.at[s, k], sr_sem.at[s, k], tm(d))
            for k, d in enumerate(OFFSETS)
        ]

    def halo_copy(s, k, ch):
        lanes = pl.ds(pl.multiple_of(ch * CW, CW), CW)
        return remote(
            flat.at[s, :, lanes], halo.at[s, k, :, lanes], hs_sem.at[s, k, ch], hr_sem.at[s, k, ch], tm(2 - k)
        )

    own_clip = clip[t]
    valid = []
    for d in (2, 1):
        src = lax.rem(t - d + nt, nt)
        valid.append(jnp.where((t - d >= 0) & (clip[src] == own_clip), 1.0, 0.0).astype(F32))
    valid.append(jnp.float32(1.0))

    lane = lax.broadcasted_iota(jnp.int32, (128, 128), 1)
    subl = lax.broadcasted_iota(jnp.int32, (128, 128), 0)
    ga = jnp.floor((subl.astype(F32) + 0.5) * (1.0 / PER_GROUP))
    gb = jnp.floor((lane.astype(F32) + 0.5) * (1.0 / PER_GROUP))
    gmat = jnp.where(ga == gb, 1.0, 0.0).astype(F32)

    def norm_params(s):
        total = st_send[s]
        frames = jnp.float32(1.0)
        for k, d in enumerate(OFFSETS):
            arrived(st_recv.at[s, k], ss_sem.at[s, k], sr_sem.at[s, k])
            src = lax.rem(t - d + nt, nt)
            inside = (t - d >= 0) & (t - d < nt)
            m = jnp.where(inside & (clip[src] == own_clip), 1.0, 0.0).astype(F32)
            total = total + m * st_recv[s, k]
            frames = frames + m
        grouped = jnp.dot(total, gmat, precision=lax.Precision.HIGHEST, preferred_element_type=F32)
        tmp[0:8, :] = grouped
        cols = tmp[...].T
        count = frames * float(PER_GROUP * CELLS)
        mean = cols[0:Q, 0:1] / count
        var = cols[0:Q, 1:2] / count - mean * mean
        inv = lax.rsqrt(var + EPSILON)
        return mean, inv * colp[0:Q, 3 * s : 3 * s + 1], colp[0:Q, 3 * s + 1 : 3 * s + 2]

    def fill_rows(s, f, ch, params):
        for r in range(2):
            cells = pl.ds(pl.multiple_of(ch * CW + r * W, W), W)
            v = (flat[s, :, cells] if f == 2 else halo[s, f, :, cells]).astype(F32)
            u = (v - params[0]) * params[1] + params[2]
            u = u / (1.0 + jnp.exp(-u))
            if f < 2:
                u = u * valid[f]
            u = u.astype(BF)
            for a in range(3):
                o = r + 1 - a
                k = (a * 3 + f) * Q
                act[ch + 1 + o // 2, k : k + Q, (o % 2) * W : (o % 2 + 1) * W] = u

    first = lax.broadcasted_iota(jnp.int32, (C, W), 1) == 0
    last = lax.broadcasted_iota(jnp.int32, (C, W), 1) == W - 1

    def sums_copy(s, d, ch):
        return remote(
            sb.at[s, ch, quarter(d), :], rb.at[s, ch, d - 1], rs_sem.at[s, d - 1, ch], rr_sem.at[s, d - 1, ch], xp(d)
        )

    def conv(s, wt, params):
        params = [jnp.broadcast_to(p, (Q, W)) for p in params]
        for ch in range(NCH):
            fill_rows(s, 2, ch, params)

        def chunk(step, carry):
            @pl.when(step < NCH)
            def _():
                lanes = pl.ds(pl.multiple_of(step * CW, CW), CW)
                for k in range(2):
                    arrived(halo.at[s, k, :, lanes], hs_sem.at[s, k, step], hr_sem.at[s, k, step])
                for f in range(2):
                    fill_rows(s, f, step, params)

            @pl.when(step > 0)
            def _():
                ch = step - 1
                yb[...] = jnp.dot(wt[...], act[step], preferred_element_type=F32)
                for h in range(2):
                    cells = slice(h * W, (h + 1) * W)
                    left = jnp.where(first, 0.0, pltpu.roll(yb[0:C, cells], 1, 1))
                    right = jnp.where(last, 0.0, pltpu.roll(yb[2 * C : 3 * C, cells], W - 1, 1))
                    sb[s, ch, :, cells] = (yb[C : 2 * C, cells] + left + right).astype(BF)
                for d in (2, 1, 3):
                    sums_copy(s, d, ch).start()

            return carry

        lax.fori_loop(0, NCH + 1, chunk, 0)

    def gathered(s, ch):
        for d in (1, 2, 3):
            arrived(rb.at[s, ch, d - 1], rs_sem.at[s, d - 1, ch], rr_sem.at[s, d - 1, ch])
        total = sb[s, ch, quarter(0), :].astype(F32)
        for d in (1, 2, 3):
            total = total + rb[s, ch, d - 1].astype(F32)
        return total + colp[0:Q, 3 * s + 2 : 3 * s + 3]

    def prep_conv(src, dst):
        for b in range(3):
            dst[b * C : (b + 1) * C, :] = src[b].T

    offset = pl.multiple_of(c * Q - half * 128, 32)

    def prep_three(f):
        taps = {}
        for a in range(3):
            for b in range(3):
                t3[a * 3 + b] = w3v[f, a, b].T
        m = valid[f]

        def tap(a, b):
            return t3[a * 3 + b, pl.ds(offset, Q), :].astype(F32)

        for pi in range(2):
            for block, di in enumerate((0, 1) if pi else (0, -1)):
                rows = ((0, 1), (2,))[block] if pi else ((1, 2), (0,))[block]
                sums = []
                for b in range(3):
                    v = tap(rows[0], b)
                    for a in rows[1:]:
                        v = v + tap(a, b)
                    sums.append(v * m if f < 2 else v)
                parts = (sums[0], sums[1] + sums[2], sums[0] + sums[1], sums[2])
                for k, part in enumerate(parts):
                    base = ((pi * 2 + block) * 4 + k) * Q
                    wf[base : base + Q, f * C : (f + 1) * C] = part.astype(BF)

    for cp in stats_copies(0):
        cp.start()
    for ch in range(NCH):
        for k in range(2):
            halo_copy(0, k, ch).start()
    for cp in wloads[0]:
        cp.wait()
    prep_conv(wv1, wt1)
    params = norm_params(0)
    conv(0, wt1, params)
    for cp in wloads[1]:
        cp.wait()
    prep_conv(wv2, wt2)
    w3load.wait()

    p1 = jnp.zeros((Q, W), F32)
    p2 = jnp.zeros((Q, W), F32)
    for ch in range(NCH):
        if ch < 3:
            prep_three(ch)
        hidden = gathered(0, ch).astype(BF)
        flat[1, :, ch * CW : (ch + 1) * CW] = hidden
        for k in range(2):
            halo_copy(1, k, ch).start()
        hidden = hidden.astype(F32)
        for h in range(2):
            row = hidden[:, h * W : (h + 1) * W]
            p1 = p1 + row
            p2 = p2 + row * row
    frame_sums(1, p1, p2)
    for cp in stats_copies(1):
        cp.start()

    params = norm_params(1)
    conv(1, wt2, params)

    def lanes_of(ch):
        return pl.ds(pl.multiple_of(W + ch * CW, W), CW)

    def own_x(d, ch):
        spot = x3.at[2, quarter(0), lanes_of(ch)]
        return remote(spot, spot, as_sem.at[d - 1, ch], ar_sem.at[d - 1, ch], xp(d))

    def own_z(k, ch):
        return remote(
            x3.at[2, quarter(2 * k), lanes_of(ch)],
            x3.at[0, quarter(2 * k), lanes_of(ch)],
            zs_sem.at[k, ch],
            zr_sem.at[k, ch],
            tm(2),
        )

    def back_x(d, ch):
        spot = x3.at[0, quarter(0), lanes_of(ch)]
        return remote(spot, spot, xs_sem.at[d // 2, ch], xr_sem.at[d // 2, ch], xp(d))

    def across(ch):
        return remote(
            x3.at[2 - 2 * core, :, lanes_of(ch)],
            x3.at[1, :, lanes_of(ch)],
            bs_sem.at[ch],
            br_sem.at[ch],
            (t + 1 - 2 * core, c),
        )

    bias = colp[0:Q, 6:7]
    first_q = first[0:Q]
    last_q = last[0:Q]

    def rows_of(f0, f1, ch, di):
        lanes = pl.ds(pl.multiple_of((1 + di) * W + ch * CW, W), CW)
        return x3[f0:f1, :, lanes].reshape((f1 - f0) * C, CW)

    def partial(pi, f0, f1, ch):
        base = pi * 8 * Q
        k = slice(f0 * C, f1 * C)
        mid = jnp.dot(wf[base : base + C, k], rows_of(f0, f1, ch, 0), preferred_element_type=F32)
        edge = rows_of(f0, f1, ch, 1 if pi else -1)
        return mid + jnp.dot(wf[base + C : base + 2 * C, k], edge, preferred_element_type=F32)

    def pipeline(step, carry):
        @pl.when(step < NCH)
        def _():
            ch = step
            cells = pl.ds(pl.multiple_of(ch * CW, CW), CW)
            residual = flat[0, :, cells].astype(F32) + gathered(1, ch)
            x3[2, quarter(0), lanes_of(ch)] = residual.astype(BF)
            own_z(0, ch).start()
            for d in (2, 1, 3):
                own_x(d, ch).start()

        @pl.when((step >= 1) & (step < NCH + 1))
        def _():
            ch = step - 1
            arrived(x3.at[2, quarter(2), lanes_of(ch)], as_sem.at[1, ch], ar_sem.at[1, ch])
            own_z(1, ch).start()
            arrived(x3.at[0, quarter(0), lanes_of(ch)], zs_sem.at[0, ch], zr_sem.at[0, ch])
            for d in (1, 3):
                back_x(d, ch).start()

        @pl.when((step >= 2) & (step < NCH + 2))
        def _():
            ch = step - 2
            for d in (1, 3):
                arrived(x3.at[2, quarter(4 - d), lanes_of(ch)], as_sem.at[d - 1, ch], ar_sem.at[d - 1, ch])
            arrived(x3.at[0, quarter(2), lanes_of(ch)], zs_sem.at[1, ch], zr_sem.at[1, ch])
            for d in (1, 3):
                arrived(x3.at[0, quarter(4 - d), lanes_of(ch)], xs_sem.at[d // 2, ch], xr_sem.at[d // 2, ch])
            across(ch).start()

        @pl.when((step >= 3) & (step < NCH + 3))
        def _():
            ch = step - 3
            for pi in range(2):
                y3[ch, pi] = partial(pi, 2, 3, ch)
            arrived(x3.at[1, :, lanes_of(ch)], bs_sem.at[ch], br_sem.at[ch])

        @pl.when(step >= 4)
        def _():
            ch = step - 4
            for pi in range(2):
                y3[ch, pi] += partial(pi, 0, 2, ch)
                for h in range(2):
                    cells = slice(h * W, (h + 1) * W)
                    left = jnp.where(first_q, 0.0, pltpu.roll(y3[ch, pi, 0:Q, cells], 1, 1))
                    right = jnp.where(last_q, 0.0, pltpu.roll(y3[ch, pi, 3 * Q : 4 * Q, cells], W - 1, 1))
                    rows = slice((2 * h + pi) * Q, (2 * h + pi + 1) * Q)
                    both[rows, 0:W] = (y3[ch, pi, Q : 2 * Q, cells] + left + bias).astype(BF)
                    both[rows, W : 2 * W] = (y3[ch, pi, 2 * Q : 3 * Q, cells] + right + bias).astype(BF)
            spread = jnp.dot(both[...], perm[...], preferred_element_type=F32)
            for k in range(4):
                for g in range(2):
                    oscr[g, pl.ds(ch * 4 + k, Q, stride=2 * H), :] = spread[k * Q : (k + 1) * Q, g * 128 : (g + 1) * 128]

        return carry

    lax.fori_loop(0, NCH + 4, pipeline, 0)
    for g in range(2):
        out[0, :, :, g * 128 : (g + 1) * 128] = oscr[g].reshape(Q, 2 * H, 128).astype(BF)

    for s in range(2):
        for cp in stats_copies(s):
            cp.wait_send()
        for ch in range(NCH):
            for k in range(2):
                halo_copy(s, k, ch).wait_send()
            for d in (1, 2, 3):
                sums_copy(s, d, ch).wait_send()
    for ch in range(NCH):
        for d in (1, 2, 3):
            own_x(d, ch).wait_send()
        for k in range(2):
            own_z(k, ch).wait_send()
        for d in (1, 3):
            back_x(d, ch).wait_send()
        across(ch).wait_send()


def on_device(nt, nc, *args):
    args = [a.reshape(1, Q) if a.ndim == 1 and a.dtype == F32 else a for a in args]
    anywhere = pl.BlockSpec(memory_space=pl.ANY)
    specs = [pl.BlockSpec(memory_space=pltpu.VMEM) if a.ndim == 2 else anywhere for a in args]
    specs[1] = pl.BlockSpec(memory_space=pltpu.SMEM)
    dma = pltpu.SemaphoreType.DMA
    scratch = [
        pltpu.VMEM((Q, H, W), BF),
        pltpu.VMEM((Q * H, W), F32),
        pltpu.VMEM((2, Q, CELLS), BF),
        pltpu.VMEM((2, 2, Q, CELLS), BF),
        pltpu.VMEM((128, 128), F32),
        pltpu.VMEM((128, 128), F32),
        pltpu.VMEM((128, 128), F32),
        pltpu.VMEM((2, 8, 128), F32),
        pltpu.VMEM((2, len(OFFSETS), 8, 128), F32),
        pltpu.VMEM((3, KP, C), BF),
        pltpu.VMEM((3, KP, C), BF),
        pltpu.VMEM((3 * C, KP), BF),
        pltpu.VMEM((3 * C, KP), BF),
        pltpu.VMEM((3, 3, 3, C, 256), BF),
        pltpu.VMEM((9, 256, C), BF),
        pltpu.VMEM((16 * Q, 3 * C), BF),
        pltpu.VMEM((NCH + 2, KP, CW), BF),
        pltpu.VMEM((3 * C, CW), F32),
        pltpu.VMEM((2, NCH, C, CW), BF),
        pltpu.VMEM((2, NCH, 3, Q, CW), BF),
        pltpu.VMEM((3, C, CELLS + 2 * W), BF),
        pltpu.VMEM((NCH, 2, C, CW), F32),
        pltpu.VMEM((C, 2 * W), BF),
        pltpu.VMEM((2 * W, 2 * W), BF),
        pltpu.VMEM((2, Q * 2 * H, 128), F32),
        dma((1,)),
        dma((19,)),
        dma((2, 2, NCH)),
        dma((2, 2, NCH)),
        dma((2, len(OFFSETS))),
        dma((2, len(OFFSETS))),
        dma((2, 3, NCH)),
        dma((2, 3, NCH)),
        dma((3, NCH)),
        dma((3, NCH)),
        dma((2, NCH)),
        dma((2, NCH)),
        dma((2, NCH)),
        dma((2, NCH)),
        dma((NCH,)),
        dma((NCH,)),
    ]
    return pl.pallas_call(
        functools.partial(kernel, nt, nc),
        out_shape=jax.ShapeDtypeStruct((1, Q, 2 * H, 2 * W), BF),
        in_specs=specs,
        out_specs=pl.BlockSpec(memory_space=pltpu.VMEM),
        scratch_shapes=scratch,
        compiler_params=pltpu.CompilerParams(
            collective_id=0, has_side_effects=True, vmem_limit_bytes=60 * 1024 * 1024
        ),
    )(*args)


def solution(mesh):
    in_specs = (
        P("tm", "chan", None, None),
        P(),
        P("chan"),
        P("chan"),
        P(None, None, None, "chan", None),
        P("chan"),
        P("chan"),
        P("chan"),
        P(None, None, None, "chan", None),
        P("chan"),
        P(),
        P("chan"),
    )
    return jax.shard_map(
        functools.partial(on_device, mesh.shape["tm"], mesh.shape["chan"]),
        mesh=mesh,
        in_specs=in_specs,
        out_specs=P("tm", "chan", None, None),
        check_vma=False,
    )
```

```python
import functools

import jax
import jax.numpy as jnp
from jax import lax
from jax.experimental import pallas as pl
from jax.experimental.pallas import tpu as pltpu
from jax.sharding import PartitionSpec as P

C = 384
GROUPS = 32
PER_GROUP = C // GROUPS
Q = 96
H = 8
W = 128
CELLS = H * W
NCH = 4
CW = CELLS // NCH
REACH = 7
HQ = Q // 2
LAG = 1
KP = 896
EPSILON = 1e-06
MESH = pl.DeviceIdType.MESH
BF = jnp.bfloat16
F32 = jnp.float32
OFFSETS = [d for d in range(-REACH, REACH + 1) if d != 0]


def kernel(
    nt,
    nc,
    lat_hbm,
    clip,
    gamma1,
    beta1,
    w1,
    bias1,
    gamma2,
    beta2,
    w2,
    bias2,
    w3,
    bias3,
    out,
    lat_raw,
    lat32,
    flat,
    halo,
    prm,
    tmp,
    colp,
    st_send,
    st_recv,
    wv1,
    wv2,
    wt1,
    wt2,
    w3v,
    t3,
    wf,
    act,
    yb,
    sb,
    added,
    rb,
    x3,
    y3,
    both,
    perm,
    oscr,
    loc_sem,
    w_sem,
    hs_sem,
    hr_sem,
    ss_sem,
    sr_sem,
    rs_sem,
    rr_sem,
    as_sem,
    ar_sem,
    zs_sem,
    zr_sem,
    xs_sem,
    xr_sem,
    bs_sem,
    br_sem,
):
    t = lax.axis_index("tm")
    c = lax.axis_index("chan")
    core = lax.rem(t, 2)

    def tm(d):
        return (lax.rem(t + d + nt, nt), c)

    def xp(d):
        return (t, lax.rem(c + d, nc))

    def quarter(d):
        return pl.ds(pl.multiple_of(lax.rem(c + d, nc) * Q, Q), Q)

    def remote(src, dst, ssem, rsem, dev):
        return pltpu.make_async_remote_copy(
            src_ref=src, dst_ref=dst, send_sem=ssem, recv_sem=rsem, device_id=dev, device_id_type=MESH
        )

    def arrived(dst, ssem, rsem):
        remote(dst, dst, ssem, rsem, xp(1)).wait_recv()

    loads = [pltpu.make_async_copy(lat_hbm.at[0], lat_raw, loc_sem.at[0])]
    for cp in loads:
        cp.start()
    wloads = [[], []]
    for s, (src, dst) in enumerate(((w1, wv1), (w2, wv2))):
        for f in range(3):
            for a in range(3):
                wloads[s].append(
                    pltpu.make_async_copy(
                        src.at[f, a], dst.at[:, pl.ds((a * 3 + f) * Q, Q), :], w_sem.at[s * 9 + f * 3 + a]
                    )
                )
    for cp in wloads[0] + wloads[1]:
        cp.start()
    half = c // 2
    w3load = pltpu.make_async_copy(
        w3.at[:, :, :, :, pl.ds(pl.multiple_of(half * 128, 128), 256)], w3v, w_sem.at[18]
    )
    w3load.start()

    prm[...] = jnp.zeros_like(prm)
    for r, ref in enumerate((gamma1, beta1, bias1, gamma2, beta2, bias2, bias3)):
        prm[r : r + 1, 0:Q] = ref[...]

    zero = jnp.zeros((3, C, W), BF)
    x3[:, :, 0:W] = zero
    x3[:, :, W + CELLS : 2 * W + CELLS] = zero
    act[...] = jnp.zeros_like(act)
    for dst in (wv1, wv2):
        dst[:, 9 * Q : KP, :] = jnp.zeros((3, KP - 9 * Q, C), BF)
    tmp[...] = jnp.zeros_like(tmp)
    er = lax.broadcasted_iota(jnp.int32, (2 * W, 2 * W), 0)
    ec = lax.broadcasted_iota(jnp.int32, (2 * W, 2 * W), 1)
    perm[...] = jnp.where(jnp.where(er < W, 2 * er, 2 * er - 2 * W + 1) == ec, 1.0, 0.0).astype(BF)

    barrier = pltpu.get_barrier_semaphore()
    for d in OFFSETS:
        pl.semaphore_signal(barrier, inc=1, device_id=tm(d), device_id_type=MESH)
    for d in range(1, nc):
        pl.semaphore_signal(barrier, inc=1, device_id=xp(d), device_id_type=MESH)

    for cp in loads:
        cp.wait()
    lat32[...] = lat_raw[...].astype(F32).reshape(Q * H, W)

    def frame_sums(slot, p1, p2):
        tmp[0:Q, :] = p1
        s1 = jnp.sum(tmp[...].T, axis=0, keepdims=True)
        tmp[0:Q, :] = p2
        s2 = jnp.sum(tmp[...].T, axis=0, keepdims=True)
        st_send[slot] = jnp.concatenate([s1, s2, jnp.zeros((6, 128), F32)], 0)

    p1 = jnp.zeros((Q, W), F32)
    p2 = jnp.zeros((Q, W), F32)
    for i in range(H):
        row = lat32[pl.ds(i, Q, stride=H), :]
        p1 = p1 + row
        p2 = p2 + row * row
        flat[0, :, i * W : (i + 1) * W] = row.astype(BF)
    frame_sums(0, p1, p2)
    colp[...] = prm[...].T

    pl.semaphore_wait(barrier, len(OFFSETS) + nc - 1)

    def stats_copies(s):
        return [
            remote(st_send.at[s], st_recv.at[s, k], ss_sem.at[s, k], sr_sem.at[s, k], tm(d))
            for k, d in enumerate(OFFSETS)
        ]

    def halo_copy(s, k, ch):
        lanes = pl.ds(pl.multiple_of(ch * CW, CW), CW)
        return remote(
            flat.at[s, :, lanes], halo.at[s, k, :, lanes], hs_sem.at[s, k, ch], hr_sem.at[s, k, ch], tm(2 - k)
        )

    own_clip = clip[t]
    valid = []
    for d in (2, 1):
        src = lax.rem(t - d + nt, nt)
        valid.append(jnp.where((t - d >= 0) & (clip[src] == own_clip), 1.0, 0.0).astype(F32))
    valid.append(jnp.float32(1.0))

    lane = lax.broadcasted_iota(jnp.int32, (128, 128), 1)
    subl = lax.broadcasted_iota(jnp.int32, (128, 128), 0)
    ga = jnp.floor((subl.astype(F32) + 0.5) * (1.0 / PER_GROUP))
    gb = jnp.floor((lane.astype(F32) + 0.5) * (1.0 / PER_GROUP))
    gmat = jnp.where(ga == gb, 1.0, 0.0).astype(F32)

    def norm_params(s):
        total = st_send[s]
        frames = jnp.float32(1.0)
        for k, d in enumerate(OFFSETS):
            arrived(st_recv.at[s, k], ss_sem.at[s, k], sr_sem.at[s, k])
            src = lax.rem(t - d + nt, nt)
            inside = (t - d >= 0) & (t - d < nt)
            m = jnp.where(inside & (clip[src] == own_clip), 1.0, 0.0).astype(F32)
            total = total + m * st_recv[s, k]
            frames = frames + m
        grouped = jnp.dot(total, gmat, precision=lax.Precision.HIGHEST, preferred_element_type=F32)
        tmp[0:8, :] = grouped
        cols = tmp[...].T
        count = frames * float(PER_GROUP * CELLS)
        mean = cols[0:Q, 0:1] / count
        var = cols[0:Q, 1:2] / count - mean * mean
        inv = lax.rsqrt(var + EPSILON)
        return mean, inv * colp[0:Q, 3 * s : 3 * s + 1], colp[0:Q, 3 * s + 1 : 3 * s + 2]

    def fill_rows(s, f, ch, params):
        for r in range(2):
            cells = pl.ds(pl.multiple_of(ch * CW + r * W, W), W)
            v = (flat[s, :, cells] if f == 2 else halo[s, f, :, cells]).astype(F32)
            u = (v - params[0]) * params[1] + params[2]
            u = u / (1.0 + jnp.exp(-u))
            if f < 2:
                u = u * valid[f]
            u = u.astype(BF)
            for a in range(3):
                o = r + 1 - a
                k = (a * 3 + f) * Q
                act[ch + 1 + o // 2, k : k + Q, (o % 2) * W : (o % 2 + 1) * W] = u

    first = lax.broadcasted_iota(jnp.int32, (Q, W), 1) == 0
    last = lax.broadcasted_iota(jnp.int32, (Q, W), 1) == W - 1
    low = slice(0, HQ)
    high = slice(HQ, Q)

    def ring_copy(s, kind, way, ch):
        if kind == 0:
            src = sb.at[s, ch, 0, high if way else low]
        elif kind == 1:
            src = sb.at[s, ch, 1, low] if way else sb.at[s, ch, 3, high]
        else:
            src = added.at[s, ch, way]
        return remote(
            src, rb.at[s, ch, kind, way], rs_sem.at[s, kind, way, ch], rr_sem.at[s, kind, way, ch], xp(3 if way else 1)
        )

    def ring_arrived(s, kind, way, ch):
        arrived(rb.at[s, ch, kind, way], rs_sem.at[s, kind, way, ch], rr_sem.at[s, kind, way, ch])

    def ring_add(s, ch):
        for way in range(2):
            ring_arrived(s, 0, way, ch)
            mine = sb[s, ch, 1, high] if way else sb[s, ch, 3, low]
            added[s, ch, way] = (mine.astype(F32) + rb[s, ch, 0, way].astype(F32)).astype(BF)
            ring_copy(s, 2, way, ch).start()

    def conv(s, wt, params):
        params = [jnp.broadcast_to(p, (Q, W)) for p in params]
        for ch in range(NCH):
            fill_rows(s, 2, ch, params)

        def chunk(step, carry):
            @pl.when(step < NCH)
            def _():
                lanes = pl.ds(pl.multiple_of(step * CW, CW), CW)
                for k in range(2):
                    arrived(halo.at[s, k, :, lanes], hs_sem.at[s, k, step], hr_sem.at[s, k, step])
                for f in range(2):
                    fill_rows(s, f, step, params)

            @pl.when((step > 0) & (step < NCH + 1))
            def _():
                ch = step - 1
                for lo, hi in ((0, 1), (1, 4)):
                    yb[lo * 3 * Q : hi * 3 * Q, :] = jnp.dot(
                        wt[lo * 3 * Q : hi * 3 * Q, :], act[step], preferred_element_type=F32
                    )
                    for p in range(lo, hi):
                        base = p * 3 * Q
                        for h in range(2):
                            cells = slice(h * W, (h + 1) * W)
                            left = jnp.where(first, 0.0, pltpu.roll(yb[base : base + Q, cells], 1, 1))
                            right = jnp.where(last, 0.0, pltpu.roll(yb[base + 2 * Q : base + 3 * Q, cells], W - 1, 1))
                            sb[s, ch, p, :, cells] = (yb[base + Q : base + 2 * Q, cells] + left + right).astype(BF)
                    for way in range(2):
                        ring_copy(s, lo, way, ch).start()

            @pl.when(step > LAG)
            def _():
                ring_add(s, step - 1 - LAG)

            return carry

        lax.fori_loop(0, NCH + 1 + LAG, chunk, 0)

    def gathered(s, ch):
        for kind in (1, 2):
            for way in range(2):
                ring_arrived(s, kind, way, ch)
        own = sb[s, ch, 2].astype(F32)
        top = own[low] + rb[s, ch, 2, 0].astype(F32) + rb[s, ch, 1, 1].astype(F32)
        bottom = own[high] + rb[s, ch, 1, 0].astype(F32) + rb[s, ch, 2, 1].astype(F32)
        return jnp.concatenate([top, bottom], 0) + colp[0:Q, 3 * s + 2 : 3 * s + 3]

    def prep_conv(src, dst):
        for b in range(3):
            turned = src[b].T
            for q in range(nc):
                place = lax.rem(q - c + 2 + nc, nc) * 3 + b
                dst[pl.ds(pl.multiple_of(place * Q, Q), Q), :] = turned[q * Q : (q + 1) * Q]

    offset = pl.multiple_of(c * Q - half * 128, 32)

    def prep_three(f):
        taps = {}
        for a in range(3):
            for b in range(3):
                t3[a * 3 + b] = w3v[f, a, b].T
        m = valid[f]

        def tap(a, b):
            return t3[a * 3 + b, pl.ds(offset, Q), :].astype(F32)

        for pi in range(2):
            for block, di in enumerate((0, 1) if pi else (0, -1)):
                rows = ((0, 1), (2,))[block] if pi else ((1, 2), (0,))[block]
                sums = []
                for b in range(3):
                    v = tap(rows[0], b)
                    for a in rows[1:]:
                        v = v + tap(a, b)
                    sums.append(v * m if f < 2 else v)
                parts = (sums[0], sums[1] + sums[2], sums[0] + sums[1], sums[2])
                for k, part in enumerate(parts):
                    base = ((pi * 2 + block) * 4 + k) * Q
                    wf[base : base + Q, f * C : (f + 1) * C] = part.astype(BF)

    for cp in stats_copies(0):
        cp.start()
    for ch in range(NCH):
        for k in range(2):
            halo_copy(0, k, ch).start()
    for cp in wloads[0]:
        cp.wait()
    prep_conv(wv1, wt1)
    params = norm_params(0)
    conv(0, wt1, params)
    for cp in wloads[1]:
        cp.wait()
    prep_conv(wv2, wt2)
    w3load.wait()

    p1 = jnp.zeros((Q, W), F32)
    p2 = jnp.zeros((Q, W), F32)
    for ch in range(NCH):
        if ch < 3:
            prep_three(ch)
        hidden = gathered(0, ch).astype(BF)
        flat[1, :, ch * CW : (ch + 1) * CW] = hidden
        for k in range(2):
            halo_copy(1, k, ch).start()
        hidden = hidden.astype(F32)
        for h in range(2):
            row = hidden[:, h * W : (h + 1) * W]
            p1 = p1 + row
            p2 = p2 + row * row
    frame_sums(1, p1, p2)
    for cp in stats_copies(1):
        cp.start()

    params = norm_params(1)
    conv(1, wt2, params)

    def lanes_of(ch):
        return pl.ds(pl.multiple_of(W + ch * CW, W), CW)

    def own_x(d, ch):
        spot = x3.at[2, quarter(0), lanes_of(ch)]
        return remote(spot, spot, as_sem.at[d - 1, ch], ar_sem.at[d - 1, ch], xp(d))

    def half_quarter(d, part):
        return pl.ds(pl.multiple_of(lax.rem(c + d, nc) * Q + part * HQ, HQ), HQ)

    def z_rows(d):
        return half_quarter(d, 0) if d % 2 else quarter(d)

    def own_z(d, ch):
        return remote(
            x3.at[2, z_rows(d), lanes_of(ch)],
            x3.at[0, z_rows(d), lanes_of(ch)],
            zs_sem.at[d, ch],
            zr_sem.at[d, ch],
            tm(2),
        )

    def back_x(d, ch):
        spot = x3.at[0, half_quarter(0, 1), lanes_of(ch)]
        return remote(spot, spot, xs_sem.at[d // 2, ch], xr_sem.at[d // 2, ch], xp(d))

    def across(ch):
        return remote(
            x3.at[2 - 2 * core, :, lanes_of(ch)],
            x3.at[1, :, lanes_of(ch)],
            bs_sem.at[ch],
            br_sem.at[ch],
            (t + 1 - 2 * core, c),
        )

    bias = colp[0:Q, 6:7]

    def rows_of(f0, f1, ch, di):
        lanes = pl.ds(pl.multiple_of((1 + di) * W + ch * CW, W), CW)
        return x3[f0:f1, :, lanes].reshape((f1 - f0) * C, CW)

    def partial(pi, f0, f1, ch):
        base = pi * 8 * Q
        k = slice(f0 * C, f1 * C)
        mid = jnp.dot(wf[base : base + C, k], rows_of(f0, f1, ch, 0), preferred_element_type=F32)
        edge = rows_of(f0, f1, ch, 1 if pi else -1)
        return mid + jnp.dot(wf[base + C : base + 2 * C, k], edge, preferred_element_type=F32)

    def pipeline(step, carry):
        @pl.when(step < NCH)
        def _():
            ch = step
            cells = pl.ds(pl.multiple_of(ch * CW, CW), CW)
            residual = flat[0, :, cells].astype(F32) + gathered(1, ch)
            x3[2, quarter(0), lanes_of(ch)] = residual.astype(BF)
            own_z(0, ch).start()
            for d in (2, 1, 3):
                own_x(d, ch).start()

        @pl.when((step >= 1) & (step < NCH + 1))
        def _():
            ch = step - 1
            for d in (1, 3):
                arrived(x3.at[2, quarter(4 - d), lanes_of(ch)], as_sem.at[d - 1, ch], ar_sem.at[d - 1, ch])
                own_z(4 - d, ch).start()
            arrived(x3.at[2, quarter(2), lanes_of(ch)], as_sem.at[1, ch], ar_sem.at[1, ch])
            own_z(2, ch).start()
            arrived(x3.at[0, quarter(0), lanes_of(ch)], zs_sem.at[0, ch], zr_sem.at[0, ch])
            for d in (1, 3):
                back_x(d, ch).start()

        @pl.when((step >= 2) & (step < NCH + 2))
        def _():
            ch = step - 2
            for d in (1, 2, 3):
                arrived(x3.at[0, z_rows(d), lanes_of(ch)], zs_sem.at[d, ch], zr_sem.at[d, ch])
            for d in (1, 3):
                arrived(x3.at[0, half_quarter(4 - d, 1), lanes_of(ch)], xs_sem.at[d // 2, ch], xr_sem.at[d // 2, ch])
            across(ch).start()

        @pl.when((step >= 3) & (step < NCH + 3))
        def _():
            ch = step - 3
            for pi in range(2):
                y3[ch, pi] = partial(pi, 2, 3, ch)
            arrived(x3.at[1, :, lanes_of(ch)], bs_sem.at[ch], br_sem.at[ch])

        @pl.when(step >= 4)
        def _():
            ch = step - 4
            for pi in range(2):
                y3[ch, pi] += partial(pi, 0, 2, ch)
                for h in range(2):
                    cells = slice(h * W, (h + 1) * W)
                    left = jnp.where(first, 0.0, pltpu.roll(y3[ch, pi, 0:Q, cells], 1, 1))
                    right = jnp.where(last, 0.0, pltpu.roll(y3[ch, pi, 3 * Q : 4 * Q, cells], W - 1, 1))
                    rows = slice((2 * h + pi) * Q, (2 * h + pi + 1) * Q)
                    both[rows, 0:W] = (y3[ch, pi, Q : 2 * Q, cells] + left + bias).astype(BF)
                    both[rows, W : 2 * W] = (y3[ch, pi, 2 * Q : 3 * Q, cells] + right + bias).astype(BF)
            spread = jnp.dot(both[...], perm[...], preferred_element_type=F32)
            for k in range(4):
                for g in range(2):
                    oscr[g, pl.ds(ch * 4 + k, Q, stride=2 * H), :] = spread[k * Q : (k + 1) * Q, g * 128 : (g + 1) * 128]

        return carry

    lax.fori_loop(0, NCH + 4, pipeline, 0)
    for g in range(2):
        out[0, :, :, g * 128 : (g + 1) * 128] = oscr[g].reshape(Q, 2 * H, 128).astype(BF)

    for s in range(2):
        for cp in stats_copies(s):
            cp.wait_send()
        for ch in range(NCH):
            for k in range(2):
                halo_copy(s, k, ch).wait_send()
            for kind in range(3):
                for way in range(2):
                    ring_copy(s, kind, way, ch).wait_send()
    for ch in range(NCH):
        for d in (1, 2, 3):
            own_x(d, ch).wait_send()
        for d in range(4):
            own_z(d, ch).wait_send()
        for d in (1, 3):
            back_x(d, ch).wait_send()
        across(ch).wait_send()


def on_device(nt, nc, *args):
    args = [a.reshape(1, Q) if a.ndim == 1 and a.dtype == F32 else a for a in args]
    anywhere = pl.BlockSpec(memory_space=pl.ANY)
    specs = [pl.BlockSpec(memory_space=pltpu.VMEM) if a.ndim == 2 else anywhere for a in args]
    specs[1] = pl.BlockSpec(memory_space=pltpu.SMEM)
    dma = pltpu.SemaphoreType.DMA
    scratch = [
        pltpu.VMEM((Q, H, W), BF),
        pltpu.VMEM((Q * H, W), F32),
        pltpu.VMEM((2, Q, CELLS), BF),
        pltpu.VMEM((2, 2, Q, CELLS), BF),
        pltpu.VMEM((128, 128), F32),
        pltpu.VMEM((128, 128), F32),
        pltpu.VMEM((128, 128), F32),
        pltpu.VMEM((2, 8, 128), F32),
        pltpu.VMEM((2, len(OFFSETS), 8, 128), F32),
        pltpu.VMEM((3, KP, C), BF),
        pltpu.VMEM((3, KP, C), BF),
        pltpu.VMEM((3 * C, KP), BF),
        pltpu.VMEM((3 * C, KP), BF),
        pltpu.VMEM((3, 3, 3, C, 256), BF),
        pltpu.VMEM((9, 256, C), BF),
        pltpu.VMEM((16 * Q, 3 * C), BF),
        pltpu.VMEM((NCH + 2, KP, CW), BF),
        pltpu.VMEM((3 * C, CW), F32),
        pltpu.VMEM((2, NCH, 4, Q, CW), BF),
        pltpu.VMEM((2, NCH, 2, HQ, CW), BF),
        pltpu.VMEM((2, NCH, 3, 2, HQ, CW), BF),
        pltpu.VMEM((3, C, CELLS + 2 * W), BF),
        pltpu.VMEM((NCH, 2, C, CW), F32),
        pltpu.VMEM((C, 2 * W), BF),
        pltpu.VMEM((2 * W, 2 * W), BF),
        pltpu.VMEM((2, Q * 2 * H, 128), F32),
        dma((1,)),
        dma((19,)),
        dma((2, 2, NCH)),
        dma((2, 2, NCH)),
        dma((2, len(OFFSETS))),
        dma((2, len(OFFSETS))),
        dma((2, 3, 2, NCH)),
        dma((2, 3, 2, NCH)),
        dma((3, NCH)),
        dma((3, NCH)),
        dma((4, NCH)),
        dma((4, NCH)),
        dma((2, NCH)),
        dma((2, NCH)),
        dma((NCH,)),
        dma((NCH,)),
    ]
    return pl.pallas_call(
        functools.partial(kernel, nt, nc),
        out_shape=jax.ShapeDtypeStruct((1, Q, 2 * H, 2 * W), BF),
        in_specs=specs,
        out_specs=pl.BlockSpec(memory_space=pltpu.VMEM),
        scratch_shapes=scratch,
        compiler_params=pltpu.CompilerParams(
            collective_id=0, has_side_effects=True, vmem_limit_bytes=60 * 1024 * 1024
        ),
    )(*args)


def solution(mesh):
    in_specs = (
        P("tm", "chan", None, None),
        P(),
        P("chan"),
        P("chan"),
        P(None, None, None, "chan", None),
        P("chan"),
        P("chan"),
        P("chan"),
        P(None, None, None, "chan", None),
        P("chan"),
        P(),
        P("chan"),
    )
    return jax.shard_map(
        functools.partial(on_device, mesh.shape["tm"], mesh.shape["chan"]),
        mesh=mesh,
        in_specs=in_specs,
        out_specs=P("tm", "chan", None, None),
        check_vma=False,
    )
```

```python
import functools

import jax
import jax.numpy as jnp
from jax import lax
from jax.experimental import pallas as pl
from jax.experimental.pallas import tpu as pltpu
from jax.sharding import PartitionSpec as P

C = 384
GROUPS = 32
PER_GROUP = C // GROUPS
Q = 96
H = 8
W = 128
CELLS = H * W
NCH = 4
CW = CELLS // NCH
REACH = 7
HQ = Q // 2
LAG = 3
LAG_B = 4
LAG_O = 6
LAG_C = 6
LAG_D = 7
LAG_E = 8
KP = 896
EPSILON = 1e-06
MESH = pl.DeviceIdType.MESH
BF = jnp.bfloat16
F32 = jnp.float32
OFFSETS = [d for d in range(-REACH, REACH + 1) if d != 0]


def kernel(
    nt,
    nc,
    lat_hbm,
    clip,
    gamma1,
    beta1,
    w1,
    bias1,
    gamma2,
    beta2,
    w2,
    bias2,
    w3,
    bias3,
    out,
    lat_raw,
    lat32,
    flat,
    halo,
    prm,
    tmp,
    colp,
    st_send,
    st_recv,
    wv1,
    wv2,
    wt1,
    wt2,
    w3v,
    t3,
    wf,
    act,
    yb,
    sb,
    added,
    rb,
    x3,
    y3,
    both,
    perm,
    oscr,
    done,
    loc_sem,
    w_sem,
    hs_sem,
    hr_sem,
    ss_sem,
    sr_sem,
    rs_sem,
    rr_sem,
    as_sem,
    ar_sem,
    zs_sem,
    zr_sem,
    xs_sem,
    xr_sem,
    bs_sem,
    br_sem,
):
    t = lax.axis_index("tm")
    c = lax.axis_index("chan")
    core = lax.rem(t, 2)

    def tm(d):
        return (lax.rem(t + d + nt, nt), c)

    def xp(d):
        return (t, lax.rem(c + d, nc))

    def quarter(d):
        return pl.ds(pl.multiple_of(lax.rem(c + d, nc) * Q, Q), Q)

    def remote(src, dst, ssem, rsem, dev):
        return pltpu.make_async_remote_copy(
            src_ref=src, dst_ref=dst, send_sem=ssem, recv_sem=rsem, device_id=dev, device_id_type=MESH
        )

    def arrived(dst, ssem, rsem):
        remote(dst, dst, ssem, rsem, xp(1)).wait_recv()

    loads = [pltpu.make_async_copy(lat_hbm.at[0], lat_raw, loc_sem.at[0])]
    for cp in loads:
        cp.start()
    wloads = [[], []]
    for s, (src, dst) in enumerate(((w1, wv1), (w2, wv2))):
        for f in range(3):
            for a in range(3):
                wloads[s].append(
                    pltpu.make_async_copy(
                        src.at[f, a], dst.at[:, pl.ds((a * 3 + f) * Q, Q), :], w_sem.at[s * 9 + f * 3 + a]
                    )
                )
    for cp in wloads[0] + wloads[1]:
        cp.start()
    half = c // 2
    w3load = pltpu.make_async_copy(
        w3.at[:, :, :, :, pl.ds(pl.multiple_of(half * 128, 128), 256)], w3v, w_sem.at[18]
    )
    w3load.start()

    prm[...] = jnp.zeros_like(prm)
    for r, ref in enumerate((gamma1, beta1, bias1, gamma2, beta2, bias2, bias3)):
        prm[r : r + 1, 0:Q] = ref[...]

    zero = jnp.zeros((3, C, W), BF)
    x3[:, :, 0:W] = zero
    x3[:, :, W + CELLS : 2 * W + CELLS] = zero
    act[...] = jnp.zeros_like(act)
    for dst in (wv1, wv2):
        dst[:, 9 * Q : KP, :] = jnp.zeros((3, KP - 9 * Q, C), BF)
    tmp[...] = jnp.zeros_like(tmp)
    er = lax.broadcasted_iota(jnp.int32, (2 * W, 2 * W), 0)
    ec = lax.broadcasted_iota(jnp.int32, (2 * W, 2 * W), 1)
    perm[...] = jnp.where(jnp.where(er < W, 2 * er, 2 * er - 2 * W + 1) == ec, 1.0, 0.0).astype(BF)

    barrier = pltpu.get_barrier_semaphore()
    for d in OFFSETS:
        pl.semaphore_signal(barrier, inc=1, device_id=tm(d), device_id_type=MESH)
    for d in range(1, nc):
        pl.semaphore_signal(barrier, inc=1, device_id=xp(d), device_id_type=MESH)

    for cp in loads:
        cp.wait()
    lat32[...] = lat_raw[...].astype(F32).reshape(Q * H, W)

    def frame_sums(slot, p1, p2):
        tmp[0:Q, :] = p1
        s1 = jnp.sum(tmp[...].T, axis=0, keepdims=True)
        tmp[0:Q, :] = p2
        s2 = jnp.sum(tmp[...].T, axis=0, keepdims=True)
        st_send[slot] = jnp.concatenate([s1, s2, jnp.zeros((6, 128), F32)], 0)

    p1 = jnp.zeros((Q, W), F32)
    p2 = jnp.zeros((Q, W), F32)
    for i in range(H):
        row = lat32[pl.ds(i, Q, stride=H), :]
        p1 = p1 + row
        p2 = p2 + row * row
        flat[0, :, i * W : (i + 1) * W] = row.astype(BF)
    frame_sums(0, p1, p2)
    colp[...] = prm[...].T

    def prep_conv(src, dst):
        for b in range(3):
            turned = src[b].T
            for q in range(nc):
                place = lax.rem(q - c + 2 + nc, nc) * 3 + b
                dst[pl.ds(pl.multiple_of(place * Q, Q), Q), :] = turned[q * Q : (q + 1) * Q]

    for cp in wloads[0]:
        cp.wait()
    prep_conv(wv1, wt1)
    pl.semaphore_wait(barrier, len(OFFSETS) + nc - 1)

    def stats_copies(s):
        return [
            remote(st_send.at[s], st_recv.at[s, k], ss_sem.at[s, k], sr_sem.at[s, k], tm(d))
            for k, d in enumerate(OFFSETS)
        ]

    def halo_copy(s, k, ch):
        lanes = pl.ds(pl.multiple_of(ch * CW, CW), CW)
        return remote(
            flat.at[s, :, lanes], halo.at[s, k, :, lanes], hs_sem.at[s, k, ch], hr_sem.at[s, k, ch], tm(2 - k)
        )

    own_clip = clip[t]
    valid = []
    for d in (2, 1):
        src = lax.rem(t - d + nt, nt)
        valid.append(jnp.where((t - d >= 0) & (clip[src] == own_clip), 1.0, 0.0).astype(F32))
    valid.append(jnp.float32(1.0))

    lane = lax.broadcasted_iota(jnp.int32, (128, 128), 1)
    subl = lax.broadcasted_iota(jnp.int32, (128, 128), 0)
    ga = jnp.floor((subl.astype(F32) + 0.5) * (1.0 / PER_GROUP))
    gb = jnp.floor((lane.astype(F32) + 0.5) * (1.0 / PER_GROUP))
    gmat = jnp.where(ga == gb, 1.0, 0.0).astype(F32)

    def norm_params(s):
        total = st_send[s]
        frames = jnp.float32(1.0)
        for k, d in enumerate(OFFSETS):
            arrived(st_recv.at[s, k], ss_sem.at[s, k], sr_sem.at[s, k])
            src = lax.rem(t - d + nt, nt)
            inside = (t - d >= 0) & (t - d < nt)
            m = jnp.where(inside & (clip[src] == own_clip), 1.0, 0.0).astype(F32)
            total = total + m * st_recv[s, k]
            frames = frames + m
        grouped = jnp.dot(total, gmat, precision=lax.Precision.HIGHEST, preferred_element_type=F32)
        tmp[0:8, :] = grouped
        cols = tmp[...].T
        count = frames * float(PER_GROUP * CELLS)
        mean = cols[0:Q, 0:1] / count
        var = cols[0:Q, 1:2] / count - mean * mean
        inv = lax.rsqrt(var + EPSILON)
        return mean, inv * colp[0:Q, 3 * s : 3 * s + 1], colp[0:Q, 3 * s + 1 : 3 * s + 2]

    def fill_rows(s, f, ch, params):
        for r in range(2):
            cells = pl.ds(pl.multiple_of(ch * CW + r * W, W), W)
            v = (flat[s, :, cells] if f == 2 else halo[s, f, :, cells]).astype(F32)
            u = (v - params[0]) * params[1] + params[2]
            u = u / (1.0 + jnp.exp(-u))
            if f < 2:
                u = u * valid[f]
            u = u.astype(BF)
            for a in range(3):
                o = r + 1 - a
                k = (a * 3 + f) * Q
                act[ch + 1 + o // 2, k : k + Q, (o % 2) * W : (o % 2 + 1) * W] = u

    first = lax.broadcasted_iota(jnp.int32, (Q, W), 1) == 0
    last = lax.broadcasted_iota(jnp.int32, (Q, W), 1) == W - 1
    low = slice(0, HQ)
    high = slice(HQ, Q)

    def ring_copy(s, kind, way, ch):
        if kind == 0:
            src = sb.at[s, ch, 0, high if way else low]
        elif kind == 1:
            src = sb.at[s, ch, 1, low] if way else sb.at[s, ch, 3, high]
        else:
            src = added.at[s, ch, way]
        return remote(
            src, rb.at[s, ch, kind, way], rs_sem.at[s, kind, way, ch], rr_sem.at[s, kind, way, ch], xp(3 if way else 1)
        )

    def ring_arrived(s, kind, way, ch):
        arrived(rb.at[s, ch, kind, way], rs_sem.at[s, kind, way, ch], rr_sem.at[s, kind, way, ch])

    def ring_add(s, ch):
        for way in range(2):
            ring_arrived(s, 0, way, ch)
            mine = sb[s, ch, 1, high] if way else sb[s, ch, 3, low]
            added[s, ch, way] = (mine.astype(F32) + rb[s, ch, 0, way].astype(F32)).astype(BF)
            ring_copy(s, 2, way, ch).start()

    def conv(s, wt, params):
        params = [jnp.broadcast_to(p, (Q, W)) for p in params]
        for ch in range(NCH):
            fill_rows(s, 2, ch, params)

        def chunk(step, carry):
            @pl.when(step < NCH)
            def _():
                lanes = pl.ds(pl.multiple_of(step * CW, CW), CW)
                for k in range(2):
                    arrived(halo.at[s, k, :, lanes], hs_sem.at[s, k, step], hr_sem.at[s, k, step])
                for f in range(2):
                    fill_rows(s, f, step, params)

            @pl.when((step > 0) & (step < NCH + 1))
            def _():
                ch = step - 1
                for lo, hi in ((0, 1), (1, 4)):
                    yb[lo * 3 * Q : hi * 3 * Q, :] = jnp.dot(
                        wt[lo * 3 * Q : hi * 3 * Q, :], act[step], preferred_element_type=F32
                    )
                    for p in range(lo, hi):
                        base = p * 3 * Q
                        for h in range(2):
                            cells = slice(h * W, (h + 1) * W)
                            left = jnp.where(first, 0.0, pltpu.roll(yb[base : base + Q, cells], 1, 1))
                            right = jnp.where(last, 0.0, pltpu.roll(yb[base + 2 * Q : base + 3 * Q, cells], W - 1, 1))
                            sb[s, ch, p, :, cells] = (yb[base + Q : base + 2 * Q, cells] + left + right).astype(BF)
                    for way in range(2):
                        ring_copy(s, lo, way, ch).start()

            @pl.when(step > LAG)
            def _():
                ring_add(s, step - 1 - LAG)

            return carry

        lax.fori_loop(0, NCH + 1 + LAG, chunk, 0)

    def gathered(s, ch):
        for kind in (1, 2):
            for way in range(2):
                ring_arrived(s, kind, way, ch)
        own = sb[s, ch, 2].astype(F32)
        top = own[low] + rb[s, ch, 2, 0].astype(F32) + rb[s, ch, 1, 1].astype(F32)
        bottom = own[high] + rb[s, ch, 1, 0].astype(F32) + rb[s, ch, 2, 1].astype(F32)
        return jnp.concatenate([top, bottom], 0) + colp[0:Q, 3 * s + 2 : 3 * s + 3]

    offset = pl.multiple_of(c * Q - half * 128, 32)

    def prep_three(f):
        taps = {}
        for a in range(3):
            for b in range(3):
                t3[a * 3 + b] = w3v[f, a, b].T
        m = valid[f]

        def tap(a, b):
            return t3[a * 3 + b, pl.ds(offset, Q), :].astype(F32)

        for pi in range(2):
            for block, di in enumerate((0, 1) if pi else (0, -1)):
                rows = ((0, 1), (2,))[block] if pi else ((1, 2), (0,))[block]
                sums = []
                for b in range(3):
                    v = tap(rows[0], b)
                    for a in rows[1:]:
                        v = v + tap(a, b)
                    sums.append(v * m if f < 2 else v)
                parts = (sums[0], sums[1] + sums[2], sums[0] + sums[1], sums[2])
                for k, part in enumerate(parts):
                    base = ((pi * 2 + block) * 4 + k) * Q
                    wf[base : base + Q, f * C : (f + 1) * C] = part.astype(BF)

    for cp in stats_copies(0):
        cp.start()
    for ch in range(NCH):
        for k in range(2):
            halo_copy(0, k, ch).start()
    for cp in wloads[1]:
        cp.wait()
    prep_conv(wv2, wt2)
    w3load.wait()
    for f in range(3):
        prep_three(f)
    params = norm_params(0)
    conv(0, wt1, params)
    p1 = jnp.zeros((Q, W), F32)
    p2 = jnp.zeros((Q, W), F32)
    for ch in range(NCH):
        hidden = gathered(0, ch).astype(BF)
        flat[1, :, ch * CW : (ch + 1) * CW] = hidden
        for k in range(2):
            halo_copy(1, k, ch).start()
        hidden = hidden.astype(F32)
        for h in range(2):
            row = hidden[:, h * W : (h + 1) * W]
            p1 = p1 + row
            p2 = p2 + row * row
    frame_sums(1, p1, p2)
    for cp in stats_copies(1):
        cp.start()

    params = norm_params(1)
    conv(1, wt2, params)

    def lanes_of(ch):
        return pl.ds(pl.multiple_of(W + ch * CW, W), CW)

    def own_x(d, ch):
        spot = x3.at[2, quarter(0), lanes_of(ch)]
        return remote(spot, spot, as_sem.at[d - 1, ch], ar_sem.at[d - 1, ch], xp(d))

    def half_quarter(d, part):
        return pl.ds(pl.multiple_of(lax.rem(c + d, nc) * Q + part * HQ, HQ), HQ)

    def z_rows(d):
        return half_quarter(d, 0) if d % 2 else quarter(d)

    def own_z(d, ch):
        return remote(
            x3.at[2, z_rows(d), lanes_of(ch)],
            x3.at[0, z_rows(d), lanes_of(ch)],
            zs_sem.at[d, ch],
            zr_sem.at[d, ch],
            tm(2),
        )

    def back_x(d, ch):
        spot = x3.at[0, half_quarter(0, 1), lanes_of(ch)]
        return remote(spot, spot, xs_sem.at[d // 2, ch], xr_sem.at[d // 2, ch], xp(d))

    def across(ch):
        return remote(
            x3.at[2 - 2 * core, :, lanes_of(ch)],
            x3.at[1, :, lanes_of(ch)],
            bs_sem.at[ch],
            br_sem.at[ch],
            (t + 1 - 2 * core, c),
        )

    bias = colp[0:Q, 6:7]

    def rows_of(f0, f1, ch, di):
        lanes = pl.ds(pl.multiple_of((1 + di) * W + ch * CW, W), CW)
        return x3[f0:f1, :, lanes].reshape((f1 - f0) * C, CW)

    def partial(pi, f0, f1, ch):
        base = pi * 8 * Q
        k = slice(f0 * C, f1 * C)
        mid = jnp.dot(wf[base : base + C, k], rows_of(f0, f1, ch, 0), preferred_element_type=F32)
        edge = rows_of(f0, f1, ch, 1 if pi else -1)
        return mid + jnp.dot(wf[base + C : base + 2 * C, k], edge, preferred_element_type=F32)

    def result_copy(block):
        lines = pl.ds(pl.multiple_of(block * H, H), H)
        return pltpu.make_async_copy(done.at[block], out.at[0, :, lines, :], loc_sem.at[1 + block])

    def pipeline(step, carry):
        @pl.when(step < NCH)
        def _():
            ch = step
            cells = pl.ds(pl.multiple_of(ch * CW, CW), CW)
            residual = flat[0, :, cells].astype(F32) + gathered(1, ch)
            x3[2, quarter(0), lanes_of(ch)] = residual.astype(BF)
            own_z(0, ch).start()
            for d in (2, 1, 3):
                own_x(d, ch).start()

        @pl.when((step >= LAG_B) & (step < NCH + LAG_B))
        def _():
            ch = step - LAG_B
            for d in (1, 3):
                arrived(x3.at[2, quarter(4 - d), lanes_of(ch)], as_sem.at[d - 1, ch], ar_sem.at[d - 1, ch])
                own_z(4 - d, ch).start()
            arrived(x3.at[2, quarter(2), lanes_of(ch)], as_sem.at[1, ch], ar_sem.at[1, ch])
            own_z(2, ch).start()
            arrived(x3.at[0, quarter(0), lanes_of(ch)], zs_sem.at[0, ch], zr_sem.at[0, ch])
            for d in (1, 3):
                back_x(d, ch).start()

        @pl.when((step >= LAG_O) & (step < NCH + LAG_O))
        def _():
            ch = step - LAG_O
            for pi in range(2):
                y3[ch, pi] = partial(pi, 2, 3, ch)

        @pl.when((step >= LAG_D) & (step < NCH + LAG_D))
        def _():
            ch = step - LAG_D
            arrived(x3.at[1, :, lanes_of(ch)], bs_sem.at[ch], br_sem.at[ch])

        @pl.when((step >= LAG_E) & (step < NCH + LAG_E))
        def _():
            ch = step - LAG_E
            for pi in range(2):
                y3[ch, pi] += partial(pi, 0, 2, ch)
                for h in range(2):
                    cells = slice(h * W, (h + 1) * W)
                    left = jnp.where(first, 0.0, pltpu.roll(y3[ch, pi, 0:Q, cells], 1, 1))
                    right = jnp.where(last, 0.0, pltpu.roll(y3[ch, pi, 3 * Q : 4 * Q, cells], W - 1, 1))
                    rows = slice((2 * h + pi) * Q, (2 * h + pi + 1) * Q)
                    both[rows, 0:W] = (y3[ch, pi, Q : 2 * Q, cells] + left + bias).astype(BF)
                    both[rows, W : 2 * W] = (y3[ch, pi, 2 * Q : 3 * Q, cells] + right + bias).astype(BF)
            spread = jnp.dot(both[...], perm[...], preferred_element_type=F32)
            for k in range(4):
                for g in range(2):
                    oscr[ch // 2, g, pl.ds(lax.rem(ch, 2) * 4 + k, Q, stride=H), :] = spread[k * Q : (k + 1) * Q, g * 128 : (g + 1) * 128]

            @pl.when(ch % 2 == 1)
            def _():
                block = ch // 2
                for g in range(2):
                    lines = oscr[block, g].reshape(Q, H, 128)
                    done[block, :, :, g * 128 : (g + 1) * 128] = lines.astype(BF)
                result_copy(block).start()

        @pl.when((step >= LAG_C) & (step < NCH + LAG_C))
        def _():
            ch = step - LAG_C
            for d in (1, 2, 3):
                arrived(x3.at[0, z_rows(d), lanes_of(ch)], zs_sem.at[d, ch], zr_sem.at[d, ch])
            for d in (1, 3):
                arrived(x3.at[0, half_quarter(4 - d, 1), lanes_of(ch)], xs_sem.at[d // 2, ch], xr_sem.at[d // 2, ch])
            across(ch).start()

        return carry

    lax.fori_loop(0, NCH + LAG_E, pipeline, 0)
    for block in range(2):
        result_copy(block).wait()

    for s in range(2):
        for cp in stats_copies(s):
            cp.wait_send()
        for ch in range(NCH):
            for k in range(2):
                halo_copy(s, k, ch).wait_send()
            for kind in range(3):
                for way in range(2):
                    ring_copy(s, kind, way, ch).wait_send()
    for ch in range(NCH):
        for d in (1, 2, 3):
            own_x(d, ch).wait_send()
        for d in range(4):
            own_z(d, ch).wait_send()
        for d in (1, 3):
            back_x(d, ch).wait_send()
        across(ch).wait_send()


def on_device(nt, nc, *args):
    args = [a.reshape(1, Q) if a.ndim == 1 and a.dtype == F32 else a for a in args]
    anywhere = pl.BlockSpec(memory_space=pl.ANY)
    specs = [pl.BlockSpec(memory_space=pltpu.VMEM) if a.ndim == 2 else anywhere for a in args]
    specs[1] = pl.BlockSpec(memory_space=pltpu.SMEM)
    dma = pltpu.SemaphoreType.DMA
    scratch = [
        pltpu.VMEM((Q, H, W), BF),
        pltpu.VMEM((Q * H, W), F32),
        pltpu.VMEM((2, Q, CELLS), BF),
        pltpu.VMEM((2, 2, Q, CELLS), BF),
        pltpu.VMEM((128, 128), F32),
        pltpu.VMEM((128, 128), F32),
        pltpu.VMEM((128, 128), F32),
        pltpu.VMEM((2, 8, 128), F32),
        pltpu.VMEM((2, len(OFFSETS), 8, 128), F32),
        pltpu.VMEM((3, KP, C), BF),
        pltpu.VMEM((3, KP, C), BF),
        pltpu.VMEM((3 * C, KP), BF),
        pltpu.VMEM((3 * C, KP), BF),
        pltpu.VMEM((3, 3, 3, C, 256), BF),
        pltpu.VMEM((9, 256, C), BF),
        pltpu.VMEM((16 * Q, 3 * C), BF),
        pltpu.VMEM((NCH + 2, KP, CW), BF),
        pltpu.VMEM((3 * C, CW), F32),
        pltpu.VMEM((2, NCH, 4, Q, CW), BF),
        pltpu.VMEM((2, NCH, 2, HQ, CW), BF),
        pltpu.VMEM((2, NCH, 3, 2, HQ, CW), BF),
        pltpu.VMEM((3, C, CELLS + 2 * W), BF),
        pltpu.VMEM((NCH, 2, C, CW), F32),
        pltpu.VMEM((C, 2 * W), BF),
        pltpu.VMEM((2 * W, 2 * W), BF),
        pltpu.VMEM((2, 2, Q * H, 128), F32),
        pltpu.VMEM((2, Q, H, 2 * W), BF),
        dma((3,)),
        dma((19,)),
        dma((2, 2, NCH)),
        dma((2, 2, NCH)),
        dma((2, len(OFFSETS))),
        dma((2, len(OFFSETS))),
        dma((2, 3, 2, NCH)),
        dma((2, 3, 2, NCH)),
        dma((3, NCH)),
        dma((3, NCH)),
        dma((4, NCH)),
        dma((4, NCH)),
        dma((2, NCH)),
        dma((2, NCH)),
        dma((NCH,)),
        dma((NCH,)),
    ]
    return pl.pallas_call(
        functools.partial(kernel, nt, nc),
        out_shape=jax.ShapeDtypeStruct((1, Q, 2 * H, 2 * W), BF),
        in_specs=specs,
        out_specs=pl.BlockSpec(memory_space=pl.ANY),
        scratch_shapes=scratch,
        compiler_params=pltpu.CompilerParams(
            collective_id=0, has_side_effects=True, vmem_limit_bytes=60 * 1024 * 1024
        ),
    )(*args)


def solution(mesh):
    in_specs = (
        P("tm", "chan", None, None),
        P(),
        P("chan"),
        P("chan"),
        P(None, None, None, "chan", None),
        P("chan"),
        P("chan"),
        P("chan"),
        P(None, None, None, "chan", None),
        P("chan"),
        P(),
        P("chan"),
    )
    return jax.shard_map(
        functools.partial(on_device, mesh.shape["tm"], mesh.shape["chan"]),
        mesh=mesh,
        in_specs=in_specs,
        out_specs=P("tm", "chan", None, None),
        check_vma=False,
    )
```

```python
import functools

import jax
import jax.numpy as jnp
from jax import lax
from jax.experimental import pallas as pl
from jax.experimental.pallas import tpu as pltpu
from jax.sharding import PartitionSpec as P

C = 384
GROUPS = 32
PER_GROUP = C // GROUPS
Q = 96
H = 8
W = 128
CELLS = H * W
NCH = 4
CW = CELLS // NCH
REACH = 7
HQ = Q // 2
LAG_R = 4
LAG_S = 5
LAG_B = 4
LAG_K = 5
LAG_P = 8
LAG_O = 9
LAG_C = 11
LAG_D = 12
LAG_E = 13
KP = 896
EPSILON = 1e-06
MESH = pl.DeviceIdType.MESH
BF = jnp.bfloat16
F32 = jnp.float32
OFFSETS = [d for d in range(-REACH, REACH + 1) if d != 0]


def kernel(
    nt,
    nc,
    lat_hbm,
    clip,
    gamma1,
    beta1,
    w1,
    bias1,
    gamma2,
    beta2,
    w2,
    bias2,
    w3,
    bias3,
    out,
    lat_raw,
    lat32,
    fr,
    prm,
    tmp,
    colp,
    st_send,
    st_recv,
    wv1,
    wv2,
    wt1,
    wt2,
    w3v,
    t3,
    wf,
    act,
    yb,
    sb,
    added,
    rb,
    x3,
    y3,
    both,
    perm,
    oscr,
    done,
    loc_sem,
    w_sem,
    hs_sem,
    hr_sem,
    ss_sem,
    sr_sem,
    rs_sem,
    rr_sem,
    as_sem,
    ar_sem,
    ps_sem,
    pr_sem,
    zs_sem,
    zr_sem,
    xs_sem,
    xr_sem,
    bs_sem,
    br_sem,
):
    t = lax.axis_index("tm")
    c = lax.axis_index("chan")
    core = lax.rem(t, 2)

    def tm(d):
        return (lax.rem(t + d + nt, nt), c)

    def xp(d):
        return (t, lax.rem(c + d, nc))

    def quarter(d):
        return pl.ds(pl.multiple_of(lax.rem(c + d, nc) * Q, Q), Q)

    def remote(src, dst, ssem, rsem, dev):
        return pltpu.make_async_remote_copy(
            src_ref=src, dst_ref=dst, send_sem=ssem, recv_sem=rsem, device_id=dev, device_id_type=MESH
        )

    def arrived(dst, ssem, rsem):
        remote(dst, dst, ssem, rsem, xp(1)).wait_recv()

    loads = [pltpu.make_async_copy(lat_hbm.at[0], lat_raw, loc_sem.at[0])]
    for cp in loads:
        cp.start()
    wloads = [[], []]
    for s, (src, dst) in enumerate(((w1, wv1), (w2, wv2))):
        for f in range(3):
            for a in range(3):
                wloads[s].append(
                    pltpu.make_async_copy(
                        src.at[f, a], dst.at[:, pl.ds((a * 3 + f) * Q, Q), :], w_sem.at[s * 9 + f * 3 + a]
                    )
                )
    for cp in wloads[0] + wloads[1]:
        cp.start()
    half = c // 2
    w3load = pltpu.make_async_copy(
        w3.at[:, :, :, :, pl.ds(pl.multiple_of(half * 128, 128), 256)], w3v, w_sem.at[18]
    )
    w3load.start()

    prm[...] = jnp.zeros_like(prm)
    for r, ref in enumerate((gamma1, beta1, bias1, gamma2, beta2, bias2, bias3)):
        prm[r : r + 1, 0:Q] = ref[...]

    zero = jnp.zeros((3, C, W), BF)
    x3[:, :, 0:W] = zero
    x3[:, :, W + CELLS : 2 * W + CELLS] = zero
    act[...] = jnp.zeros_like(act)
    for dst in (wv1, wv2):
        dst[:, 9 * Q : KP, :] = jnp.zeros((3, KP - 9 * Q, C), BF)
    tmp[...] = jnp.zeros_like(tmp)
    er = lax.broadcasted_iota(jnp.int32, (2 * W, 2 * W), 0)
    ec = lax.broadcasted_iota(jnp.int32, (2 * W, 2 * W), 1)
    perm[...] = jnp.where(jnp.where(er < W, 2 * er, 2 * er - 2 * W + 1) == ec, 1.0, 0.0).astype(BF)

    barrier = pltpu.get_barrier_semaphore()
    for d in OFFSETS:
        pl.semaphore_signal(barrier, inc=1, device_id=tm(d), device_id_type=MESH)
    for d in range(1, nc):
        pl.semaphore_signal(barrier, inc=1, device_id=xp(d), device_id_type=MESH)

    for cp in loads:
        cp.wait()
    lat32[...] = lat_raw[...].astype(F32).reshape(Q * H, W)

    def frame_sums(slot, p1, p2):
        tmp[0:Q, :] = p1
        s1 = jnp.sum(tmp[...].T, axis=0, keepdims=True)
        tmp[0:Q, :] = p2
        s2 = jnp.sum(tmp[...].T, axis=0, keepdims=True)
        st_send[slot] = jnp.concatenate([s1, s2, jnp.zeros((6, 128), F32)], 0)

    p1 = jnp.zeros((Q, W), F32)
    p2 = jnp.zeros((Q, W), F32)
    for i in range(H):
        row = lat32[pl.ds(i, Q, stride=H), :]
        p1 = p1 + row
        p2 = p2 + row * row
        fr[0, 2, :, i * W : (i + 1) * W] = row.astype(BF)
    frame_sums(0, p1, p2)
    colp[...] = prm[...].T

    def prep_conv(src, dst):
        for b in range(3):
            turned = src[b].T
            for q in range(nc):
                place = lax.rem(q - c + 2 + nc, nc) * 3 + b
                dst[pl.ds(pl.multiple_of(place * Q, Q), Q), :] = turned[q * Q : (q + 1) * Q]

    for cp in wloads[0]:
        cp.wait()
    prep_conv(wv1, wt1)
    pl.semaphore_wait(barrier, len(OFFSETS) + nc - 1)

    def stats_copies(s):
        return [
            remote(st_send.at[s], st_recv.at[s, k], ss_sem.at[s, k], sr_sem.at[s, k], tm(d))
            for k, d in enumerate(OFFSETS)
        ]

    sibling = (t + 1 - 2 * core, c)

    def lanes(ch):
        return pl.ds(pl.multiple_of(ch * CW, CW), CW)

    def halo_copy(s, ch):
        return remote(
            fr.at[s, 2, :, lanes(ch)], fr.at[s, 0, :, lanes(ch)], hs_sem.at[s, 0, ch], hr_sem.at[s, 0, ch], tm(2)
        )

    def halo_across(s, ch):
        return remote(
            fr.at[s, 2 - 2 * core, :, lanes(ch)],
            fr.at[s, 1, :, lanes(ch)],
            hs_sem.at[s, 1, ch],
            hr_sem.at[s, 1, ch],
            sibling,
        )

    own_clip = clip[t]
    valid = []
    for d in (2, 1):
        src = lax.rem(t - d + nt, nt)
        valid.append(jnp.where((t - d >= 0) & (clip[src] == own_clip), 1.0, 0.0).astype(F32))
    valid.append(jnp.float32(1.0))

    lane = lax.broadcasted_iota(jnp.int32, (128, 128), 1)
    subl = lax.broadcasted_iota(jnp.int32, (128, 128), 0)
    ga = jnp.floor((subl.astype(F32) + 0.5) * (1.0 / PER_GROUP))
    gb = jnp.floor((lane.astype(F32) + 0.5) * (1.0 / PER_GROUP))
    gmat = jnp.where(ga == gb, 1.0, 0.0).astype(F32)

    def norm_params(s):
        total = st_send[s]
        frames = jnp.float32(1.0)
        for k, d in enumerate(OFFSETS):
            arrived(st_recv.at[s, k], ss_sem.at[s, k], sr_sem.at[s, k])
            src = lax.rem(t - d + nt, nt)
            inside = (t - d >= 0) & (t - d < nt)
            m = jnp.where(inside & (clip[src] == own_clip), 1.0, 0.0).astype(F32)
            total = total + m * st_recv[s, k]
            frames = frames + m
        grouped = jnp.dot(total, gmat, precision=lax.Precision.HIGHEST, preferred_element_type=F32)
        tmp[0:8, :] = grouped
        cols = tmp[...].T
        count = frames * float(PER_GROUP * CELLS)
        mean = cols[0:Q, 0:1] / count
        var = cols[0:Q, 1:2] / count - mean * mean
        inv = lax.rsqrt(var + EPSILON)
        return mean, inv * colp[0:Q, 3 * s : 3 * s + 1], colp[0:Q, 3 * s + 1 : 3 * s + 2]

    def fill_rows(s, f, ch, params):
        for r in range(2):
            cells = pl.ds(pl.multiple_of(ch * CW + r * W, W), W)
            v = fr[s, f, :, cells].astype(F32)
            u = (v - params[0]) * params[1] + params[2]
            u = u / (1.0 + jnp.exp(-u))
            if f < 2:
                u = u * valid[f]
            u = u.astype(BF)
            for a in range(3):
                o = r + 1 - a
                k = (a * 3 + f) * Q
                act[ch + 1 + o // 2, k : k + Q, (o % 2) * W : (o % 2 + 1) * W] = u

    first = lax.broadcasted_iota(jnp.int32, (Q, W), 1) == 0
    last = lax.broadcasted_iota(jnp.int32, (Q, W), 1) == W - 1
    low = slice(0, HQ)
    high = slice(HQ, Q)

    def ring_copy(s, kind, way, ch):
        if kind == 0:
            src = sb.at[s, ch, 0, high if way else low]
        elif kind == 1:
            src = sb.at[s, ch, 1, low] if way else sb.at[s, ch, 3, high]
        else:
            src = added.at[s, ch, way]
        return remote(
            src, rb.at[s, ch, kind, way], rs_sem.at[s, kind, way, ch], rr_sem.at[s, kind, way, ch], xp(3 if way else 1)
        )

    def ring_arrived(s, kind, way, ch):
        arrived(rb.at[s, ch, kind, way], rs_sem.at[s, kind, way, ch], rr_sem.at[s, kind, way, ch])

    def ring_add(s, ch):
        for way in range(2):
            ring_arrived(s, 0, way, ch)
            mine = sb[s, ch, 1, high] if way else sb[s, ch, 3, low]
            added[s, ch, way] = (mine.astype(F32) + rb[s, ch, 0, way].astype(F32)).astype(BF)
            ring_copy(s, 2, way, ch).start()

    def conv(s, wt, params):
        params = [jnp.broadcast_to(p, (Q, W)) for p in params]
        for ch in range(NCH):
            fill_rows(s, 2, ch, params)

        def contribute(lo, hi, ch):
            yb[lo * 3 * Q : hi * 3 * Q, :] = jnp.dot(
                wt[lo * 3 * Q : hi * 3 * Q, :], act[ch + 1], preferred_element_type=F32
            )
            for p in range(lo, hi):
                base = p * 3 * Q
                for h in range(2):
                    cells = slice(h * W, (h + 1) * W)
                    left = jnp.where(first, 0.0, pltpu.roll(yb[base : base + Q, cells], 1, 1))
                    right = jnp.where(last, 0.0, pltpu.roll(yb[base + 2 * Q : base + 3 * Q, cells], W - 1, 1))
                    sb[s, ch, p, :, cells] = (yb[base + Q : base + 2 * Q, cells] + left + right).astype(BF)
            for way in range(2):
                ring_copy(s, lo, way, ch).start()

        def chunk(step, carry):
            @pl.when(step < NCH)
            def _():
                arrived(fr.at[s, 0, :, lanes(step)], hs_sem.at[s, 0, step], hr_sem.at[s, 0, step])
                halo_across(s, step).start()
                fill_rows(s, 0, step, params)

            @pl.when((step >= 1) & (step < NCH + 1))
            def _():
                ch = step - 1
                arrived(fr.at[s, 1, :, lanes(ch)], hs_sem.at[s, 1, ch], hr_sem.at[s, 1, ch])
                fill_rows(s, 1, ch, params)

            @pl.when((step >= 2) & (step < NCH + 2))
            def _():
                contribute(0, 1, step - 2)

            @pl.when((step >= LAG_R) & (step < NCH + LAG_R))
            def _():
                contribute(1, 4, step - LAG_R)

            @pl.when(step >= LAG_S)
            def _():
                ring_add(s, step - LAG_S)

            return carry

        lax.fori_loop(0, NCH + LAG_S, chunk, 0)

    def gathered(s, ch):
        for kind in (1, 2):
            for way in range(2):
                ring_arrived(s, kind, way, ch)
        own = sb[s, ch, 2].astype(F32)
        top = own[low] + rb[s, ch, 2, 0].astype(F32) + rb[s, ch, 1, 1].astype(F32)
        bottom = own[high] + rb[s, ch, 1, 0].astype(F32) + rb[s, ch, 2, 1].astype(F32)
        return jnp.concatenate([top, bottom], 0) + colp[0:Q, 3 * s + 2 : 3 * s + 3]

    offset = pl.multiple_of(c * Q - half * 128, 32)

    def prep_three(f):
        taps = {}
        for a in range(3):
            for b in range(3):
                t3[a * 3 + b] = w3v[f, a, b].T
        m = valid[f]

        def tap(a, b):
            return t3[a * 3 + b, pl.ds(offset, Q), :].astype(F32)

        for pi in range(2):
            for block, di in enumerate((0, 1) if pi else (0, -1)):
                rows = ((0, 1), (2,))[block] if pi else ((1, 2), (0,))[block]
                sums = []
                for b in range(3):
                    v = tap(rows[0], b)
                    for a in rows[1:]:
                        v = v + tap(a, b)
                    sums.append(v * m if f < 2 else v)
                parts = (sums[0], sums[1] + sums[2], sums[0] + sums[1], sums[2])
                for k, part in enumerate(parts):
                    base = ((pi * 2 + block) * 4 + k) * Q
                    wf[base : base + Q, f * C : (f + 1) * C] = part.astype(BF)

    for cp in stats_copies(0):
        cp.start()
    for ch in range(NCH):
        halo_copy(0, ch).start()
    for cp in wloads[1]:
        cp.wait()
    prep_conv(wv2, wt2)
    w3load.wait()
    for f in range(3):
        prep_three(f)
    params = norm_params(0)
    conv(0, wt1, params)
    p1 = jnp.zeros((Q, W), F32)
    p2 = jnp.zeros((Q, W), F32)
    for ch in range(NCH):
        hidden = gathered(0, ch).astype(BF)
        fr[1, 2, :, ch * CW : (ch + 1) * CW] = hidden
        if ch < 2:
            halo_copy(1, ch).start()
        hidden = hidden.astype(F32)
        for h in range(2):
            row = hidden[:, h * W : (h + 1) * W]
            p1 = p1 + row
            p2 = p2 + row * row
    frame_sums(1, p1, p2)
    for cp in stats_copies(1):
        cp.start()
    for ch in range(2, NCH):
        halo_copy(1, ch).start()

    def sent(s):
        for cp in stats_copies(s):
            cp.wait_send()
        for ch in range(NCH):
            halo_copy(s, ch).wait_send()
            halo_across(s, ch).wait_send()

    sent(0)
    for ch in range(NCH):
        for kind in range(3):
            for way in range(2):
                ring_copy(0, kind, way, ch).wait_send()

    params = norm_params(1)
    conv(1, wt2, params)
    sent(1)

    def lanes_of(ch):
        return pl.ds(pl.multiple_of(W + ch * CW, W), CW)

    def own_x(d, ch):
        spot = x3.at[2, quarter(0), lanes_of(ch)]
        return remote(spot, spot, as_sem.at[d // 2, ch], ar_sem.at[d // 2, ch], xp(d))

    def half_quarter(d, part):
        return pl.ds(pl.multiple_of(lax.rem(c + d, nc) * Q + part * HQ, HQ), HQ)

    def pass_x(way, ch):
        spot = x3.at[2, half_quarter(1 if way else 3, way), lanes_of(ch)]
        return remote(spot, spot, ps_sem.at[way, ch], pr_sem.at[way, ch], xp(3 if way else 1))

    def pass_arrived(way, ch):
        arrived(x3.at[2, half_quarter(2, way), lanes_of(ch)], ps_sem.at[way, ch], pr_sem.at[way, ch])

    def own_z(k, ch):
        return remote(
            x3.at[2, quarter(2 * k), lanes_of(ch)],
            x3.at[0, quarter(2 * k), lanes_of(ch)],
            zs_sem.at[k, ch],
            zr_sem.at[k, ch],
            tm(2),
        )

    def back_x(d, ch):
        spot = x3.at[0, quarter(0), lanes_of(ch)]
        return remote(spot, spot, xs_sem.at[d // 2, ch], xr_sem.at[d // 2, ch], xp(d))

    def across(ch):
        return remote(
            x3.at[2 - 2 * core, :, lanes_of(ch)],
            x3.at[1, :, lanes_of(ch)],
            bs_sem.at[ch],
            br_sem.at[ch],
            sibling,
        )

    bias = colp[0:Q, 6:7]

    def rows_of(f0, f1, ch, di):
        lanes = pl.ds(pl.multiple_of((1 + di) * W + ch * CW, W), CW)
        return x3[f0:f1, :, lanes].reshape((f1 - f0) * C, CW)

    def partial(pi, f0, f1, ch):
        base = pi * 8 * Q
        k = slice(f0 * C, f1 * C)
        mid = jnp.dot(wf[base : base + C, k], rows_of(f0, f1, ch, 0), preferred_element_type=F32)
        edge = rows_of(f0, f1, ch, 1 if pi else -1)
        return mid + jnp.dot(wf[base + C : base + 2 * C, k], edge, preferred_element_type=F32)

    def result_copy(block):
        lines = pl.ds(pl.multiple_of(block * H, H), H)
        return pltpu.make_async_copy(done.at[block], out.at[0, :, lines, :], loc_sem.at[1 + block])

    def pipeline(step, carry):
        @pl.when(step < NCH)
        def _():
            ch = step
            cells = pl.ds(pl.multiple_of(ch * CW, CW), CW)
            residual = fr[0, 2, :, cells].astype(F32) + gathered(1, ch)
            x3[2, quarter(0), lanes_of(ch)] = residual.astype(BF)
            own_z(0, ch).start()
            for d in (1, 3):
                own_x(d, ch).start()

        @pl.when((step >= LAG_B) & (step < NCH + LAG_B))
        def _():
            ch = step - LAG_B
            for d in (1, 3):
                arrived(x3.at[2, quarter(4 - d), lanes_of(ch)], as_sem.at[d // 2, ch], ar_sem.at[d // 2, ch])
                pass_x(d // 2, ch).start()

        @pl.when((step >= LAG_K) & (step < NCH + LAG_K))
        def _():
            ch = step - LAG_K
            arrived(x3.at[0, quarter(0), lanes_of(ch)], zs_sem.at[0, ch], zr_sem.at[0, ch])
            for d in (1, 3):
                back_x(d, ch).start()

        @pl.when((step >= LAG_P) & (step < NCH + LAG_P))
        def _():
            ch = step - LAG_P
            for way in range(2):
                pass_arrived(way, ch)
            own_z(1, ch).start()
            for kind in range(3):
                for way in range(2):
                    ring_copy(1, kind, way, ch).wait_send()
            for d in (1, 3):
                own_x(d, ch).wait_send()
            own_z(0, ch).wait_send()

        @pl.when((step >= LAG_O) & (step < NCH + LAG_O))
        def _():
            ch = step - LAG_O
            for pi in range(2):
                y3[ch, pi] = partial(pi, 2, 3, ch)

        @pl.when((step >= LAG_D) & (step < NCH + LAG_D))
        def _():
            ch = step - LAG_D
            for way in range(2):
                pass_x(way, ch).wait_send()
            for d in (1, 3):
                back_x(d, ch).wait_send()
            own_z(1, ch).wait_send()
            arrived(x3.at[1, :, lanes_of(ch)], bs_sem.at[ch], br_sem.at[ch])

        @pl.when((step >= LAG_E) & (step < NCH + LAG_E))
        def _():
            ch = step - LAG_E
            for pi in range(2):
                y3[ch, pi] += partial(pi, 0, 2, ch)
                for h in range(2):
                    cells = slice(h * W, (h + 1) * W)
                    left = jnp.where(first, 0.0, pltpu.roll(y3[ch, pi, 0:Q, cells], 1, 1))
                    right = jnp.where(last, 0.0, pltpu.roll(y3[ch, pi, 3 * Q : 4 * Q, cells], W - 1, 1))
                    rows = slice((2 * h + pi) * Q, (2 * h + pi + 1) * Q)
                    both[rows, 0:W] = (y3[ch, pi, Q : 2 * Q, cells] + left + bias).astype(BF)
                    both[rows, W : 2 * W] = (y3[ch, pi, 2 * Q : 3 * Q, cells] + right + bias).astype(BF)
            spread = jnp.dot(both[...], perm[...], preferred_element_type=F32)
            for k in range(4):
                for g in range(2):
                    oscr[ch // 2, g, pl.ds(lax.rem(ch, 2) * 4 + k, Q, stride=H), :] = spread[k * Q : (k + 1) * Q, g * 128 : (g + 1) * 128]

            @pl.when(ch % 2 == 1)
            def _():
                block = ch // 2
                for g in range(2):
                    lines = oscr[block, g].reshape(Q, H, 128)
                    done[block, :, :, g * 128 : (g + 1) * 128] = lines.astype(BF)
                result_copy(block).start()

        @pl.when((step >= LAG_C) & (step < NCH + LAG_C))
        def _():
            ch = step - LAG_C
            for d in (1, 3):
                arrived(x3.at[0, quarter(4 - d), lanes_of(ch)], xs_sem.at[d // 2, ch], xr_sem.at[d // 2, ch])
            arrived(x3.at[0, quarter(2), lanes_of(ch)], zs_sem.at[1, ch], zr_sem.at[1, ch])
            across(ch).start()

        return carry

    lax.fori_loop(0, NCH + LAG_E, pipeline, 0)
    for ch in range(NCH):
        across(ch).wait_send()
    for block in range(2):
        result_copy(block).wait()


def on_device(nt, nc, *args):
    args = [a.reshape(1, Q) if a.ndim == 1 and a.dtype == F32 else a for a in args]
    anywhere = pl.BlockSpec(memory_space=pl.ANY)
    specs = [pl.BlockSpec(memory_space=pltpu.VMEM) if a.ndim == 2 else anywhere for a in args]
    specs[1] = pl.BlockSpec(memory_space=pltpu.SMEM)
    dma = pltpu.SemaphoreType.DMA
    scratch = [
        pltpu.VMEM((Q, H, W), BF),
        pltpu.VMEM((Q * H, W), F32),
        pltpu.VMEM((2, 3, Q, CELLS), BF),
        pltpu.VMEM((128, 128), F32),
        pltpu.VMEM((128, 128), F32),
        pltpu.VMEM((128, 128), F32),
        pltpu.VMEM((2, 8, 128), F32),
        pltpu.VMEM((2, len(OFFSETS), 8, 128), F32),
        pltpu.VMEM((3, KP, C), BF),
        pltpu.VMEM((3, KP, C), BF),
        pltpu.VMEM((3 * C, KP), BF),
        pltpu.VMEM((3 * C, KP), BF),
        pltpu.VMEM((3, 3, 3, C, 256), BF),
        pltpu.VMEM((9, 256, C), BF),
        pltpu.VMEM((16 * Q, 3 * C), BF),
        pltpu.VMEM((NCH + 2, KP, CW), BF),
        pltpu.VMEM((3 * C, CW), F32),
        pltpu.VMEM((2, NCH, 4, Q, CW), BF),
        pltpu.VMEM((2, NCH, 2, HQ, CW), BF),
        pltpu.VMEM((2, NCH, 3, 2, HQ, CW), BF),
        pltpu.VMEM((3, C, CELLS + 2 * W), BF),
        pltpu.VMEM((NCH, 2, C, CW), F32),
        pltpu.VMEM((C, 2 * W), BF),
        pltpu.VMEM((2 * W, 2 * W), BF),
        pltpu.VMEM((2, 2, Q * H, 128), F32),
        pltpu.VMEM((2, Q, H, 2 * W), BF),
        dma((3,)),
        dma((19,)),
        dma((2, 2, NCH)),
        dma((2, 2, NCH)),
        dma((2, len(OFFSETS))),
        dma((2, len(OFFSETS))),
        dma((2, 3, 2, NCH)),
        dma((2, 3, 2, NCH)),
        dma((2, NCH)),
        dma((2, NCH)),
        dma((2, NCH)),
        dma((2, NCH)),
        dma((2, NCH)),
        dma((2, NCH)),
        dma((2, NCH)),
        dma((2, NCH)),
        dma((NCH,)),
        dma((NCH,)),
    ]
    return pl.pallas_call(
        functools.partial(kernel, nt, nc),
        out_shape=jax.ShapeDtypeStruct((1, Q, 2 * H, 2 * W), BF),
        in_specs=specs,
        out_specs=pl.BlockSpec(memory_space=pl.ANY),
        scratch_shapes=scratch,
        compiler_params=pltpu.CompilerParams(
            collective_id=0, has_side_effects=True, vmem_limit_bytes=60 * 1024 * 1024
        ),
    )(*args)


def solution(mesh):
    in_specs = (
        P("tm", "chan", None, None),
        P(),
        P("chan"),
        P("chan"),
        P(None, None, None, "chan", None),
        P("chan"),
        P("chan"),
        P("chan"),
        P(None, None, None, "chan", None),
        P("chan"),
        P(),
        P("chan"),
    )
    return jax.shard_map(
        functools.partial(on_device, mesh.shape["tm"], mesh.shape["chan"]),
        mesh=mesh,
        in_specs=in_specs,
        out_specs=P("tm", "chan", None, None),
        check_vma=False,
    )
```

```python
import functools

import jax
import jax.numpy as jnp
from jax import lax
from jax.experimental import pallas as pl
from jax.experimental.pallas import tpu as pltpu
from jax.sharding import PartitionSpec as P

C = 384
GROUPS = 32
PER_GROUP = C // GROUPS
Q = 96
H = 8
W = 128
CELLS = H * W
NCH = 4
CW = CELLS // NCH
REACH = 7
HQ = Q // 2
LAG_R = 4
LAG_S = 5
LAG_B = 4
LAG_K = 7
LAG_P = 8
LAG_O = 9
LAG_C = 11
LAG_D = 12
LAG_E = 12
KP = 896
EPSILON = 1e-06
MESH = pl.DeviceIdType.MESH
BF = jnp.bfloat16
F32 = jnp.float32
OFFSETS = [d for d in range(-REACH, REACH + 1) if d != 0]


def kernel(
    nt,
    nc,
    lat_hbm,
    clip,
    gamma1,
    beta1,
    w1,
    bias1,
    gamma2,
    beta2,
    w2,
    bias2,
    w3,
    bias3,
    out,
    lat_raw,
    lat32,
    fr,
    prm,
    tmp,
    colp,
    st_send,
    st_recv,
    wv1,
    wv2,
    wt1,
    wt2,
    w3v,
    t3,
    wf,
    act,
    yb,
    sb,
    added,
    rb,
    x3,
    y3,
    both,
    perm,
    oscr,
    done,
    loc_sem,
    w_sem,
    hs_sem,
    hr_sem,
    ss_sem,
    sr_sem,
    rs_sem,
    rr_sem,
    as_sem,
    ar_sem,
    ps_sem,
    pr_sem,
    zs_sem,
    zr_sem,
    xs_sem,
    xr_sem,
    bs_sem,
    br_sem,
):
    t = lax.axis_index("tm")
    c = lax.axis_index("chan")
    core = lax.rem(t, 2)

    def tm(d):
        return (lax.rem(t + d + nt, nt), c)

    def xp(d):
        return (t, lax.rem(c + d, nc))

    def quarter(d):
        return pl.ds(pl.multiple_of(lax.rem(c + d, nc) * Q, Q), Q)

    def remote(src, dst, ssem, rsem, dev):
        return pltpu.make_async_remote_copy(
            src_ref=src, dst_ref=dst, send_sem=ssem, recv_sem=rsem, device_id=dev, device_id_type=MESH
        )

    def arrived(dst, ssem, rsem):
        remote(dst, dst, ssem, rsem, xp(1)).wait_recv()

    loads = [pltpu.make_async_copy(lat_hbm.at[0], lat_raw, loc_sem.at[0])]
    for cp in loads:
        cp.start()
    wloads = [[], []]
    for s, (src, dst) in enumerate(((w1, wv1), (w2, wv2))):
        for f in range(3):
            for a in range(3):
                wloads[s].append(
                    pltpu.make_async_copy(
                        src.at[f, a], dst.at[:, pl.ds((a * 3 + f) * Q, Q), :], w_sem.at[s * 9 + f * 3 + a]
                    )
                )
    for cp in wloads[0] + wloads[1]:
        cp.start()
    half = c // 2
    w3load = pltpu.make_async_copy(
        w3.at[:, :, :, :, pl.ds(pl.multiple_of(half * 128, 128), 256)], w3v, w_sem.at[18]
    )
    w3load.start()

    prm[...] = jnp.zeros_like(prm)
    for r, ref in enumerate((gamma1, beta1, bias1, gamma2, beta2, bias2, bias3)):
        prm[r : r + 1, 0:Q] = ref[...]

    zero = jnp.zeros((3, C, W), BF)
    x3[:, :, 0:W] = zero
    x3[:, :, W + CELLS : 2 * W + CELLS] = zero
    act[...] = jnp.zeros_like(act)
    for dst in (wv1, wv2):
        dst[:, 9 * Q : KP, :] = jnp.zeros((3, KP - 9 * Q, C), BF)
    tmp[...] = jnp.zeros_like(tmp)
    er = lax.broadcasted_iota(jnp.int32, (2 * W, 2 * W), 0)
    ec = lax.broadcasted_iota(jnp.int32, (2 * W, 2 * W), 1)
    perm[...] = jnp.where(jnp.where(er < W, 2 * er, 2 * er - 2 * W + 1) == ec, 1.0, 0.0).astype(BF)

    barrier = pltpu.get_barrier_semaphore()
    for d in OFFSETS:
        pl.semaphore_signal(barrier, inc=1, device_id=tm(d), device_id_type=MESH)
    for d in range(1, nc):
        pl.semaphore_signal(barrier, inc=1, device_id=xp(d), device_id_type=MESH)

    for cp in loads:
        cp.wait()
    lat32[...] = lat_raw[...].astype(F32).reshape(Q * H, W)

    def frame_sums(slot, p1, p2):
        tmp[0:Q, :] = p1
        s1 = jnp.sum(tmp[...].T, axis=0, keepdims=True)
        tmp[0:Q, :] = p2
        s2 = jnp.sum(tmp[...].T, axis=0, keepdims=True)
        st_send[slot] = jnp.concatenate([s1, s2, jnp.zeros((6, 128), F32)], 0)

    p1 = jnp.zeros((Q, W), F32)
    p2 = jnp.zeros((Q, W), F32)
    for i in range(H):
        row = lat32[pl.ds(i, Q, stride=H), :]
        p1 = p1 + row
        p2 = p2 + row * row
        fr[0, 2, :, i * W : (i + 1) * W] = row.astype(BF)
    frame_sums(0, p1, p2)
    colp[...] = prm[...].T

    def prep_conv(src, dst):
        for b in range(3):
            turned = src[b].T
            for q in range(nc):
                place = lax.rem(q - c + 2 + nc, nc) * 3 + b
                dst[pl.ds(pl.multiple_of(place * Q, Q), Q), :] = turned[q * Q : (q + 1) * Q]

    for cp in wloads[0]:
        cp.wait()
    prep_conv(wv1, wt1)
    pl.semaphore_wait(barrier, len(OFFSETS) + nc - 1)

    def stats_copies(s):
        return [
            remote(st_send.at[s], st_recv.at[s, k], ss_sem.at[s, k], sr_sem.at[s, k], tm(d))
            for k, d in enumerate(OFFSETS)
        ]

    sibling = (t + 1 - 2 * core, c)

    def lanes(ch):
        return pl.ds(pl.multiple_of(ch * CW, CW), CW)

    def halo_copy(s, ch):
        return remote(
            fr.at[s, 2, :, lanes(ch)], fr.at[s, 0, :, lanes(ch)], hs_sem.at[s, 0, ch], hr_sem.at[s, 0, ch], tm(2)
        )

    def halo_across(s, ch):
        return remote(
            fr.at[s, 2 - 2 * core, :, lanes(ch)],
            fr.at[s, 1, :, lanes(ch)],
            hs_sem.at[s, 1, ch],
            hr_sem.at[s, 1, ch],
            sibling,
        )

    own_clip = clip[t]
    valid = []
    for d in (2, 1):
        src = lax.rem(t - d + nt, nt)
        valid.append(jnp.where((t - d >= 0) & (clip[src] == own_clip), 1.0, 0.0).astype(F32))
    valid.append(jnp.float32(1.0))

    lane = lax.broadcasted_iota(jnp.int32, (128, 128), 1)
    subl = lax.broadcasted_iota(jnp.int32, (128, 128), 0)
    ga = jnp.floor((subl.astype(F32) + 0.5) * (1.0 / PER_GROUP))
    gb = jnp.floor((lane.astype(F32) + 0.5) * (1.0 / PER_GROUP))
    gmat = jnp.where(ga == gb, 1.0, 0.0).astype(F32)

    def norm_params(s):
        total = st_send[s]
        frames = jnp.float32(1.0)
        for k, d in enumerate(OFFSETS):
            arrived(st_recv.at[s, k], ss_sem.at[s, k], sr_sem.at[s, k])
            src = lax.rem(t - d + nt, nt)
            inside = (t - d >= 0) & (t - d < nt)
            m = jnp.where(inside & (clip[src] == own_clip), 1.0, 0.0).astype(F32)
            total = total + m * st_recv[s, k]
            frames = frames + m
        grouped = jnp.dot(total, gmat, precision=lax.Precision.HIGHEST, preferred_element_type=F32)
        tmp[0:8, :] = grouped
        cols = tmp[...].T
        count = frames * float(PER_GROUP * CELLS)
        mean = cols[0:Q, 0:1] / count
        var = cols[0:Q, 1:2] / count - mean * mean
        inv = lax.rsqrt(var + EPSILON)
        return mean, inv * colp[0:Q, 3 * s : 3 * s + 1], colp[0:Q, 3 * s + 1 : 3 * s + 2]

    def fill_rows(s, f, ch, params):
        for r in range(2):
            cells = pl.ds(pl.multiple_of(ch * CW + r * W, W), W)
            v = fr[s, f, :, cells].astype(F32)
            u = (v - params[0]) * params[1] + params[2]
            u = u / (1.0 + jnp.exp(-u))
            if f < 2:
                u = u * valid[f]
            u = u.astype(BF)
            for a in range(3):
                o = r + 1 - a
                k = (a * 3 + f) * Q
                act[ch + 1 + o // 2, k : k + Q, (o % 2) * W : (o % 2 + 1) * W] = u

    first = lax.broadcasted_iota(jnp.int32, (Q, W), 1) == 0
    last = lax.broadcasted_iota(jnp.int32, (Q, W), 1) == W - 1
    low = slice(0, HQ)
    high = slice(HQ, Q)

    def ring_copy(s, kind, way, ch):
        if kind == 0:
            src = sb.at[s, ch, 0, high if way else low]
        elif kind == 1:
            src = sb.at[s, ch, 1, low] if way else sb.at[s, ch, 3, high]
        else:
            src = added.at[s, ch, way]
        return remote(
            src, rb.at[s, ch, kind, way], rs_sem.at[s, kind, way, ch], rr_sem.at[s, kind, way, ch], xp(3 if way else 1)
        )

    def ring_arrived(s, kind, way, ch):
        arrived(rb.at[s, ch, kind, way], rs_sem.at[s, kind, way, ch], rr_sem.at[s, kind, way, ch])

    def ring_add(s, ch):
        for way in range(2):
            ring_arrived(s, 0, way, ch)
            mine = sb[s, ch, 1, high] if way else sb[s, ch, 3, low]
            added[s, ch, way] = (mine.astype(F32) + rb[s, ch, 0, way].astype(F32)).astype(BF)
            ring_copy(s, 2, way, ch).start()

    def conv(s, wt, params):
        params = [jnp.broadcast_to(p, (Q, W)) for p in params]
        for ch in range(NCH):
            fill_rows(s, 2, ch, params)

        def contribute(lo, hi, ch):
            yb[lo * 3 * Q : hi * 3 * Q, :] = jnp.dot(
                wt[lo * 3 * Q : hi * 3 * Q, :], act[ch + 1], preferred_element_type=F32
            )
            for p in range(lo, hi):
                base = p * 3 * Q
                for h in range(2):
                    cells = slice(h * W, (h + 1) * W)
                    left = jnp.where(first, 0.0, pltpu.roll(yb[base : base + Q, cells], 1, 1))
                    right = jnp.where(last, 0.0, pltpu.roll(yb[base + 2 * Q : base + 3 * Q, cells], W - 1, 1))
                    sb[s, ch, p, :, cells] = (yb[base + Q : base + 2 * Q, cells] + left + right).astype(BF)
            for way in range(2):
                ring_copy(s, lo, way, ch).start()

        def chunk(step, carry):
            @pl.when(step < NCH)
            def _():
                arrived(fr.at[s, 0, :, lanes(step)], hs_sem.at[s, 0, step], hr_sem.at[s, 0, step])
                halo_across(s, step).start()
                fill_rows(s, 0, step, params)

            @pl.when((step >= 1) & (step < NCH + 1))
            def _():
                ch = step - 1
                arrived(fr.at[s, 1, :, lanes(ch)], hs_sem.at[s, 1, ch], hr_sem.at[s, 1, ch])
                fill_rows(s, 1, ch, params)

            @pl.when((step >= 2) & (step < NCH + 2))
            def _():
                contribute(0, 1, step - 2)

            @pl.when((step >= LAG_R) & (step < NCH + LAG_R))
            def _():
                contribute(1, 4, step - LAG_R)

            @pl.when(step >= LAG_S)
            def _():
                ring_add(s, step - LAG_S)

            return carry

        lax.fori_loop(0, NCH + LAG_S, chunk, 0)

    def gathered(s, ch):
        for kind in (1, 2):
            for way in range(2):
                ring_arrived(s, kind, way, ch)
        own = sb[s, ch, 2].astype(F32)
        top = own[low] + rb[s, ch, 2, 0].astype(F32) + rb[s, ch, 1, 1].astype(F32)
        bottom = own[high] + rb[s, ch, 1, 0].astype(F32) + rb[s, ch, 2, 1].astype(F32)
        return jnp.concatenate([top, bottom], 0) + colp[0:Q, 3 * s + 2 : 3 * s + 3]

    offset = pl.multiple_of(c * Q - half * 128, 32)

    def prep_three(f):
        taps = {}
        for a in range(3):
            for b in range(3):
                t3[a * 3 + b] = w3v[f, a, b].T
        m = valid[f]

        def tap(a, b):
            return t3[a * 3 + b, pl.ds(offset, Q), :].astype(F32)

        for pi in range(2):
            for block, di in enumerate((0, 1) if pi else (0, -1)):
                rows = ((0, 1), (2,))[block] if pi else ((1, 2), (0,))[block]
                sums = []
                for b in range(3):
                    v = tap(rows[0], b)
                    for a in rows[1:]:
                        v = v + tap(a, b)
                    sums.append(v * m if f < 2 else v)
                parts = (sums[0], sums[1] + sums[2], sums[0] + sums[1], sums[2])
                for k, part in enumerate(parts):
                    base = ((pi * 2 + block) * 4 + k) * Q
                    wf[base : base + Q, f * C : (f + 1) * C] = part.astype(BF)

    for cp in stats_copies(0):
        cp.start()
    for ch in range(NCH):
        halo_copy(0, ch).start()
    for cp in wloads[1]:
        cp.wait()
    prep_conv(wv2, wt2)
    w3load.wait()
    for f in range(3):
        prep_three(f)
    params = norm_params(0)
    conv(0, wt1, params)
    p1 = jnp.zeros((Q, W), F32)
    p2 = jnp.zeros((Q, W), F32)
    for ch in range(NCH):
        hidden = gathered(0, ch).astype(BF)
        fr[1, 2, :, ch * CW : (ch + 1) * CW] = hidden
        if ch < 2:
            halo_copy(1, ch).start()
        hidden = hidden.astype(F32)
        for h in range(2):
            row = hidden[:, h * W : (h + 1) * W]
            p1 = p1 + row
            p2 = p2 + row * row
    frame_sums(1, p1, p2)
    for cp in stats_copies(1):
        cp.start()
    for ch in range(2, NCH):
        halo_copy(1, ch).start()

    def sent(s):
        for cp in stats_copies(s):
            cp.wait_send()
        for ch in range(NCH):
            halo_copy(s, ch).wait_send()
            halo_across(s, ch).wait_send()

    sent(0)
    for ch in range(NCH):
        for kind in range(3):
            for way in range(2):
                ring_copy(0, kind, way, ch).wait_send()

    params = norm_params(1)
    conv(1, wt2, params)
    sent(1)

    def lanes_of(ch):
        return pl.ds(pl.multiple_of(W + ch * CW, W), CW)

    def own_x(d, ch):
        spot = x3.at[2, quarter(0), lanes_of(ch)]
        return remote(spot, spot, as_sem.at[d // 2, ch], ar_sem.at[d // 2, ch], xp(d))

    def half_quarter(d, part):
        return pl.ds(pl.multiple_of(lax.rem(c + d, nc) * Q + part * HQ, HQ), HQ)

    def pass_x(way, ch):
        spot = x3.at[2, half_quarter(1 if way else 3, way), lanes_of(ch)]
        return remote(spot, spot, ps_sem.at[way, ch], pr_sem.at[way, ch], xp(3 if way else 1))

    def far_x(ch):
        spot = x3.at[2, quarter(0), lanes_of(ch)]
        return remote(spot, spot, ps_sem.at[0, ch], pr_sem.at[0, ch], xp(2))

    def pass_arrived(way, ch):
        arrived(x3.at[2, half_quarter(2, way), lanes_of(ch)], ps_sem.at[way, ch], pr_sem.at[way, ch])

    def own_z(k, ch):
        return remote(
            x3.at[2, quarter(2 * k), lanes_of(ch)],
            x3.at[0, quarter(2 * k), lanes_of(ch)],
            zs_sem.at[k, ch],
            zr_sem.at[k, ch],
            tm(2),
        )

    def back_x(d, ch):
        spot = x3.at[0, quarter(0), lanes_of(ch)]
        return remote(spot, spot, xs_sem.at[d // 2, ch], xr_sem.at[d // 2, ch], xp(d))

    def across(ch):
        return remote(
            x3.at[2 - 2 * core, :, lanes_of(ch)],
            x3.at[1, :, lanes_of(ch)],
            bs_sem.at[ch],
            br_sem.at[ch],
            sibling,
        )

    bias = colp[0:Q, 6:7]

    def rows_of(f0, f1, ch, di):
        lanes = pl.ds(pl.multiple_of((1 + di) * W + ch * CW, W), CW)
        return x3[f0:f1, :, lanes].reshape((f1 - f0) * C, CW)

    def late_edge(ch):
        k = slice(0, 2 * C)
        base = 3 * C
        lanes = pl.ds(pl.multiple_of(3 * W + ch * CW, W), W)
        rows = x3[0:2, :, lanes].reshape(2 * C, W)
        y3[ch, 1, :, W:CW] += jnp.dot(wf[base : base + C, k], rows, preferred_element_type=F32)

    def early(ch):
        k = slice(0, 2 * C)
        y3[ch, 0] += partial(0, 0, 2, ch)
        y3[ch, 1] += jnp.dot(wf[2 * C : 3 * C, k], rows_of(0, 2, ch, 0), preferred_element_type=F32)
        lanes = pl.ds(pl.multiple_of(2 * W + ch * CW, W), W)
        rows = x3[0:2, :, lanes].reshape(2 * C, W)
        y3[ch, 1, :, 0:W] += jnp.dot(wf[3 * C : 4 * C, k], rows, preferred_element_type=F32)

    def line_to(place, ch, h, pi):
        cells = slice(h * W, (h + 1) * W)
        left = jnp.where(first, 0.0, pltpu.roll(y3[ch, pi, 0:Q, cells], 1, 1))
        right = jnp.where(last, 0.0, pltpu.roll(y3[ch, pi, 3 * Q : 4 * Q, cells], W - 1, 1))
        rows = slice(place * Q, (place + 1) * Q)
        both[rows, 0:W] = (y3[ch, pi, Q : 2 * Q, cells] + left + bias).astype(BF)
        both[rows, W : 2 * W] = (y3[ch, pi, 2 * Q : 3 * Q, cells] + right + bias).astype(BF)

    def lines_out(count, start):
        spread = jnp.dot(both[0 : count * Q, :], perm[...], preferred_element_type=F32)
        for k in range(count):
            for g in range(2):
                oscr[g, pl.ds(start + H + k, Q, stride=3 * H), :] = spread[k * Q : (k + 1) * Q, g * 128 : (g + 1) * 128]

    def block_out(block):
        for g in range(2):
            lines = oscr[g].reshape(Q, 3, H, 128)[:, 1 + block]
            done[block, :, :, g * 128 : (g + 1) * 128] = lines.astype(BF)
        result_copy(block).start()

    def partial(pi, f0, f1, ch):
        base = pi * 8 * Q
        k = slice(f0 * C, f1 * C)
        mid = jnp.dot(wf[base : base + C, k], rows_of(f0, f1, ch, 0), preferred_element_type=F32)
        edge = rows_of(f0, f1, ch, 1 if pi else -1)
        return mid + jnp.dot(wf[base + C : base + 2 * C, k], edge, preferred_element_type=F32)

    def result_copy(block):
        lines = pl.ds(pl.multiple_of(block * H, H), H)
        return pltpu.make_async_copy(done.at[block], out.at[0, :, lines, :], loc_sem.at[1 + block])

    def pipeline(step, carry):
        @pl.when(step < NCH)
        def _():
            ch = step
            cells = pl.ds(pl.multiple_of(ch * CW, CW), CW)
            residual = fr[0, 2, :, cells].astype(F32) + gathered(1, ch)
            x3[2, quarter(0), lanes_of(ch)] = residual.astype(BF)
            own_z(0, ch).start()
            for d in (1, 3):
                own_x(d, ch).start()

            @pl.when(ch == NCH - 1)
            def _():
                far_x(ch).start()

        @pl.when((step >= LAG_B) & (step < NCH + LAG_B))
        def _():
            ch = step - LAG_B
            for d in (1, 3):
                arrived(x3.at[2, quarter(4 - d), lanes_of(ch)], as_sem.at[d // 2, ch], ar_sem.at[d // 2, ch])

                @pl.when(ch < NCH - 1)
                def _():
                    pass_x(d // 2, ch).start()

        @pl.when((step >= LAG_K) & (step < NCH + LAG_K))
        def _():
            ch = step - LAG_K
            arrived(x3.at[0, quarter(0), lanes_of(ch)], zs_sem.at[0, ch], zr_sem.at[0, ch])
            for d in (1, 3):
                back_x(d, ch).start()

        @pl.when((step >= LAG_P) & (step < NCH + LAG_P))
        def _():
            ch = step - LAG_P

            @pl.when(ch < NCH - 1)
            def _():
                for way in range(2):
                    pass_arrived(way, ch)

            @pl.when(ch == NCH - 1)
            def _():
                arrived(x3.at[2, quarter(2), lanes_of(ch)], ps_sem.at[0, ch], pr_sem.at[0, ch])

            own_z(1, ch).start()
            for kind in range(3):
                for way in range(2):
                    ring_copy(1, kind, way, ch).wait_send()
            for d in (1, 3):
                own_x(d, ch).wait_send()
            own_z(0, ch).wait_send()

        @pl.when((step >= LAG_O) & (step < NCH + LAG_O))
        def _():
            ch = step - LAG_O
            for pi in range(2):
                y3[ch, pi] = partial(pi, 2, 3, ch)

        @pl.when((step >= LAG_D) & (step < NCH + LAG_D))
        def _():
            ch = step - LAG_D

            @pl.when(ch < NCH - 1)
            def _():
                for way in range(2):
                    pass_x(way, ch).wait_send()

            @pl.when(ch == NCH - 1)
            def _():
                far_x(ch).wait_send()

            for d in (1, 3):
                back_x(d, ch).wait_send()
            own_z(1, ch).wait_send()
            arrived(x3.at[1, :, lanes_of(ch)], bs_sem.at[ch], br_sem.at[ch])

        @pl.when((step >= LAG_E) & (step < NCH + LAG_E))
        def _():
            ch = step - LAG_E
            before = lax.rem(ch + NCH - 1, NCH)

            @pl.when(ch > 0)
            def _():
                late_edge(before)

            early(ch)
            line_to(0, before, 1, 1)
            line_to(1, ch, 0, 0)
            line_to(2, ch, 0, 1)
            line_to(3, ch, 1, 0)
            lines_out(4, ch * 4 - 1)

            @pl.when(ch == 2)
            def _():
                block_out(0)

        @pl.when((step >= LAG_C) & (step < NCH + LAG_C))
        def _():
            ch = step - LAG_C
            for d in (1, 3):
                arrived(x3.at[0, quarter(4 - d), lanes_of(ch)], xs_sem.at[d // 2, ch], xr_sem.at[d // 2, ch])
            arrived(x3.at[0, quarter(2), lanes_of(ch)], zs_sem.at[1, ch], zr_sem.at[1, ch])
            across(ch).start()

        return carry

    lax.fori_loop(0, NCH + LAG_E, pipeline, 0)
    line_to(0, NCH - 1, 1, 1)
    lines_out(1, 2 * H - 1)
    block_out(1)
    for ch in range(NCH):
        across(ch).wait_send()
    for block in range(2):
        result_copy(block).wait()


def on_device(nt, nc, *args):
    args = [a.reshape(1, Q) if a.ndim == 1 and a.dtype == F32 else a for a in args]
    anywhere = pl.BlockSpec(memory_space=pl.ANY)
    specs = [pl.BlockSpec(memory_space=pltpu.VMEM) if a.ndim == 2 else anywhere for a in args]
    specs[1] = pl.BlockSpec(memory_space=pltpu.SMEM)
    dma = pltpu.SemaphoreType.DMA
    scratch = [
        pltpu.VMEM((Q, H, W), BF),
        pltpu.VMEM((Q * H, W), F32),
        pltpu.VMEM((2, 3, Q, CELLS), BF),
        pltpu.VMEM((128, 128), F32),
        pltpu.VMEM((128, 128), F32),
        pltpu.VMEM((128, 128), F32),
        pltpu.VMEM((2, 8, 128), F32),
        pltpu.VMEM((2, len(OFFSETS), 8, 128), F32),
        pltpu.VMEM((3, KP, C), BF),
        pltpu.VMEM((3, KP, C), BF),
        pltpu.VMEM((3 * C, KP), BF),
        pltpu.VMEM((3 * C, KP), BF),
        pltpu.VMEM((3, 3, 3, C, 256), BF),
        pltpu.VMEM((9, 256, C), BF),
        pltpu.VMEM((16 * Q, 3 * C), BF),
        pltpu.VMEM((NCH + 2, KP, CW), BF),
        pltpu.VMEM((3 * C, CW), F32),
        pltpu.VMEM((2, NCH, 4, Q, CW), BF),
        pltpu.VMEM((2, NCH, 2, HQ, CW), BF),
        pltpu.VMEM((2, NCH, 3, 2, HQ, CW), BF),
        pltpu.VMEM((3, C, CELLS + 2 * W), BF),
        pltpu.VMEM((NCH, 2, C, CW), F32),
        pltpu.VMEM((C, 2 * W), BF),
        pltpu.VMEM((2 * W, 2 * W), BF),
        pltpu.VMEM((2, Q * 3 * H, 128), F32),
        pltpu.VMEM((2, Q, H, 2 * W), BF),
        dma((3,)),
        dma((19,)),
        dma((2, 2, NCH)),
        dma((2, 2, NCH)),
        dma((2, len(OFFSETS))),
        dma((2, len(OFFSETS))),
        dma((2, 3, 2, NCH)),
        dma((2, 3, 2, NCH)),
        dma((2, NCH)),
        dma((2, NCH)),
        dma((2, NCH)),
        dma((2, NCH)),
        dma((2, NCH)),
        dma((2, NCH)),
        dma((2, NCH)),
        dma((2, NCH)),
        dma((NCH,)),
        dma((NCH,)),
    ]
    return pl.pallas_call(
        functools.partial(kernel, nt, nc),
        out_shape=jax.ShapeDtypeStruct((1, Q, 2 * H, 2 * W), BF),
        in_specs=specs,
        out_specs=pl.BlockSpec(memory_space=pl.ANY),
        scratch_shapes=scratch,
        compiler_params=pltpu.CompilerParams(
            collective_id=0, has_side_effects=True, vmem_limit_bytes=60 * 1024 * 1024
        ),
    )(*args)


def solution(mesh):
    in_specs = (
        P("tm", "chan", None, None),
        P(),
        P("chan"),
        P("chan"),
        P(None, None, None, "chan", None),
        P("chan"),
        P("chan"),
        P("chan"),
        P(None, None, None, "chan", None),
        P("chan"),
        P(),
        P("chan"),
    )
    return jax.shard_map(
        functools.partial(on_device, mesh.shape["tm"], mesh.shape["chan"]),
        mesh=mesh,
        in_specs=in_specs,
        out_specs=P("tm", "chan", None, None),
        check_vma=False,
    )
```

```python
import functools

import jax
import jax.numpy as jnp
from jax import lax
from jax.experimental import pallas as pl
from jax.experimental.pallas import tpu as pltpu
from jax.sharding import PartitionSpec as P

C = 384
GROUPS = 32
PER_GROUP = C // GROUPS
Q = 96
H = 8
W = 128
CELLS = H * W
NCH = 4
CW = CELLS // NCH
REACH = 7
HQ = Q // 2
LAG_R = 4
LAG_S = 5
LAG_P = 3
LAG_K = 3
LAG_O = 5
LAG_C = 6
LAG_D = 7
LAG_E = 8
KP = 896
EPSILON = 1e-06
MESH = pl.DeviceIdType.MESH
BF = jnp.bfloat16
F32 = jnp.float32
OFFSETS = [d for d in range(-REACH, REACH + 1) if d != 0]


def kernel(
    nt,
    nc,
    lat_hbm,
    clip,
    gamma1,
    beta1,
    w1,
    bias1,
    gamma2,
    beta2,
    w2,
    bias2,
    w3,
    bias3,
    out,
    lat_raw,
    lat32,
    fr,
    prm,
    tmp,
    colp,
    st_send,
    st_recv,
    wv1,
    wv2,
    wt1,
    wt2,
    w3v,
    t3,
    wf,
    act,
    yb,
    sb,
    added,
    rb,
    x3,
    y3,
    both,
    perm,
    oscr,
    done,
    loc_sem,
    w_sem,
    hs_sem,
    hr_sem,
    ss_sem,
    sr_sem,
    rs_sem,
    rr_sem,
    as_sem,
    ar_sem,
    zs_sem,
    zr_sem,
    xs_sem,
    xr_sem,
    bs_sem,
    br_sem,
):
    t = lax.axis_index("tm")
    c = lax.axis_index("chan")
    core = lax.rem(t, 2)

    def tm(d):
        return (lax.rem(t + d + nt, nt), c)

    def xp(d):
        return (t, lax.rem(c + d, nc))

    def quarter(d):
        return pl.ds(pl.multiple_of(lax.rem(c + d, nc) * Q, Q), Q)

    def remote(src, dst, ssem, rsem, dev):
        return pltpu.make_async_remote_copy(
            src_ref=src, dst_ref=dst, send_sem=ssem, recv_sem=rsem, device_id=dev, device_id_type=MESH
        )

    def arrived(dst, ssem, rsem):
        remote(dst, dst, ssem, rsem, xp(1)).wait_recv()

    loads = [pltpu.make_async_copy(lat_hbm.at[0], lat_raw, loc_sem.at[0])]
    for cp in loads:
        cp.start()
    wloads = [[], []]
    for s, (src, dst) in enumerate(((w1, wv1), (w2, wv2))):
        for f in range(3):
            for a in range(3):
                wloads[s].append(
                    pltpu.make_async_copy(
                        src.at[f, a], dst.at[:, pl.ds((a * 3 + f) * Q, Q), :], w_sem.at[s * 9 + f * 3 + a]
                    )
                )
    for cp in wloads[0] + wloads[1]:
        cp.start()
    half = c // 2
    w3load = pltpu.make_async_copy(
        w3.at[:, :, :, :, pl.ds(pl.multiple_of(half * 128, 128), 256)], w3v, w_sem.at[18]
    )
    w3load.start()

    prm[...] = jnp.zeros_like(prm)
    for r, ref in enumerate((gamma1, beta1, bias1, gamma2, beta2, bias2, bias3)):
        prm[r : r + 1, 0:Q] = ref[...]

    zero = jnp.zeros((3, C, W), BF)
    x3[:, :, 0:W] = zero
    x3[:, :, W + CELLS : 2 * W + CELLS] = zero
    act[...] = jnp.zeros_like(act)
    for dst in (wv1, wv2):
        dst[:, 9 * Q : KP, :] = jnp.zeros((3, KP - 9 * Q, C), BF)
    tmp[...] = jnp.zeros_like(tmp)
    er = lax.broadcasted_iota(jnp.int32, (2 * W, 2 * W), 0)
    ec = lax.broadcasted_iota(jnp.int32, (2 * W, 2 * W), 1)
    perm[...] = jnp.where(jnp.where(er < W, 2 * er, 2 * er - 2 * W + 1) == ec, 1.0, 0.0).astype(BF)

    barrier = pltpu.get_barrier_semaphore()
    for d in OFFSETS:
        pl.semaphore_signal(barrier, inc=1, device_id=tm(d), device_id_type=MESH)
    for d in range(1, nc):
        pl.semaphore_signal(barrier, inc=1, device_id=xp(d), device_id_type=MESH)

    for cp in loads:
        cp.wait()
    lat32[...] = lat_raw[...].astype(F32).reshape(Q * H, W)

    def frame_sums(slot, p1, p2):
        tmp[0:Q, :] = p1
        s1 = jnp.sum(tmp[...].T, axis=0, keepdims=True)
        tmp[0:Q, :] = p2
        s2 = jnp.sum(tmp[...].T, axis=0, keepdims=True)
        st_send[slot] = jnp.concatenate([s1, s2, jnp.zeros((6, 128), F32)], 0)

    p1 = jnp.zeros((Q, W), F32)
    p2 = jnp.zeros((Q, W), F32)
    for i in range(H):
        row = lat32[pl.ds(i, Q, stride=H), :]
        p1 = p1 + row
        p2 = p2 + row * row
        fr[0, 2, :, i * W : (i + 1) * W] = row.astype(BF)
    frame_sums(0, p1, p2)
    colp[...] = prm[...].T

    def prep_conv(src, dst):
        for b in range(3):
            turned = src[b].T
            for q in range(nc):
                place = lax.rem(q - c + 2 + nc, nc) * 3 + b
                dst[pl.ds(pl.multiple_of(place * Q, Q), Q), :] = turned[q * Q : (q + 1) * Q]

    for cp in wloads[0]:
        cp.wait()
    prep_conv(wv1, wt1)
    pl.semaphore_wait(barrier, len(OFFSETS) + nc - 1)

    def stats_copies(s):
        return [
            remote(st_send.at[s], st_recv.at[s, k], ss_sem.at[s, k], sr_sem.at[s, k], tm(d))
            for k, d in enumerate(OFFSETS)
        ]

    sibling = (t + 1 - 2 * core, c)

    def lanes(ch):
        return pl.ds(pl.multiple_of(ch * CW, CW), CW)

    def halo_copy(s, ch):
        return remote(
            fr.at[s, 2, :, lanes(ch)], fr.at[s, 0, :, lanes(ch)], hs_sem.at[s, 0, ch], hr_sem.at[s, 0, ch], tm(2)
        )

    def halo_across(s, ch):
        return remote(
            fr.at[s, 2 - 2 * core, :, lanes(ch)],
            fr.at[s, 1, :, lanes(ch)],
            hs_sem.at[s, 1, ch],
            hr_sem.at[s, 1, ch],
            sibling,
        )

    own_clip = clip[t]
    valid = []
    for d in (2, 1):
        src = lax.rem(t - d + nt, nt)
        valid.append(jnp.where((t - d >= 0) & (clip[src] == own_clip), 1.0, 0.0).astype(F32))
    valid.append(jnp.float32(1.0))

    lane = lax.broadcasted_iota(jnp.int32, (128, 128), 1)
    subl = lax.broadcasted_iota(jnp.int32, (128, 128), 0)
    ga = jnp.floor((subl.astype(F32) + 0.5) * (1.0 / PER_GROUP))
    gb = jnp.floor((lane.astype(F32) + 0.5) * (1.0 / PER_GROUP))
    gmat = jnp.where(ga == gb, 1.0, 0.0).astype(F32)

    def norm_params(s):
        total = st_send[s]
        frames = jnp.float32(1.0)
        for k, d in enumerate(OFFSETS):
            arrived(st_recv.at[s, k], ss_sem.at[s, k], sr_sem.at[s, k])
            src = lax.rem(t - d + nt, nt)
            inside = (t - d >= 0) & (t - d < nt)
            m = jnp.where(inside & (clip[src] == own_clip), 1.0, 0.0).astype(F32)
            total = total + m * st_recv[s, k]
            frames = frames + m
        grouped = jnp.dot(total, gmat, precision=lax.Precision.HIGHEST, preferred_element_type=F32)
        tmp[0:8, :] = grouped
        cols = tmp[...].T
        count = frames * float(PER_GROUP * CELLS)
        mean = cols[0:Q, 0:1] / count
        var = cols[0:Q, 1:2] / count - mean * mean
        inv = lax.rsqrt(var + EPSILON)
        return mean, inv * colp[0:Q, 3 * s : 3 * s + 1], colp[0:Q, 3 * s + 1 : 3 * s + 2]

    def fill_rows(s, f, ch, params):
        for r in range(2):
            cells = pl.ds(pl.multiple_of(ch * CW + r * W, W), W)
            v = fr[s, f, :, cells].astype(F32)
            u = (v - params[0]) * params[1] + params[2]
            u = u / (1.0 + jnp.exp(-u))
            if f < 2:
                u = u * valid[f]
            u = u.astype(BF)
            for a in range(3):
                o = r + 1 - a
                k = (a * 3 + f) * Q
                act[ch + 1 + o // 2, k : k + Q, (o % 2) * W : (o % 2 + 1) * W] = u

    first = lax.broadcasted_iota(jnp.int32, (Q, W), 1) == 0
    last = lax.broadcasted_iota(jnp.int32, (Q, W), 1) == W - 1
    low = slice(0, HQ)
    high = slice(HQ, Q)

    def ring_copy(s, kind, way, ch):
        if kind == 0:
            src = sb.at[s, ch, 0, high if way else low]
        elif kind == 1:
            src = sb.at[s, ch, 1, low] if way else sb.at[s, ch, 3, high]
        else:
            src = added.at[s, ch, way]
        return remote(
            src, rb.at[s, ch, kind, way], rs_sem.at[s, kind, way, ch], rr_sem.at[s, kind, way, ch], xp(3 if way else 1)
        )

    def ring_arrived(s, kind, way, ch):
        arrived(rb.at[s, ch, kind, way], rs_sem.at[s, kind, way, ch], rr_sem.at[s, kind, way, ch])

    def ring_add(s, ch):
        for way in range(2):
            ring_arrived(s, 0, way, ch)
            mine = sb[s, ch, 1, high] if way else sb[s, ch, 3, low]
            added[s, ch, way] = (mine.astype(F32) + rb[s, ch, 0, way].astype(F32)).astype(BF)
            ring_copy(s, 2, way, ch).start()

    def conv(s, wt, params):
        params = [jnp.broadcast_to(p, (Q, W)) for p in params]
        for ch in range(NCH):
            fill_rows(s, 2, ch, params)

        def contribute(lo, hi, ch):
            yb[lo * 3 * Q : hi * 3 * Q, :] = jnp.dot(
                wt[lo * 3 * Q : hi * 3 * Q, :], act[ch + 1], preferred_element_type=F32
            )
            for p in range(lo, hi):
                base = p * 3 * Q
                for h in range(2):
                    cells = slice(h * W, (h + 1) * W)
                    left = jnp.where(first, 0.0, pltpu.roll(yb[base : base + Q, cells], 1, 1))
                    right = jnp.where(last, 0.0, pltpu.roll(yb[base + 2 * Q : base + 3 * Q, cells], W - 1, 1))
                    sb[s, ch, p, :, cells] = (yb[base + Q : base + 2 * Q, cells] + left + right).astype(BF)
            for way in range(2):
                ring_copy(s, lo, way, ch).start()

        def chunk(step, carry):
            @pl.when(step < NCH)
            def _():
                arrived(fr.at[s, 0, :, lanes(step)], hs_sem.at[s, 0, step], hr_sem.at[s, 0, step])
                halo_across(s, step).start()
                fill_rows(s, 0, step, params)

            @pl.when((step >= 1) & (step < NCH + 1))
            def _():
                ch = step - 1
                arrived(fr.at[s, 1, :, lanes(ch)], hs_sem.at[s, 1, ch], hr_sem.at[s, 1, ch])
                fill_rows(s, 1, ch, params)

            @pl.when((step >= 2) & (step < NCH + 2))
            def _():
                contribute(0, 1, step - 2)

            @pl.when((step >= LAG_R) & (step < NCH + LAG_R))
            def _():
                contribute(1, 4, step - LAG_R)

            @pl.when(step >= LAG_S)
            def _():
                ring_add(s, step - LAG_S)

            return carry

        lax.fori_loop(0, NCH + LAG_S, chunk, 0)

    def gathered(s, ch):
        for kind in (1, 2):
            for way in range(2):
                ring_arrived(s, kind, way, ch)
        own = sb[s, ch, 2].astype(F32)
        top = own[low] + rb[s, ch, 2, 0].astype(F32) + rb[s, ch, 1, 1].astype(F32)
        bottom = own[high] + rb[s, ch, 1, 0].astype(F32) + rb[s, ch, 2, 1].astype(F32)
        return jnp.concatenate([top, bottom], 0) + colp[0:Q, 3 * s + 2 : 3 * s + 3]

    offset = pl.multiple_of(c * Q - half * 128, 32)

    def prep_three(f):
        taps = {}
        for a in range(3):
            for b in range(3):
                t3[a * 3 + b] = w3v[f, a, b].T
        m = valid[f]

        def tap(a, b):
            return t3[a * 3 + b, pl.ds(offset, Q), :].astype(F32)

        for pi in range(2):
            for block, di in enumerate((0, 1) if pi else (0, -1)):
                rows = ((0, 1), (2,))[block] if pi else ((1, 2), (0,))[block]
                sums = []
                for b in range(3):
                    v = tap(rows[0], b)
                    for a in rows[1:]:
                        v = v + tap(a, b)
                    sums.append(v * m if f < 2 else v)
                parts = (sums[0], sums[1] + sums[2], sums[0] + sums[1], sums[2])
                for k, part in enumerate(parts):
                    base = ((pi * 2 + block) * 4 + k) * Q
                    wf[base : base + Q, f * C : (f + 1) * C] = part.astype(BF)

    for cp in stats_copies(0):
        cp.start()
    for ch in range(NCH):
        halo_copy(0, ch).start()
    for cp in wloads[1]:
        cp.wait()
    prep_conv(wv2, wt2)
    w3load.wait()
    for f in range(3):
        prep_three(f)
    params = norm_params(0)
    conv(0, wt1, params)
    p1 = jnp.zeros((Q, W), F32)
    p2 = jnp.zeros((Q, W), F32)
    for ch in range(NCH):
        hidden = gathered(0, ch).astype(BF)
        fr[1, 2, :, ch * CW : (ch + 1) * CW] = hidden
        if ch < 2:
            halo_copy(1, ch).start()
        hidden = hidden.astype(F32)
        for h in range(2):
            row = hidden[:, h * W : (h + 1) * W]
            p1 = p1 + row
            p2 = p2 + row * row
    frame_sums(1, p1, p2)
    for cp in stats_copies(1):
        cp.start()
    for ch in range(2, NCH):
        halo_copy(1, ch).start()

    def sent(s):
        for cp in stats_copies(s):
            cp.wait_send()
        for ch in range(NCH):
            halo_copy(s, ch).wait_send()
            halo_across(s, ch).wait_send()

    sent(0)
    for ch in range(NCH):
        for kind in range(3):
            for way in range(2):
                ring_copy(0, kind, way, ch).wait_send()

    params = norm_params(1)
    conv(1, wt2, params)
    sent(1)

    def lanes_of(ch):
        return pl.ds(pl.multiple_of(W + ch * CW, W), CW)

    def own_x(d, ch):
        spot = x3.at[2, quarter(0), lanes_of(ch)]
        return remote(spot, spot, as_sem.at[d - 1, ch], ar_sem.at[d - 1, ch], xp(d))

    def half_quarter(d, part):
        return pl.ds(pl.multiple_of(lax.rem(c + d, nc) * Q + part * HQ, HQ), HQ)

    def own_z(k, ch):
        return remote(
            x3.at[2, quarter(2 * k), lanes_of(ch)],
            x3.at[0, quarter(2 * k), lanes_of(ch)],
            zs_sem.at[k, ch],
            zr_sem.at[k, ch],
            tm(2),
        )

    def back_x(d, ch):
        spot = x3.at[0, quarter(0), lanes_of(ch)]
        return remote(spot, spot, xs_sem.at[d // 2, ch], xr_sem.at[d // 2, ch], xp(d))

    def across(ch):
        return remote(
            x3.at[2 - 2 * core, :, lanes_of(ch)],
            x3.at[1, :, lanes_of(ch)],
            bs_sem.at[ch],
            br_sem.at[ch],
            sibling,
        )

    bias = colp[0:Q, 6:7]

    def rows_of(f0, f1, ch, di):
        lanes = pl.ds(pl.multiple_of((1 + di) * W + ch * CW, W), CW)
        return x3[f0:f1, :, lanes].reshape((f1 - f0) * C, CW)

    def partial(pi, f0, f1, ch):
        base = pi * 8 * Q
        k = slice(f0 * C, f1 * C)
        mid = jnp.dot(wf[base : base + C, k], rows_of(f0, f1, ch, 0), preferred_element_type=F32)
        edge = rows_of(f0, f1, ch, 1 if pi else -1)
        return mid + jnp.dot(wf[base + C : base + 2 * C, k], edge, preferred_element_type=F32)

    def result_copy(block):
        lines = pl.ds(pl.multiple_of(block * H, H), H)
        return pltpu.make_async_copy(done.at[block], out.at[0, :, lines, :], loc_sem.at[1 + block])

    def pipeline(step, carry):
        @pl.when(step < NCH)
        def _():
            ch = step
            cells = pl.ds(pl.multiple_of(ch * CW, CW), CW)
            residual = fr[0, 2, :, cells].astype(F32) + gathered(1, ch)
            x3[2, quarter(0), lanes_of(ch)] = residual.astype(BF)
            own_z(0, ch).start()
            for d in (2, 1, 3):
                own_x(d, ch).start()

        @pl.when((step >= LAG_P) & (step < NCH + LAG_P))
        def _():
            ch = step - LAG_P
            arrived(x3.at[2, quarter(2), lanes_of(ch)], as_sem.at[1, ch], ar_sem.at[1, ch])
            own_z(1, ch).start()
            for d in (1, 3):
                arrived(x3.at[2, quarter(4 - d), lanes_of(ch)], as_sem.at[d - 1, ch], ar_sem.at[d - 1, ch])
            for kind in range(3):
                for way in range(2):
                    ring_copy(1, kind, way, ch).wait_send()
            for d in (1, 2, 3):
                own_x(d, ch).wait_send()
            own_z(0, ch).wait_send()

        @pl.when((step >= LAG_K) & (step < NCH + LAG_K))
        def _():
            ch = step - LAG_K
            arrived(x3.at[0, quarter(0), lanes_of(ch)], zs_sem.at[0, ch], zr_sem.at[0, ch])
            for d in (1, 3):
                back_x(d, ch).start()

        @pl.when((step >= LAG_C) & (step < NCH + LAG_C))
        def _():
            ch = step - LAG_C
            for d in (1, 3):
                arrived(x3.at[0, quarter(4 - d), lanes_of(ch)], xs_sem.at[d // 2, ch], xr_sem.at[d // 2, ch])
            arrived(x3.at[0, quarter(2), lanes_of(ch)], zs_sem.at[1, ch], zr_sem.at[1, ch])
            across(ch).start()

        @pl.when((step >= LAG_O) & (step < NCH + LAG_O))
        def _():
            ch = step - LAG_O
            for pi in range(2):
                y3[ch, pi] = partial(pi, 2, 3, ch)

        @pl.when((step >= LAG_D) & (step < NCH + LAG_D))
        def _():
            ch = step - LAG_D
            for d in (1, 3):
                back_x(d, ch).wait_send()
            own_z(1, ch).wait_send()
            arrived(x3.at[1, :, lanes_of(ch)], bs_sem.at[ch], br_sem.at[ch])

        @pl.when((step >= LAG_E) & (step < NCH + LAG_E))
        def _():
            ch = step - LAG_E
            for pi in range(2):
                y3[ch, pi] += partial(pi, 0, 2, ch)
                for h in range(2):
                    cells = slice(h * W, (h + 1) * W)
                    left = jnp.where(first, 0.0, pltpu.roll(y3[ch, pi, 0:Q, cells], 1, 1))
                    right = jnp.where(last, 0.0, pltpu.roll(y3[ch, pi, 3 * Q : 4 * Q, cells], W - 1, 1))
                    rows = slice((2 * h + pi) * Q, (2 * h + pi + 1) * Q)
                    both[rows, 0:W] = (y3[ch, pi, Q : 2 * Q, cells] + left + bias).astype(BF)
                    both[rows, W : 2 * W] = (y3[ch, pi, 2 * Q : 3 * Q, cells] + right + bias).astype(BF)
            spread = jnp.dot(both[...], perm[...], preferred_element_type=F32)
            for k in range(4):
                for g in range(2):
                    oscr[ch // 2, g, pl.ds(lax.rem(ch, 2) * 4 + k, Q, stride=H), :] = spread[k * Q : (k + 1) * Q, g * 128 : (g + 1) * 128]

            @pl.when(ch % 2 == 1)
            def _():
                block = ch // 2
                for g in range(2):
                    lines = oscr[block, g].reshape(Q, H, 128)
                    done[block, :, :, g * 128 : (g + 1) * 128] = lines.astype(BF)
                result_copy(block).start()

        return carry

    lax.fori_loop(0, NCH + LAG_E, pipeline, 0)
    for ch in range(NCH):
        across(ch).wait_send()
    for block in range(2):
        result_copy(block).wait()


def on_device(nt, nc, *args):
    args = [a.reshape(1, Q) if a.ndim == 1 and a.dtype == F32 else a for a in args]
    anywhere = pl.BlockSpec(memory_space=pl.ANY)
    specs = [pl.BlockSpec(memory_space=pltpu.VMEM) if a.ndim == 2 else anywhere for a in args]
    specs[1] = pl.BlockSpec(memory_space=pltpu.SMEM)
    dma = pltpu.SemaphoreType.DMA
    scratch = [
        pltpu.VMEM((Q, H, W), BF),
        pltpu.VMEM((Q * H, W), F32),
        pltpu.VMEM((2, 3, Q, CELLS), BF),
        pltpu.VMEM((128, 128), F32),
        pltpu.VMEM((128, 128), F32),
        pltpu.VMEM((128, 128), F32),
        pltpu.VMEM((2, 8, 128), F32),
        pltpu.VMEM((2, len(OFFSETS), 8, 128), F32),
        pltpu.VMEM((3, KP, C), BF),
        pltpu.VMEM((3, KP, C), BF),
        pltpu.VMEM((3 * C, KP), BF),
        pltpu.VMEM((3 * C, KP), BF),
        pltpu.VMEM((3, 3, 3, C, 256), BF),
        pltpu.VMEM((9, 256, C), BF),
        pltpu.VMEM((16 * Q, 3 * C), BF),
        pltpu.VMEM((NCH + 2, KP, CW), BF),
        pltpu.VMEM((3 * C, CW), F32),
        pltpu.VMEM((2, NCH, 4, Q, CW), BF),
        pltpu.VMEM((2, NCH, 2, HQ, CW), BF),
        pltpu.VMEM((2, NCH, 3, 2, HQ, CW), BF),
        pltpu.VMEM((3, C, CELLS + 2 * W), BF),
        pltpu.VMEM((NCH, 2, C, CW), F32),
        pltpu.VMEM((C, 2 * W), BF),
        pltpu.VMEM((2 * W, 2 * W), BF),
        pltpu.VMEM((2, 2, Q * H, 128), F32),
        pltpu.VMEM((2, Q, H, 2 * W), BF),
        dma((3,)),
        dma((19,)),
        dma((2, 2, NCH)),
        dma((2, 2, NCH)),
        dma((2, len(OFFSETS))),
        dma((2, len(OFFSETS))),
        dma((2, 3, 2, NCH)),
        dma((2, 3, 2, NCH)),
        dma((3, NCH)),
        dma((3, NCH)),
        dma((2, NCH)),
        dma((2, NCH)),
        dma((2, NCH)),
        dma((2, NCH)),
        dma((NCH,)),
        dma((NCH,)),
    ]
    return pl.pallas_call(
        functools.partial(kernel, nt, nc),
        out_shape=jax.ShapeDtypeStruct((1, Q, 2 * H, 2 * W), BF),
        in_specs=specs,
        out_specs=pl.BlockSpec(memory_space=pl.ANY),
        scratch_shapes=scratch,
        compiler_params=pltpu.CompilerParams(
            collective_id=0, has_side_effects=True, vmem_limit_bytes=60 * 1024 * 1024
        ),
    )(*args)


def solution(mesh):
    in_specs = (
        P("tm", "chan", None, None),
        P(),
        P("chan"),
        P("chan"),
        P(None, None, None, "chan", None),
        P("chan"),
        P("chan"),
        P("chan"),
        P(None, None, None, "chan", None),
        P("chan"),
        P(),
        P("chan"),
    )
    return jax.shard_map(
        functools.partial(on_device, mesh.shape["tm"], mesh.shape["chan"]),
        mesh=mesh,
        in_specs=in_specs,
        out_specs=P("tm", "chan", None, None),
        check_vma=False,
    )
```

```python
import functools

import jax
import jax.numpy as jnp
from jax import lax
from jax.experimental import pallas as pl
from jax.experimental.pallas import tpu as pltpu
from jax.sharding import PartitionSpec as P

C = 384
GROUPS = 32
PER_GROUP = C // GROUPS
Q = 96
H = 8
W = 128
CELLS = H * W
NCH = 4
CW = CELLS // NCH
REACH = 7
HQ = Q // 2
LAG_R = 4
LAG_S = 5
LAG_P = 3
LAG_K = 3
LAG_O = 5
LAG_C = 6
LAG_D = 7
LAG_E = 8
KP = 896
EPSILON = 1e-06
MESH = pl.DeviceIdType.MESH
BF = jnp.bfloat16
F32 = jnp.float32
OFFSETS = [d for d in range(-REACH, REACH + 1) if d != 0]


def kernel(
    nt,
    nc,
    lat_hbm,
    clip,
    gamma1,
    beta1,
    w1,
    bias1,
    gamma2,
    beta2,
    w2,
    bias2,
    w3,
    bias3,
    out,
    lat_raw,
    lat32,
    fr,
    prm,
    tmp,
    colp,
    st_send,
    st_recv,
    wv1,
    wv2,
    wt1,
    wt2,
    w3v,
    t3,
    wf,
    act,
    yb,
    sb,
    added,
    rb,
    x3,
    y3,
    both,
    perm,
    oscr,
    done,
    loc_sem,
    w_sem,
    hs_sem,
    hr_sem,
    ss_sem,
    sr_sem,
    rs_sem,
    rr_sem,
    as_sem,
    ar_sem,
    zs_sem,
    zr_sem,
    xs_sem,
    xr_sem,
    bs_sem,
    br_sem,
):
    t = lax.axis_index("tm")
    c = lax.axis_index("chan")
    core = lax.rem(t, 2)

    def tm(d):
        return (lax.rem(t + d + nt, nt), c)

    def xp(d):
        return (t, lax.rem(c + d, nc))

    def quarter(d):
        return pl.ds(pl.multiple_of(lax.rem(c + d, nc) * Q, Q), Q)

    def remote(src, dst, ssem, rsem, dev):
        return pltpu.make_async_remote_copy(
            src_ref=src, dst_ref=dst, send_sem=ssem, recv_sem=rsem, device_id=dev, device_id_type=MESH
        )

    def arrived(dst, ssem, rsem):
        remote(dst, dst, ssem, rsem, xp(1)).wait_recv()

    loads = [pltpu.make_async_copy(lat_hbm.at[0], lat_raw, loc_sem.at[0])]
    for cp in loads:
        cp.start()
    barrier = pltpu.get_barrier_semaphore()
    for d in OFFSETS:
        pl.semaphore_signal(barrier, inc=1, device_id=tm(d), device_id_type=MESH)
    for d in range(1, nc):
        pl.semaphore_signal(barrier, inc=1, device_id=xp(d), device_id_type=MESH)

    wloads = [[], []]
    for s, (src, dst) in enumerate(((w1, wv1), (w2, wv2))):
        for f in range(3):
            for a in range(3):
                wloads[s].append(
                    pltpu.make_async_copy(
                        src.at[f, a], dst.at[:, pl.ds((a * 3 + f) * Q, Q), :], w_sem.at[s * 9 + f * 3 + a]
                    )
                )
    for cp in wloads[0] + wloads[1]:
        cp.start()
    half = c // 2
    w3load = pltpu.make_async_copy(
        w3.at[:, :, :, :, pl.ds(pl.multiple_of(half * 128, 128), 256)], w3v, w_sem.at[18]
    )
    w3load.start()

    prm[...] = jnp.zeros_like(prm)
    for r, ref in enumerate((gamma1, beta1, bias1, gamma2, beta2, bias2, bias3)):
        prm[r : r + 1, 0:Q] = ref[...]

    zero = jnp.zeros((3, C, W), BF)
    x3[:, :, 0:W] = zero
    x3[:, :, W + CELLS : 2 * W + CELLS] = zero
    tmp[...] = jnp.zeros_like(tmp)
    for cp in loads:
        cp.wait()
    lat32[...] = lat_raw[...].astype(F32).reshape(Q * H, W)

    def frame_sums(slot, p1, p2):
        tmp[0:Q, :] = p1
        s1 = jnp.sum(tmp[...].T, axis=0, keepdims=True)
        tmp[0:Q, :] = p2
        s2 = jnp.sum(tmp[...].T, axis=0, keepdims=True)
        st_send[slot] = jnp.concatenate([s1, s2, jnp.zeros((6, 128), F32)], 0)

    p1 = jnp.zeros((Q, W), F32)
    p2 = jnp.zeros((Q, W), F32)
    for i in range(H):
        row = lat32[pl.ds(i, Q, stride=H), :]
        p1 = p1 + row
        p2 = p2 + row * row
        fr[0, 2, :, i * W : (i + 1) * W] = row.astype(BF)
    frame_sums(0, p1, p2)
    colp[...] = prm[...].T

    def prep_conv(src, dst):
        for b in range(3):
            turned = src[b].T
            for q in range(nc):
                place = lax.rem(q - c + 2 + nc, nc) * 3 + b
                dst[pl.ds(pl.multiple_of(place * Q, Q), Q), :] = turned[q * Q : (q + 1) * Q]

    pl.semaphore_wait(barrier, len(OFFSETS) + nc - 1)

    def stats_copies(s):
        return [
            remote(st_send.at[s], st_recv.at[s, k], ss_sem.at[s, k], sr_sem.at[s, k], tm(d))
            for k, d in enumerate(OFFSETS)
        ]

    sibling = (t + 1 - 2 * core, c)

    def lanes(ch):
        return pl.ds(pl.multiple_of(ch * CW, CW), CW)

    def halo_copy(s, ch):
        return remote(
            fr.at[s, 2, :, lanes(ch)], fr.at[s, 0, :, lanes(ch)], hs_sem.at[s, 0, ch], hr_sem.at[s, 0, ch], tm(2)
        )

    def halo_across(s, ch):
        return remote(
            fr.at[s, 2 - 2 * core, :, lanes(ch)],
            fr.at[s, 1, :, lanes(ch)],
            hs_sem.at[s, 1, ch],
            hr_sem.at[s, 1, ch],
            sibling,
        )

    own_clip = clip[t]
    valid = []
    for d in (2, 1):
        src = lax.rem(t - d + nt, nt)
        valid.append(jnp.where((t - d >= 0) & (clip[src] == own_clip), 1.0, 0.0).astype(F32))
    valid.append(jnp.float32(1.0))

    lane = lax.broadcasted_iota(jnp.int32, (128, 128), 1)
    subl = lax.broadcasted_iota(jnp.int32, (128, 128), 0)
    ga = jnp.floor((subl.astype(F32) + 0.5) * (1.0 / PER_GROUP))
    gb = jnp.floor((lane.astype(F32) + 0.5) * (1.0 / PER_GROUP))
    gmat = jnp.where(ga == gb, 1.0, 0.0).astype(F32)

    def norm_params(s):
        total = st_send[s]
        frames = jnp.float32(1.0)
        for k, d in enumerate(OFFSETS):
            arrived(st_recv.at[s, k], ss_sem.at[s, k], sr_sem.at[s, k])
            src = lax.rem(t - d + nt, nt)
            inside = (t - d >= 0) & (t - d < nt)
            m = jnp.where(inside & (clip[src] == own_clip), 1.0, 0.0).astype(F32)
            total = total + m * st_recv[s, k]
            frames = frames + m
        grouped = jnp.dot(total, gmat, precision=lax.Precision.HIGHEST, preferred_element_type=F32)
        tmp[0:8, :] = grouped
        cols = tmp[...].T
        count = frames * float(PER_GROUP * CELLS)
        mean = cols[0:Q, 0:1] / count
        var = cols[0:Q, 1:2] / count - mean * mean
        inv = lax.rsqrt(var + EPSILON)
        return mean, inv * colp[0:Q, 3 * s : 3 * s + 1], colp[0:Q, 3 * s + 1 : 3 * s + 2]

    def fill_rows(s, f, ch, params):
        for r in range(2):
            cells = pl.ds(pl.multiple_of(ch * CW + r * W, W), W)
            v = fr[s, f, :, cells].astype(F32)
            u = (v - params[0]) * params[1] + params[2]
            u = u / (1.0 + jnp.exp(-u))
            if f < 2:
                u = u * valid[f]
            u = u.astype(BF)
            for a in range(3):
                o = r + 1 - a
                k = (a * 3 + f) * Q
                act[ch + 1 + o // 2, k : k + Q, (o % 2) * W : (o % 2 + 1) * W] = u

    first = lax.broadcasted_iota(jnp.int32, (Q, W), 1) == 0
    last = lax.broadcasted_iota(jnp.int32, (Q, W), 1) == W - 1
    low = slice(0, HQ)
    high = slice(HQ, Q)

    def ring_copy(s, kind, way, ch):
        if kind == 0:
            src = sb.at[s, ch, 0, high if way else low]
        elif kind == 1:
            src = sb.at[s, ch, 1, low] if way else sb.at[s, ch, 3, high]
        else:
            src = added.at[s, ch, way]
        return remote(
            src, rb.at[s, ch, kind, way], rs_sem.at[s, kind, way, ch], rr_sem.at[s, kind, way, ch], xp(3 if way else 1)
        )

    def ring_arrived(s, kind, way, ch):
        arrived(rb.at[s, ch, kind, way], rs_sem.at[s, kind, way, ch], rr_sem.at[s, kind, way, ch])

    def ring_add(s, ch):
        for way in range(2):
            ring_arrived(s, 0, way, ch)
            mine = sb[s, ch, 1, high] if way else sb[s, ch, 3, low]
            added[s, ch, way] = (mine.astype(F32) + rb[s, ch, 0, way].astype(F32)).astype(BF)
            ring_copy(s, 2, way, ch).start()

    def conv(s, wt, params):
        params = [jnp.broadcast_to(p, (Q, W)) for p in params]
        for ch in range(NCH):
            fill_rows(s, 2, ch, params)

        def contribute(lo, hi, ch):
            yb[lo * 3 * Q : hi * 3 * Q, :] = jnp.dot(
                wt[lo * 3 * Q : hi * 3 * Q, :], act[ch + 1], preferred_element_type=F32
            )
            for p in range(lo, hi):
                base = p * 3 * Q
                for h in range(2):
                    cells = slice(h * W, (h + 1) * W)
                    left = jnp.where(first, 0.0, pltpu.roll(yb[base : base + Q, cells], 1, 1))
                    right = jnp.where(last, 0.0, pltpu.roll(yb[base + 2 * Q : base + 3 * Q, cells], W - 1, 1))
                    sb[s, ch, p, :, cells] = (yb[base + Q : base + 2 * Q, cells] + left + right).astype(BF)
            for way in range(2):
                ring_copy(s, lo, way, ch).start()

        def chunk(step, carry):
            @pl.when(step < NCH)
            def _():
                arrived(fr.at[s, 0, :, lanes(step)], hs_sem.at[s, 0, step], hr_sem.at[s, 0, step])
                halo_across(s, step).start()
                fill_rows(s, 0, step, params)

            @pl.when((step >= 1) & (step < NCH + 1))
            def _():
                ch = step - 1
                arrived(fr.at[s, 1, :, lanes(ch)], hs_sem.at[s, 1, ch], hr_sem.at[s, 1, ch])
                fill_rows(s, 1, ch, params)

            @pl.when((step >= 2) & (step < NCH + 2))
            def _():
                contribute(0, 1, step - 2)

            @pl.when((step >= LAG_R) & (step < NCH + LAG_R))
            def _():
                contribute(1, 4, step - LAG_R)

            @pl.when(step >= LAG_S)
            def _():
                ring_add(s, step - LAG_S)

            return carry

        lax.fori_loop(0, NCH + LAG_S, chunk, 0)

    def gathered(s, ch):
        for kind in (1, 2):
            for way in range(2):
                ring_arrived(s, kind, way, ch)
        own = sb[s, ch, 2].astype(F32)
        top = own[low] + rb[s, ch, 2, 0].astype(F32) + rb[s, ch, 1, 1].astype(F32)
        bottom = own[high] + rb[s, ch, 1, 0].astype(F32) + rb[s, ch, 2, 1].astype(F32)
        return jnp.concatenate([top, bottom], 0) + colp[0:Q, 3 * s + 2 : 3 * s + 3]

    offset = pl.multiple_of(c * Q - half * 128, 32)

    def prep_three(f):
        taps = {}
        for a in range(3):
            for b in range(3):
                t3[a * 3 + b] = w3v[f, a, b].T
        m = valid[f]

        def tap(a, b):
            return t3[a * 3 + b, pl.ds(offset, Q), :].astype(F32)

        for pi in range(2):
            for block, di in enumerate((0, 1) if pi else (0, -1)):
                rows = ((0, 1), (2,))[block] if pi else ((1, 2), (0,))[block]
                sums = []
                for b in range(3):
                    v = tap(rows[0], b)
                    for a in rows[1:]:
                        v = v + tap(a, b)
                    sums.append(v * m if f < 2 else v)
                parts = (sums[0], sums[1] + sums[2], sums[0] + sums[1], sums[2])
                for k, part in enumerate(parts):
                    base = ((pi * 2 + block) * 4 + k) * Q
                    wf[base : base + Q, f * C : (f + 1) * C] = part.astype(BF)

    for cp in stats_copies(0):
        cp.start()
    for ch in range(NCH):
        halo_copy(0, ch).start()
    act[...] = jnp.zeros_like(act)
    for dst in (wv1, wv2):
        dst[:, 9 * Q : KP, :] = jnp.zeros((3, KP - 9 * Q, C), BF)
    er = lax.broadcasted_iota(jnp.int32, (2 * W, 2 * W), 0)
    ec = lax.broadcasted_iota(jnp.int32, (2 * W, 2 * W), 1)
    perm[...] = jnp.where(jnp.where(er < W, 2 * er, 2 * er - 2 * W + 1) == ec, 1.0, 0.0).astype(BF)
    for cp in wloads[0]:
        cp.wait()
    prep_conv(wv1, wt1)
    for cp in wloads[1]:
        cp.wait()
    prep_conv(wv2, wt2)
    w3load.wait()
    for f in range(3):
        prep_three(f)
    params = norm_params(0)
    conv(0, wt1, params)
    p1 = jnp.zeros((Q, W), F32)
    p2 = jnp.zeros((Q, W), F32)
    for ch in range(NCH):
        hidden = gathered(0, ch).astype(BF)
        fr[1, 2, :, ch * CW : (ch + 1) * CW] = hidden
        if ch < 2:
            halo_copy(1, ch).start()
        hidden = hidden.astype(F32)
        for h in range(2):
            row = hidden[:, h * W : (h + 1) * W]
            p1 = p1 + row
            p2 = p2 + row * row
    frame_sums(1, p1, p2)
    for cp in stats_copies(1):
        cp.start()
    for ch in range(2, NCH):
        halo_copy(1, ch).start()

    def sent(s):
        for cp in stats_copies(s):
            cp.wait_send()
        for ch in range(NCH):
            halo_copy(s, ch).wait_send()
            halo_across(s, ch).wait_send()

    sent(0)
    for ch in range(NCH):
        for kind in range(3):
            for way in range(2):
                ring_copy(0, kind, way, ch).wait_send()

    params = norm_params(1)
    conv(1, wt2, params)
    sent(1)

    def lanes_of(ch):
        return pl.ds(pl.multiple_of(W + ch * CW, W), CW)

    def own_x(d, ch):
        spot = x3.at[2, quarter(0), lanes_of(ch)]
        return remote(spot, spot, as_sem.at[d - 1, ch], ar_sem.at[d - 1, ch], xp(d))

    def half_quarter(d, part):
        return pl.ds(pl.multiple_of(lax.rem(c + d, nc) * Q + part * HQ, HQ), HQ)

    def own_z(k, ch):
        return remote(
            x3.at[2, quarter(2 * k), lanes_of(ch)],
            x3.at[0, quarter(2 * k), lanes_of(ch)],
            zs_sem.at[k, ch],
            zr_sem.at[k, ch],
            tm(2),
        )

    def back_x(d, ch):
        spot = x3.at[0, quarter(0), lanes_of(ch)]
        return remote(spot, spot, xs_sem.at[d // 2, ch], xr_sem.at[d // 2, ch], xp(d))

    def across(ch):
        return remote(
            x3.at[2 - 2 * core, :, lanes_of(ch)],
            x3.at[1, :, lanes_of(ch)],
            bs_sem.at[ch],
            br_sem.at[ch],
            sibling,
        )

    bias = colp[0:Q, 6:7]

    def rows_of(f0, f1, ch, di):
        lanes = pl.ds(pl.multiple_of((1 + di) * W + ch * CW, W), CW)
        return x3[f0:f1, :, lanes].reshape((f1 - f0) * C, CW)

    def partial(pi, f0, f1, ch):
        base = pi * 8 * Q
        k = slice(f0 * C, f1 * C)
        mid = jnp.dot(wf[base : base + C, k], rows_of(f0, f1, ch, 0), preferred_element_type=F32)
        edge = rows_of(f0, f1, ch, 1 if pi else -1)
        return mid + jnp.dot(wf[base + C : base + 2 * C, k], edge, preferred_element_type=F32)

    def result_copy(block):
        lines = pl.ds(pl.multiple_of(block * H, H), H)
        return pltpu.make_async_copy(done.at[block], out.at[0, :, lines, :], loc_sem.at[1 + block])

    def pipeline(step, carry):
        @pl.when(step < NCH)
        def _():
            ch = step
            cells = pl.ds(pl.multiple_of(ch * CW, CW), CW)
            residual = fr[0, 2, :, cells].astype(F32) + gathered(1, ch)
            x3[2, quarter(0), lanes_of(ch)] = residual.astype(BF)
            own_z(0, ch).start()
            for d in (2, 1, 3):
                own_x(d, ch).start()

        @pl.when((step >= LAG_P) & (step < NCH + LAG_P))
        def _():
            ch = step - LAG_P
            arrived(x3.at[2, quarter(2), lanes_of(ch)], as_sem.at[1, ch], ar_sem.at[1, ch])
            own_z(1, ch).start()
            for d in (1, 3):
                arrived(x3.at[2, quarter(4 - d), lanes_of(ch)], as_sem.at[d - 1, ch], ar_sem.at[d - 1, ch])
            for kind in range(3):
                for way in range(2):
                    ring_copy(1, kind, way, ch).wait_send()
            for d in (1, 2, 3):
                own_x(d, ch).wait_send()
            own_z(0, ch).wait_send()

        @pl.when((step >= LAG_K) & (step < NCH + LAG_K))
        def _():
            ch = step - LAG_K
            arrived(x3.at[0, quarter(0), lanes_of(ch)], zs_sem.at[0, ch], zr_sem.at[0, ch])
            for d in (1, 3):
                back_x(d, ch).start()

        @pl.when((step >= LAG_C) & (step < NCH + LAG_C))
        def _():
            ch = step - LAG_C
            for d in (1, 3):
                arrived(x3.at[0, quarter(4 - d), lanes_of(ch)], xs_sem.at[d // 2, ch], xr_sem.at[d // 2, ch])
            arrived(x3.at[0, quarter(2), lanes_of(ch)], zs_sem.at[1, ch], zr_sem.at[1, ch])
            across(ch).start()

        @pl.when((step >= LAG_O) & (step < NCH + LAG_O))
        def _():
            ch = step - LAG_O
            for pi in range(2):
                y3[ch, pi] = partial(pi, 2, 3, ch)

        @pl.when((step >= LAG_D) & (step < NCH + LAG_D))
        def _():
            ch = step - LAG_D
            for d in (1, 3):
                back_x(d, ch).wait_send()
            own_z(1, ch).wait_send()
            arrived(x3.at[1, :, lanes_of(ch)], bs_sem.at[ch], br_sem.at[ch])

        @pl.when((step >= LAG_E) & (step < NCH + LAG_E))
        def _():
            ch = step - LAG_E
            for pi in range(2):
                y3[ch, pi] += partial(pi, 0, 2, ch)
                for h in range(2):
                    cells = slice(h * W, (h + 1) * W)
                    left = jnp.where(first, 0.0, pltpu.roll(y3[ch, pi, 0:Q, cells], 1, 1))
                    right = jnp.where(last, 0.0, pltpu.roll(y3[ch, pi, 3 * Q : 4 * Q, cells], W - 1, 1))
                    rows = slice((2 * h + pi) * Q, (2 * h + pi + 1) * Q)
                    both[rows, 0:W] = (y3[ch, pi, Q : 2 * Q, cells] + left + bias).astype(BF)
                    both[rows, W : 2 * W] = (y3[ch, pi, 2 * Q : 3 * Q, cells] + right + bias).astype(BF)
            spread = jnp.dot(both[...], perm[...], preferred_element_type=F32)
            for k in range(4):
                for g in range(2):
                    oscr[ch // 2, g, pl.ds(lax.rem(ch, 2) * 4 + k, Q, stride=H), :] = spread[k * Q : (k + 1) * Q, g * 128 : (g + 1) * 128]

            @pl.when(ch % 2 == 1)
            def _():
                block = ch // 2
                for g in range(2):
                    lines = oscr[block, g].reshape(Q, H, 128)
                    done[block, :, :, g * 128 : (g + 1) * 128] = lines.astype(BF)
                result_copy(block).start()

        return carry

    lax.fori_loop(0, NCH + LAG_E, pipeline, 0)
    for ch in range(NCH):
        across(ch).wait_send()
    for block in range(2):
        result_copy(block).wait()


def on_device(nt, nc, *args):
    args = [a.reshape(1, Q) if a.ndim == 1 and a.dtype == F32 else a for a in args]
    anywhere = pl.BlockSpec(memory_space=pl.ANY)
    specs = [pl.BlockSpec(memory_space=pltpu.VMEM) if a.ndim == 2 else anywhere for a in args]
    specs[1] = pl.BlockSpec(memory_space=pltpu.SMEM)
    dma = pltpu.SemaphoreType.DMA
    scratch = [
        pltpu.VMEM((Q, H, W), BF),
        pltpu.VMEM((Q * H, W), F32),
        pltpu.VMEM((2, 3, Q, CELLS), BF),
        pltpu.VMEM((128, 128), F32),
        pltpu.VMEM((128, 128), F32),
        pltpu.VMEM((128, 128), F32),
        pltpu.VMEM((2, 8, 128), F32),
        pltpu.VMEM((2, len(OFFSETS), 8, 128), F32),
        pltpu.VMEM((3, KP, C), BF),
        pltpu.VMEM((3, KP, C), BF),
        pltpu.VMEM((3 * C, KP), BF),
        pltpu.VMEM((3 * C, KP), BF),
        pltpu.VMEM((3, 3, 3, C, 256), BF),
        pltpu.VMEM((9, 256, C), BF),
        pltpu.VMEM((16 * Q, 3 * C), BF),
        pltpu.VMEM((NCH + 2, KP, CW), BF),
        pltpu.VMEM((3 * C, CW), F32),
        pltpu.VMEM((2, NCH, 4, Q, CW), BF),
        pltpu.VMEM((2, NCH, 2, HQ, CW), BF),
        pltpu.VMEM((2, NCH, 3, 2, HQ, CW), BF),
        pltpu.VMEM((3, C, CELLS + 2 * W), BF),
        pltpu.VMEM((NCH, 2, C, CW), F32),
        pltpu.VMEM((C, 2 * W), BF),
        pltpu.VMEM((2 * W, 2 * W), BF),
        pltpu.VMEM((2, 2, Q * H, 128), F32),
        pltpu.VMEM((2, Q, H, 2 * W), BF),
        dma((3,)),
        dma((19,)),
        dma((2, 2, NCH)),
        dma((2, 2, NCH)),
        dma((2, len(OFFSETS))),
        dma((2, len(OFFSETS))),
        dma((2, 3, 2, NCH)),
        dma((2, 3, 2, NCH)),
        dma((3, NCH)),
        dma((3, NCH)),
        dma((2, NCH)),
        dma((2, NCH)),
        dma((2, NCH)),
        dma((2, NCH)),
        dma((NCH,)),
        dma((NCH,)),
    ]
    return pl.pallas_call(
        functools.partial(kernel, nt, nc),
        out_shape=jax.ShapeDtypeStruct((1, Q, 2 * H, 2 * W), BF),
        in_specs=specs,
        out_specs=pl.BlockSpec(memory_space=pl.ANY),
        scratch_shapes=scratch,
        compiler_params=pltpu.CompilerParams(
            collective_id=0, has_side_effects=True, vmem_limit_bytes=60 * 1024 * 1024
        ),
    )(*args)


def solution(mesh):
    in_specs = (
        P("tm", "chan", None, None),
        P(),
        P("chan"),
        P("chan"),
        P(None, None, None, "chan", None),
        P("chan"),
        P("chan"),
        P("chan"),
        P(None, None, None, "chan", None),
        P("chan"),
        P(),
        P("chan"),
    )
    return jax.shard_map(
        functools.partial(on_device, mesh.shape["tm"], mesh.shape["chan"]),
        mesh=mesh,
        in_specs=in_specs,
        out_specs=P("tm", "chan", None, None),
        check_vma=False,
    )
```

```python
import functools

import jax
import jax.numpy as jnp
from jax import lax
from jax.experimental import pallas as pl
from jax.experimental.pallas import tpu as pltpu
from jax.sharding import PartitionSpec as P

C = 384
GROUPS = 32
PER_GROUP = C // GROUPS
Q = 96
H = 8
W = 128
CELLS = H * W
NCH = 4
CW = CELLS // NCH
REACH = 7
HQ = Q // 2
LAG_R = 4
LAG_S = 5
LAG_P = 3
LAG_K = 3
LAG_O = 5
LAG_C = 6
LAG_D = 7
LAG_E = 8
KP = 896
EPSILON = 1e-06
MESH = pl.DeviceIdType.MESH
BF = jnp.bfloat16
F32 = jnp.float32
OFFSETS = [d for d in range(-REACH, REACH + 1) if d != 0]


def kernel(
    nt,
    nc,
    lat_hbm,
    clip,
    gamma1,
    beta1,
    w1,
    bias1,
    gamma2,
    beta2,
    w2,
    bias2,
    w3,
    bias3,
    out,
    lat_raw,
    lat32,
    fr,
    prm,
    tmp,
    colp,
    st_send,
    st_recv,
    wv1,
    wv2,
    wt1,
    wt2,
    w3v,
    t3,
    wf,
    act,
    yb,
    sb,
    added,
    rb,
    x3,
    y3,
    both,
    perm,
    oscr,
    done,
    loc_sem,
    w_sem,
    hs_sem,
    hr_sem,
    ss_sem,
    sr_sem,
    rs_sem,
    rr_sem,
    as_sem,
    ar_sem,
    zs_sem,
    zr_sem,
    xs_sem,
    xr_sem,
    bs_sem,
    br_sem,
):
    t = lax.axis_index("tm")
    c = lax.axis_index("chan")
    core = lax.rem(t, 2)

    def tm(d):
        return (lax.rem(t + d + nt, nt), c)

    def xp(d):
        return (t, lax.rem(c + d, nc))

    def quarter(d):
        return pl.ds(pl.multiple_of(lax.rem(c + d, nc) * Q, Q), Q)

    def remote(src, dst, ssem, rsem, dev):
        return pltpu.make_async_remote_copy(
            src_ref=src, dst_ref=dst, send_sem=ssem, recv_sem=rsem, device_id=dev, device_id_type=MESH
        )

    def arrived(dst, ssem, rsem):
        remote(dst, dst, ssem, rsem, xp(1)).wait_recv()

    loads = [pltpu.make_async_copy(lat_hbm.at[0], lat_raw, loc_sem.at[0])]
    for cp in loads:
        cp.start()
    barrier = pltpu.get_barrier_semaphore()
    for d in OFFSETS:
        pl.semaphore_signal(barrier, inc=1, device_id=tm(d), device_id_type=MESH)
    for d in range(1, nc):
        pl.semaphore_signal(barrier, inc=1, device_id=xp(d), device_id_type=MESH)

    wloads = [[], []]
    for s, (src, dst) in enumerate(((w1, wv1), (w2, wv2))):
        for f in range(3):
            for a in range(3):
                wloads[s].append(
                    pltpu.make_async_copy(
                        src.at[f, a], dst.at[:, pl.ds((a * 3 + f) * Q, Q), :], w_sem.at[s * 9 + f * 3 + a]
                    )
                )
    for cp in wloads[0] + wloads[1]:
        cp.start()
    half = c // 2
    w3load = pltpu.make_async_copy(
        w3.at[:, :, :, :, pl.ds(pl.multiple_of(half * 128, 128), 256)], w3v, w_sem.at[18]
    )
    w3load.start()

    prm[...] = jnp.zeros_like(prm)
    for r, ref in enumerate((gamma1, beta1, bias1, gamma2, beta2, bias2, bias3)):
        prm[r : r + 1, 0:Q] = ref[...]

    zero = jnp.zeros((3, C, W), BF)
    x3[:, :, 0:W] = zero
    x3[:, :, W + CELLS : 2 * W + CELLS] = zero
    tmp[...] = jnp.zeros_like(tmp)
    for cp in loads:
        cp.wait()
    lat32[...] = lat_raw[...].astype(F32).reshape(Q * H, W)

    def frame_sums(slot, p1, p2):
        tmp[0:Q, :] = p1
        s1 = jnp.sum(tmp[...].T, axis=0, keepdims=True)
        tmp[0:Q, :] = p2
        s2 = jnp.sum(tmp[...].T, axis=0, keepdims=True)
        st_send[slot] = jnp.concatenate([s1, s2, jnp.zeros((6, 128), F32)], 0)

    p1 = jnp.zeros((Q, W), F32)
    p2 = jnp.zeros((Q, W), F32)
    for i in range(H):
        row = lat32[pl.ds(i, Q, stride=H), :]
        p1 = p1 + row
        p2 = p2 + row * row
        fr[0, 2, :, i * W : (i + 1) * W] = row.astype(BF)
    frame_sums(0, p1, p2)
    colp[...] = prm[...].T

    def prep_conv(src, dst):
        for b in range(3):
            turned = src[b].T
            for q in range(nc):
                place = lax.rem(q - c + 2 + nc, nc) * 3 + b
                dst[pl.ds(pl.multiple_of(place * Q, Q), Q), :] = turned[q * Q : (q + 1) * Q]

    pl.semaphore_wait(barrier, len(OFFSETS) + nc - 1)

    def stats_copies(s):
        return [
            remote(st_send.at[s], st_recv.at[s, k], ss_sem.at[s, k], sr_sem.at[s, k], tm(d))
            for k, d in enumerate(OFFSETS)
        ]

    sibling = (t + 1 - 2 * core, c)

    def lanes(ch):
        return pl.ds(pl.multiple_of(ch * CW, CW), CW)

    def halo_copy(s, ch):
        return remote(
            fr.at[s, 2, :, lanes(ch)], fr.at[s, 0, :, lanes(ch)], hs_sem.at[s, 0, ch], hr_sem.at[s, 0, ch], tm(2)
        )

    def halo_across(s, ch):
        return remote(
            fr.at[s, 2 - 2 * core, :, lanes(ch)],
            fr.at[s, 1, :, lanes(ch)],
            hs_sem.at[s, 1, ch],
            hr_sem.at[s, 1, ch],
            sibling,
        )

    own_clip = clip[t]
    valid = []
    for d in (2, 1):
        src = lax.rem(t - d + nt, nt)
        valid.append(jnp.where((t - d >= 0) & (clip[src] == own_clip), 1.0, 0.0).astype(F32))
    valid.append(jnp.float32(1.0))

    lane = lax.broadcasted_iota(jnp.int32, (128, 128), 1)
    subl = lax.broadcasted_iota(jnp.int32, (128, 128), 0)
    ga = jnp.floor((subl.astype(F32) + 0.5) * (1.0 / PER_GROUP))
    gb = jnp.floor((lane.astype(F32) + 0.5) * (1.0 / PER_GROUP))
    gmat = jnp.where(ga == gb, 1.0, 0.0).astype(F32)

    def norm_params(s):
        total = st_send[s]
        frames = jnp.float32(1.0)
        for k, d in enumerate(OFFSETS):
            arrived(st_recv.at[s, k], ss_sem.at[s, k], sr_sem.at[s, k])
            src = lax.rem(t - d + nt, nt)
            inside = (t - d >= 0) & (t - d < nt)
            m = jnp.where(inside & (clip[src] == own_clip), 1.0, 0.0).astype(F32)
            total = total + m * st_recv[s, k]
            frames = frames + m
        grouped = jnp.dot(total, gmat, precision=lax.Precision.HIGHEST, preferred_element_type=F32)
        tmp[0:8, :] = grouped
        cols = tmp[...].T
        count = frames * float(PER_GROUP * CELLS)
        mean = cols[0:Q, 0:1] / count
        var = cols[0:Q, 1:2] / count - mean * mean
        inv = lax.rsqrt(var + EPSILON)
        return mean, inv * colp[0:Q, 3 * s : 3 * s + 1], colp[0:Q, 3 * s + 1 : 3 * s + 2]

    def fill_rows(s, f, ch, params):
        for r in range(2):
            cells = pl.ds(pl.multiple_of(ch * CW + r * W, W), W)
            v = fr[s, f, :, cells].astype(F32)
            u = (v - params[0]) * params[1] + params[2]
            u = u / (1.0 + jnp.exp(-u))
            if f < 2:
                u = u * valid[f]
            u = u.astype(BF)
            for a in range(3):
                o = r + 1 - a
                k = (a * 3 + f) * Q
                act[ch + 1 + o // 2, k : k + Q, (o % 2) * W : (o % 2 + 1) * W] = u

    first = lax.broadcasted_iota(jnp.int32, (Q, W), 1) == 0
    last = lax.broadcasted_iota(jnp.int32, (Q, W), 1) == W - 1
    low = slice(0, HQ)
    high = slice(HQ, Q)

    def ring_copy(s, kind, way, ch):
        if kind == 0:
            src = sb.at[s, ch, 0, high if way else low]
        elif kind == 1:
            src = sb.at[s, ch, 1, low] if way else sb.at[s, ch, 3, high]
        else:
            src = added.at[s, ch, way]
        return remote(
            src, rb.at[s, ch, kind, way], rs_sem.at[s, kind, way, ch], rr_sem.at[s, kind, way, ch], xp(3 if way else 1)
        )

    def ring_arrived(s, kind, way, ch):
        arrived(rb.at[s, ch, kind, way], rs_sem.at[s, kind, way, ch], rr_sem.at[s, kind, way, ch])

    def ring_add(s, ch):
        for way in range(2):
            ring_arrived(s, 0, way, ch)
            mine = sb[s, ch, 1, high] if way else sb[s, ch, 3, low]
            added[s, ch, way] = (mine.astype(F32) + rb[s, ch, 0, way].astype(F32)).astype(BF)
            ring_copy(s, 2, way, ch).start()

    def conv(s, wt, params):
        params = [jnp.broadcast_to(p, (Q, W)) for p in params]
        for ch in range(NCH):
            fill_rows(s, 2, ch, params)

        def contribute(lo, hi, ch):
            yb[lo * 3 * Q : hi * 3 * Q, :] = jnp.dot(
                wt[lo * 3 * Q : hi * 3 * Q, :], act[ch + 1], preferred_element_type=F32
            )
            for p in range(lo, hi):
                base = p * 3 * Q
                for h in range(2):
                    cells = slice(h * W, (h + 1) * W)
                    left = jnp.where(first, 0.0, pltpu.roll(yb[base : base + Q, cells], 1, 1))
                    right = jnp.where(last, 0.0, pltpu.roll(yb[base + 2 * Q : base + 3 * Q, cells], W - 1, 1))
                    sb[s, ch, p, :, cells] = (yb[base + Q : base + 2 * Q, cells] + left + right).astype(BF)
            for way in range(2):
                ring_copy(s, lo, way, ch).start()

        def chunk(step, carry):
            @pl.when(step < NCH)
            def _():
                arrived(fr.at[s, 0, :, lanes(step)], hs_sem.at[s, 0, step], hr_sem.at[s, 0, step])
                halo_across(s, step).start()
                fill_rows(s, 0, step, params)

            @pl.when((step >= 1) & (step < NCH + 1))
            def _():
                ch = step - 1
                arrived(fr.at[s, 1, :, lanes(ch)], hs_sem.at[s, 1, ch], hr_sem.at[s, 1, ch])
                fill_rows(s, 1, ch, params)

            @pl.when((step >= 2) & (step < NCH + 2))
            def _():
                contribute(0, 1, step - 2)

            @pl.when((step >= LAG_R) & (step < NCH + LAG_R))
            def _():
                contribute(1, 4, step - LAG_R)

            @pl.when(step >= LAG_S)
            def _():
                ring_add(s, step - LAG_S)

            return carry

        lax.fori_loop(0, NCH + LAG_S, chunk, 0)

    def gathered(s, ch):
        for kind in (1, 2):
            for way in range(2):
                ring_arrived(s, kind, way, ch)
        own = sb[s, ch, 2].astype(F32)
        top = own[low] + rb[s, ch, 2, 0].astype(F32) + rb[s, ch, 1, 1].astype(F32)
        bottom = own[high] + rb[s, ch, 1, 0].astype(F32) + rb[s, ch, 2, 1].astype(F32)
        return jnp.concatenate([top, bottom], 0) + colp[0:Q, 3 * s + 2 : 3 * s + 3]

    offset = pl.multiple_of(c * Q - half * 128, 32)

    def prep_three(f):
        taps = {}
        for a in range(3):
            for b in range(3):
                t3[a * 3 + b] = w3v[f, a, b].T
        m = valid[f]

        def tap(a, b):
            return t3[a * 3 + b, pl.ds(offset, Q), :].astype(F32)

        for pi in range(2):
            for block, di in enumerate((0, 1) if pi else (0, -1)):
                rows = ((0, 1), (2,))[block] if pi else ((1, 2), (0,))[block]
                sums = []
                for b in range(3):
                    v = tap(rows[0], b)
                    for a in rows[1:]:
                        v = v + tap(a, b)
                    sums.append(v * m if f < 2 else v)
                parts = (sums[0], sums[1] + sums[2], sums[0] + sums[1], sums[2])
                for k, part in enumerate(parts):
                    base = ((pi * 2 + block) * 4 + k) * Q
                    wf[base : base + Q, f * C : (f + 1) * C] = part.astype(BF)

    for cp in stats_copies(0):
        cp.start()
    for ch in range(NCH):
        halo_copy(0, ch).start()
    act[...] = jnp.zeros_like(act)
    for dst in (wv1, wv2):
        dst[:, 9 * Q : KP, :] = jnp.zeros((3, KP - 9 * Q, C), BF)
    er = lax.broadcasted_iota(jnp.int32, (2 * W, 2 * W), 0)
    ec = lax.broadcasted_iota(jnp.int32, (2 * W, 2 * W), 1)
    perm[...] = jnp.where(jnp.where(er < W, 2 * er, 2 * er - 2 * W + 1) == ec, 1.0, 0.0).astype(BF)
    for cp in wloads[0]:
        cp.wait()
    prep_conv(wv1, wt1)
    for cp in wloads[1]:
        cp.wait()
    prep_conv(wv2, wt2)
    w3load.wait()
    for f in range(3):
        prep_three(f)
    params = norm_params(0)
    conv(0, wt1, params)
    p1 = jnp.zeros((Q, W), F32)
    p2 = jnp.zeros((Q, W), F32)
    for ch in range(NCH):
        hidden = gathered(0, ch).astype(BF)
        fr[1, 2, :, ch * CW : (ch + 1) * CW] = hidden
        if ch < 2:
            halo_copy(1, ch).start()
        hidden = hidden.astype(F32)
        for h in range(2):
            row = hidden[:, h * W : (h + 1) * W]
            p1 = p1 + row
            p2 = p2 + row * row
    frame_sums(1, p1, p2)
    for cp in stats_copies(1):
        cp.start()
    for ch in range(2, NCH):
        halo_copy(1, ch).start()

    def sent(s):
        for cp in stats_copies(s):
            cp.wait_send()
        for ch in range(NCH):
            halo_copy(s, ch).wait_send()
            halo_across(s, ch).wait_send()

    sent(0)
    for ch in range(NCH):
        for kind in range(3):
            for way in range(2):
                ring_copy(0, kind, way, ch).wait_send()

    params = norm_params(1)
    conv(1, wt2, params)
    sent(1)

    def lanes_of(ch):
        return pl.ds(W + ch * CW, CW)

    def own_x(d, ch):
        spot = x3.at[2, quarter(0), lanes_of(ch)]
        return remote(spot, spot, as_sem.at[d - 1, ch], ar_sem.at[d - 1, ch], xp(d))

    def half_quarter(d, part):
        return pl.ds(pl.multiple_of(lax.rem(c + d, nc) * Q + part * HQ, HQ), HQ)

    def own_z(k, ch):
        return remote(
            x3.at[2, quarter(2 * k), lanes_of(ch)],
            x3.at[0, quarter(2 * k), lanes_of(ch)],
            zs_sem.at[k, ch],
            zr_sem.at[k, ch],
            tm(2),
        )

    def back_x(d, ch):
        spot = x3.at[0, quarter(0), lanes_of(ch)]
        return remote(spot, spot, xs_sem.at[d // 2, ch], xr_sem.at[d // 2, ch], xp(d))

    def across(ch):
        return remote(
            x3.at[2 - 2 * core, :, lanes_of(ch)],
            x3.at[1, :, lanes_of(ch)],
            bs_sem.at[ch],
            br_sem.at[ch],
            sibling,
        )

    bias = colp[0:Q, 6:7]

    def rows_of(f0, f1, ch, di):
        lanes = pl.ds((1 + di) * W + ch * CW, CW)
        return x3[f0:f1, :, lanes].reshape((f1 - f0) * C, CW)

    def partial(pi, f0, f1, ch):
        base = pi * 8 * Q
        k = slice(f0 * C, f1 * C)
        mid = jnp.dot(wf[base : base + C, k], rows_of(f0, f1, ch, 0), preferred_element_type=F32)
        edge = rows_of(f0, f1, ch, 1 if pi else -1)
        return mid + jnp.dot(wf[base + C : base + 2 * C, k], edge, preferred_element_type=F32)

    def result_copy(block):
        lines = pl.ds(block * H, H)
        return pltpu.make_async_copy(done.at[block], out.at[0, :, lines, :], loc_sem.at[1 + block])

    def static_when(condition):
        return lambda block: block() if condition else None

    def pipeline(step, carry):
        @static_when(step < NCH)
        def _():
            ch = step
            cells = pl.ds(ch * CW, CW)
            residual = fr[0, 2, :, cells].astype(F32) + gathered(1, ch)
            x3[2, quarter(0), lanes_of(ch)] = residual.astype(BF)
            own_z(0, ch).start()
            for d in (2, 1, 3):
                own_x(d, ch).start()

        @static_when((step >= LAG_P) and (step < NCH + LAG_P))
        def _():
            ch = step - LAG_P
            arrived(x3.at[2, quarter(2), lanes_of(ch)], as_sem.at[1, ch], ar_sem.at[1, ch])
            own_z(1, ch).start()
            for d in (1, 3):
                arrived(x3.at[2, quarter(4 - d), lanes_of(ch)], as_sem.at[d - 1, ch], ar_sem.at[d - 1, ch])
            for kind in range(3):
                for way in range(2):
                    ring_copy(1, kind, way, ch).wait_send()
            for d in (1, 2, 3):
                own_x(d, ch).wait_send()
            own_z(0, ch).wait_send()

        @static_when((step >= LAG_K) and (step < NCH + LAG_K))
        def _():
            ch = step - LAG_K
            arrived(x3.at[0, quarter(0), lanes_of(ch)], zs_sem.at[0, ch], zr_sem.at[0, ch])
            for d in (1, 3):
                back_x(d, ch).start()

        @static_when((step >= LAG_C) and (step < NCH + LAG_C))
        def _():
            ch = step - LAG_C
            for d in (1, 3):
                arrived(x3.at[0, quarter(4 - d), lanes_of(ch)], xs_sem.at[d // 2, ch], xr_sem.at[d // 2, ch])
            arrived(x3.at[0, quarter(2), lanes_of(ch)], zs_sem.at[1, ch], zr_sem.at[1, ch])
            across(ch).start()

        @static_when((step >= LAG_O) and (step < NCH + LAG_O))
        def _():
            ch = step - LAG_O
            for pi in range(2):
                y3[ch, pi] = partial(pi, 2, 3, ch)

        @static_when((step >= LAG_D) and (step < NCH + LAG_D))
        def _():
            ch = step - LAG_D
            for d in (1, 3):
                back_x(d, ch).wait_send()
            own_z(1, ch).wait_send()
            arrived(x3.at[1, :, lanes_of(ch)], bs_sem.at[ch], br_sem.at[ch])

        @static_when((step >= LAG_E) and (step < NCH + LAG_E))
        def _():
            ch = step - LAG_E
            for pi in range(2):
                y3[ch, pi] += partial(pi, 0, 2, ch)
                for h in range(2):
                    cells = slice(h * W, (h + 1) * W)
                    left = jnp.where(first, 0.0, pltpu.roll(y3[ch, pi, 0:Q, cells], 1, 1))
                    right = jnp.where(last, 0.0, pltpu.roll(y3[ch, pi, 3 * Q : 4 * Q, cells], W - 1, 1))
                    rows = slice((2 * h + pi) * Q, (2 * h + pi + 1) * Q)
                    both[rows, 0:W] = (y3[ch, pi, Q : 2 * Q, cells] + left + bias).astype(BF)
                    both[rows, W : 2 * W] = (y3[ch, pi, 2 * Q : 3 * Q, cells] + right + bias).astype(BF)
            spread = jnp.dot(both[...], perm[...], preferred_element_type=F32)
            for k in range(4):
                for g in range(2):
                    oscr[ch // 2, g, pl.ds((ch % 2) * 4 + k, Q, stride=H), :] = spread[k * Q : (k + 1) * Q, g * 128 : (g + 1) * 128]

            @static_when(ch % 2 == 1)
            def _():
                block = ch // 2
                for g in range(2):
                    lines = oscr[block, g].reshape(Q, H, 128)
                    done[block, :, :, g * 128 : (g + 1) * 128] = lines.astype(BF)
                result_copy(block).start()

        return carry

    for step in range(NCH + LAG_E):
        pipeline(step, 0)
    for ch in range(NCH):
        across(ch).wait_send()
    for block in range(2):
        result_copy(block).wait()


def on_device(nt, nc, *args):
    args = [a.reshape(1, Q) if a.ndim == 1 and a.dtype == F32 else a for a in args]
    anywhere = pl.BlockSpec(memory_space=pl.ANY)
    specs = [pl.BlockSpec(memory_space=pltpu.VMEM) if a.ndim == 2 else anywhere for a in args]
    specs[1] = pl.BlockSpec(memory_space=pltpu.SMEM)
    dma = pltpu.SemaphoreType.DMA
    scratch = [
        pltpu.VMEM((Q, H, W), BF),
        pltpu.VMEM((Q * H, W), F32),
        pltpu.VMEM((2, 3, Q, CELLS), BF),
        pltpu.VMEM((128, 128), F32),
        pltpu.VMEM((128, 128), F32),
        pltpu.VMEM((128, 128), F32),
        pltpu.VMEM((2, 8, 128), F32),
        pltpu.VMEM((2, len(OFFSETS), 8, 128), F32),
        pltpu.VMEM((3, KP, C), BF),
        pltpu.VMEM((3, KP, C), BF),
        pltpu.VMEM((3 * C, KP), BF),
        pltpu.VMEM((3 * C, KP), BF),
        pltpu.VMEM((3, 3, 3, C, 256), BF),
        pltpu.VMEM((9, 256, C), BF),
        pltpu.VMEM((16 * Q, 3 * C), BF),
        pltpu.VMEM((NCH + 2, KP, CW), BF),
        pltpu.VMEM((3 * C, CW), F32),
        pltpu.VMEM((2, NCH, 4, Q, CW), BF),
        pltpu.VMEM((2, NCH, 2, HQ, CW), BF),
        pltpu.VMEM((2, NCH, 3, 2, HQ, CW), BF),
        pltpu.VMEM((3, C, CELLS + 2 * W), BF),
        pltpu.VMEM((NCH, 2, C, CW), F32),
        pltpu.VMEM((C, 2 * W), BF),
        pltpu.VMEM((2 * W, 2 * W), BF),
        pltpu.VMEM((2, 2, Q * H, 128), F32),
        pltpu.VMEM((2, Q, H, 2 * W), BF),
        dma((3,)),
        dma((19,)),
        dma((2, 2, NCH)),
        dma((2, 2, NCH)),
        dma((2, len(OFFSETS))),
        dma((2, len(OFFSETS))),
        dma((2, 3, 2, NCH)),
        dma((2, 3, 2, NCH)),
        dma((3, NCH)),
        dma((3, NCH)),
        dma((2, NCH)),
        dma((2, NCH)),
        dma((2, NCH)),
        dma((2, NCH)),
        dma((NCH,)),
        dma((NCH,)),
    ]
    return pl.pallas_call(
        functools.partial(kernel, nt, nc),
        out_shape=jax.ShapeDtypeStruct((1, Q, 2 * H, 2 * W), BF),
        in_specs=specs,
        out_specs=pl.BlockSpec(memory_space=pl.ANY),
        scratch_shapes=scratch,
        compiler_params=pltpu.CompilerParams(
            collective_id=0, has_side_effects=True, vmem_limit_bytes=60 * 1024 * 1024
        ),
    )(*args)


def solution(mesh):
    in_specs = (
        P("tm", "chan", None, None),
        P(),
        P("chan"),
        P("chan"),
        P(None, None, None, "chan", None),
        P("chan"),
        P("chan"),
        P("chan"),
        P(None, None, None, "chan", None),
        P("chan"),
        P(),
        P("chan"),
    )
    return jax.shard_map(
        functools.partial(on_device, mesh.shape["tm"], mesh.shape["chan"]),
        mesh=mesh,
        in_specs=in_specs,
        out_specs=P("tm", "chan", None, None),
        check_vma=False,
    )
```

```python
import functools

import jax
import jax.numpy as jnp
from jax import lax
from jax.experimental import pallas as pl
from jax.experimental.pallas import tpu as pltpu
from jax.sharding import PartitionSpec as P

C = 384
GROUPS = 32
PER_GROUP = C // GROUPS
Q = 96
H = 8
W = 128
CELLS = H * W
NCH = 4
CW = CELLS // NCH
REACH = 7
HQ = Q // 2
LAG_R = 4
LAG_S = 5
LAG_P = 3
LAG_K = 3
LAG_O = 5
LAG_C = 6
LAG_D = 7
LAG_E = 8
KP = 896
EPSILON = 1e-06
MESH = pl.DeviceIdType.MESH
BF = jnp.bfloat16
F32 = jnp.float32
OFFSETS = [d for d in range(-REACH, REACH + 1) if d != 0]


def kernel(
    nt,
    nc,
    lat_hbm,
    clip,
    gamma1,
    beta1,
    w1,
    bias1,
    gamma2,
    beta2,
    w2,
    bias2,
    w3,
    bias3,
    out,
    lat_raw,
    lat32,
    fr,
    prm,
    tmp,
    colp,
    st_send,
    st_recv,
    wv1,
    wv2,
    wt1,
    wt2,
    w3v,
    t3,
    wf,
    act,
    yb,
    sb,
    added,
    rb,
    x3,
    y3,
    both,
    perm,
    oscr,
    done,
    loc_sem,
    w_sem,
    hs_sem,
    hr_sem,
    ss_sem,
    sr_sem,
    rs_sem,
    rr_sem,
    as_sem,
    ar_sem,
    zs_sem,
    zr_sem,
    xs_sem,
    xr_sem,
    bs_sem,
    br_sem,
):
    t = lax.axis_index("tm")
    c = lax.axis_index("chan")
    core = lax.rem(t, 2)

    def tm(d):
        return (lax.rem(t + d + nt, nt), c)

    def xp(d):
        return (t, lax.rem(c + d, nc))

    def quarter(d):
        return pl.ds(pl.multiple_of(lax.rem(c + d, nc) * Q, Q), Q)

    def remote(src, dst, ssem, rsem, dev):
        return pltpu.make_async_remote_copy(
            src_ref=src, dst_ref=dst, send_sem=ssem, recv_sem=rsem, device_id=dev, device_id_type=MESH
        )

    def arrived(dst, ssem, rsem):
        remote(dst, dst, ssem, rsem, xp(1)).wait_recv()

    loads = [pltpu.make_async_copy(lat_hbm.at[0], lat_raw, loc_sem.at[0])]
    for cp in loads:
        cp.start()
    barrier = pltpu.get_barrier_semaphore()
    for d in OFFSETS:
        pl.semaphore_signal(barrier, inc=1, device_id=tm(d), device_id_type=MESH)
    for d in range(1, nc):
        pl.semaphore_signal(barrier, inc=1, device_id=xp(d), device_id_type=MESH)

    wloads = [[], []]
    for s, (src, dst) in enumerate(((w1, wv1), (w2, wv2))):
        for f in range(3):
            for a in range(3):
                wloads[s].append(
                    pltpu.make_async_copy(
                        src.at[f, a], dst.at[:, pl.ds((a * 3 + f) * Q, Q), :], w_sem.at[s * 9 + f * 3 + a]
                    )
                )
    for cp in wloads[0] + wloads[1]:
        cp.start()
    half = c // 2
    w3load = pltpu.make_async_copy(
        w3.at[:, :, :, :, pl.ds(pl.multiple_of(half * 128, 128), 256)], w3v, w_sem.at[18]
    )
    w3load.start()

    prm[...] = jnp.zeros_like(prm)
    for r, ref in enumerate((gamma1, beta1, bias1, gamma2, beta2, bias2, bias3)):
        prm[r : r + 1, 0:Q] = ref[...]

    zero = jnp.zeros((3, C, W), BF)
    x3[:, :, 0:W] = zero
    x3[:, :, W + CELLS : 2 * W + CELLS] = zero
    tmp[...] = jnp.zeros_like(tmp)
    for cp in loads:
        cp.wait()
    lat32[...] = lat_raw[...].astype(F32).reshape(Q * H, W)

    def frame_sums(slot, p1, p2):
        tmp[0:Q, :] = p1
        s1 = jnp.sum(tmp[...].T, axis=0, keepdims=True)
        tmp[0:Q, :] = p2
        s2 = jnp.sum(tmp[...].T, axis=0, keepdims=True)
        st_send[slot] = jnp.concatenate([s1, s2, jnp.zeros((6, 128), F32)], 0)

    p1 = jnp.zeros((Q, W), F32)
    p2 = jnp.zeros((Q, W), F32)
    for i in range(H):
        row = lat32[pl.ds(i, Q, stride=H), :]
        p1 = p1 + row
        p2 = p2 + row * row
        fr[0, 2, :, i * W : (i + 1) * W] = row.astype(BF)
    frame_sums(0, p1, p2)
    colp[...] = prm[...].T

    def prep_conv(src, dst):
        for b in range(3):
            turned = src[b].T
            for q in range(nc):
                place = lax.rem(q - c + 2 + nc, nc) * 3 + b
                dst[pl.ds(pl.multiple_of(place * Q, Q), Q), :] = turned[q * Q : (q + 1) * Q]

    pl.semaphore_wait(barrier, len(OFFSETS) + nc - 1)

    def stats_copies(s):
        return [
            remote(st_send.at[s], st_recv.at[s, k], ss_sem.at[s, k], sr_sem.at[s, k], tm(d))
            for k, d in enumerate(OFFSETS)
        ]

    sibling = (t + 1 - 2 * core, c)

    def lanes(ch):
        return pl.ds(pl.multiple_of(ch * CW, CW), CW)

    def halo_copy(s, ch):
        return remote(
            fr.at[s, 2, :, lanes(ch)], fr.at[s, 0, :, lanes(ch)], hs_sem.at[s, 0, ch], hr_sem.at[s, 0, ch], tm(2)
        )

    def halo_across(s, ch):
        return remote(
            fr.at[s, 2 - 2 * core, :, lanes(ch)],
            fr.at[s, 1, :, lanes(ch)],
            hs_sem.at[s, 1, ch],
            hr_sem.at[s, 1, ch],
            sibling,
        )

    own_clip = clip[t]
    valid = []
    for d in (2, 1):
        src = lax.rem(t - d + nt, nt)
        valid.append(jnp.where((t - d >= 0) & (clip[src] == own_clip), 1.0, 0.0).astype(F32))
    valid.append(jnp.float32(1.0))

    lane = lax.broadcasted_iota(jnp.int32, (128, 128), 1)
    subl = lax.broadcasted_iota(jnp.int32, (128, 128), 0)
    ga = jnp.floor((subl.astype(F32) + 0.5) * (1.0 / PER_GROUP))
    gb = jnp.floor((lane.astype(F32) + 0.5) * (1.0 / PER_GROUP))
    gmat = jnp.where(ga == gb, 1.0, 0.0).astype(F32)

    def norm_params(s):
        total = st_send[s]
        frames = jnp.float32(1.0)
        for k, d in enumerate(OFFSETS):
            arrived(st_recv.at[s, k], ss_sem.at[s, k], sr_sem.at[s, k])
            src = lax.rem(t - d + nt, nt)
            inside = (t - d >= 0) & (t - d < nt)
            m = jnp.where(inside & (clip[src] == own_clip), 1.0, 0.0).astype(F32)
            total = total + m * st_recv[s, k]
            frames = frames + m
        grouped = jnp.dot(total, gmat, precision=lax.Precision.HIGHEST, preferred_element_type=F32)
        tmp[0:8, :] = grouped
        cols = tmp[...].T
        count = frames * float(PER_GROUP * CELLS)
        mean = cols[0:Q, 0:1] / count
        var = cols[0:Q, 1:2] / count - mean * mean
        inv = lax.rsqrt(var + EPSILON)
        return mean, inv * colp[0:Q, 3 * s : 3 * s + 1], colp[0:Q, 3 * s + 1 : 3 * s + 2]

    def fill_rows(s, f, ch, params):
        for r in range(2):
            cells = pl.ds(pl.multiple_of(ch * CW + r * W, W), W)
            v = fr[s, f, :, cells].astype(F32)
            u = (v - params[0]) * params[1] + params[2]
            u = u / (1.0 + jnp.exp(-u))
            if f < 2:
                u = u * valid[f]
            u = u.astype(BF)
            for a in range(3):
                o = r + 1 - a
                k = (a * 3 + f) * Q
                act[ch + 1 + o // 2, k : k + Q, (o % 2) * W : (o % 2 + 1) * W] = u

    first = lax.broadcasted_iota(jnp.int32, (Q, W), 1) == 0
    last = lax.broadcasted_iota(jnp.int32, (Q, W), 1) == W - 1
    low = slice(0, HQ)
    high = slice(HQ, Q)

    def ring_copy(s, kind, way, ch):
        if kind == 0:
            src = sb.at[s, ch, 0, high if way else low]
        elif kind == 1:
            src = sb.at[s, ch, 1, low] if way else sb.at[s, ch, 3, high]
        else:
            src = added.at[s, ch, way]
        return remote(
            src, rb.at[s, ch, kind, way], rs_sem.at[s, kind, way, ch], rr_sem.at[s, kind, way, ch], xp(3 if way else 1)
        )

    def ring_arrived(s, kind, way, ch):
        arrived(rb.at[s, ch, kind, way], rs_sem.at[s, kind, way, ch], rr_sem.at[s, kind, way, ch])

    def ring_add(s, ch):
        for way in range(2):
            ring_arrived(s, 0, way, ch)
            mine = sb[s, ch, 1, high] if way else sb[s, ch, 3, low]
            added[s, ch, way] = (mine.astype(F32) + rb[s, ch, 0, way].astype(F32)).astype(BF)
            ring_copy(s, 2, way, ch).start()

    def conv(s, wt, params):
        params = [jnp.broadcast_to(p, (Q, W)) for p in params]
        for ch in range(NCH):
            fill_rows(s, 2, ch, params)

        def contribute(lo, hi, ch):
            yb[lo * 3 * Q : hi * 3 * Q, :] = jnp.dot(
                wt[lo * 3 * Q : hi * 3 * Q, :], act[ch + 1], preferred_element_type=F32
            )
            for p in range(lo, hi):
                base = p * 3 * Q
                for h in range(2):
                    cells = slice(h * W, (h + 1) * W)
                    left = jnp.where(first, 0.0, pltpu.roll(yb[base : base + Q, cells], 1, 1))
                    right = jnp.where(last, 0.0, pltpu.roll(yb[base + 2 * Q : base + 3 * Q, cells], W - 1, 1))
                    sb[s, ch, p, :, cells] = (yb[base + Q : base + 2 * Q, cells] + left + right).astype(BF)
            for way in range(2):
                ring_copy(s, lo, way, ch).start()

        def chunk(step, carry):
            @pl.when(step < NCH)
            def _():
                arrived(fr.at[s, 0, :, lanes(step)], hs_sem.at[s, 0, step], hr_sem.at[s, 0, step])
                halo_across(s, step).start()
                fill_rows(s, 0, step, params)

            @pl.when((step >= 1) & (step < NCH + 1))
            def _():
                ch = step - 1
                arrived(fr.at[s, 1, :, lanes(ch)], hs_sem.at[s, 1, ch], hr_sem.at[s, 1, ch])
                fill_rows(s, 1, ch, params)

            @pl.when((step >= 2) & (step < NCH + 2))
            def _():
                contribute(0, 1, step - 2)

            @pl.when((step >= LAG_R) & (step < NCH + LAG_R))
            def _():
                contribute(1, 4, step - LAG_R)

            @pl.when(step >= LAG_S)
            def _():
                ring_add(s, step - LAG_S)

            return carry

        lax.fori_loop(0, NCH + LAG_S, chunk, 0)

    def gathered(s, ch):
        for kind in (1, 2):
            for way in range(2):
                ring_arrived(s, kind, way, ch)
        own = sb[s, ch, 2].astype(F32)
        top = own[low] + rb[s, ch, 2, 0].astype(F32) + rb[s, ch, 1, 1].astype(F32)
        bottom = own[high] + rb[s, ch, 1, 0].astype(F32) + rb[s, ch, 2, 1].astype(F32)
        return jnp.concatenate([top, bottom], 0) + colp[0:Q, 3 * s + 2 : 3 * s + 3]

    offset = pl.multiple_of(c * Q - half * 128, 32)

    def prep_three(f):
        taps = {}
        for a in range(3):
            for b in range(3):
                t3[a * 3 + b] = w3v[f, a, b].T
        m = valid[f]

        def tap(a, b):
            return t3[a * 3 + b, pl.ds(offset, Q), :].astype(F32)

        for pi in range(2):
            for block, di in enumerate((0, 1) if pi else (0, -1)):
                rows = ((0, 1), (2,))[block] if pi else ((1, 2), (0,))[block]
                sums = []
                for b in range(3):
                    v = tap(rows[0], b)
                    for a in rows[1:]:
                        v = v + tap(a, b)
                    sums.append(v * m if f < 2 else v)
                parts = (sums[0], sums[1] + sums[2], sums[0] + sums[1], sums[2])
                for k, part in enumerate(parts):
                    base = ((pi * 2 + block) * 4 + k) * Q
                    wf[base : base + Q, f * C : (f + 1) * C] = part.astype(BF)

    for cp in stats_copies(0):
        cp.start()
    for ch in range(NCH):
        halo_copy(0, ch).start()
    act[...] = jnp.zeros_like(act)
    for dst in (wv1, wv2):
        dst[:, 9 * Q : KP, :] = jnp.zeros((3, KP - 9 * Q, C), BF)
    er = lax.broadcasted_iota(jnp.int32, (2 * W, 2 * W), 0)
    ec = lax.broadcasted_iota(jnp.int32, (2 * W, 2 * W), 1)
    perm[...] = jnp.where(jnp.where(er < W, 2 * er, 2 * er - 2 * W + 1) == ec, 1.0, 0.0).astype(BF)
    for cp in wloads[0]:
        cp.wait()
    prep_conv(wv1, wt1)
    for cp in wloads[1]:
        cp.wait()
    prep_conv(wv2, wt2)
    w3load.wait()
    for f in range(3):
        prep_three(f)
    params = norm_params(0)
    conv(0, wt1, params)
    p1 = jnp.zeros((Q, W), F32)
    p2 = jnp.zeros((Q, W), F32)
    for ch in range(NCH):
        hidden = gathered(0, ch).astype(BF)
        fr[1, 2, :, ch * CW : (ch + 1) * CW] = hidden
        if ch < 2:
            halo_copy(1, ch).start()
        hidden = hidden.astype(F32)
        for h in range(2):
            row = hidden[:, h * W : (h + 1) * W]
            p1 = p1 + row
            p2 = p2 + row * row
    frame_sums(1, p1, p2)
    for cp in stats_copies(1):
        cp.start()
    for ch in range(2, NCH):
        halo_copy(1, ch).start()

    def sent(s):
        for cp in stats_copies(s):
            cp.wait_send()
        for ch in range(NCH):
            halo_copy(s, ch).wait_send()
            halo_across(s, ch).wait_send()

    sent(0)
    for ch in range(NCH):
        for kind in range(3):
            for way in range(2):
                ring_copy(0, kind, way, ch).wait_send()

    params = norm_params(1)
    conv(1, wt2, params)
    sent(1)

    def lanes_of(ch):
        return pl.ds(W + ch * CW, CW)

    def own_x(d, ch):
        spot = x3.at[2, quarter(0), lanes_of(ch)]
        return remote(spot, spot, as_sem.at[d - 1, ch], ar_sem.at[d - 1, ch], xp(d))

    def half_quarter(d, part):
        return pl.ds(pl.multiple_of(lax.rem(c + d, nc) * Q + part * HQ, HQ), HQ)

    def own_z(k, ch):
        return remote(
            x3.at[2, quarter(2 * k), lanes_of(ch)],
            x3.at[0, quarter(2 * k), lanes_of(ch)],
            zs_sem.at[k, ch],
            zr_sem.at[k, ch],
            tm(2),
        )

    def back_x(d, ch):
        spot = x3.at[0, quarter(0), lanes_of(ch)]
        return remote(spot, spot, xs_sem.at[d // 2, ch], xr_sem.at[d // 2, ch], xp(d))

    def across(ch):
        return remote(
            x3.at[2 - 2 * core, :, lanes_of(ch)],
            x3.at[1, :, lanes_of(ch)],
            bs_sem.at[ch],
            br_sem.at[ch],
            sibling,
        )

    bias = colp[0:Q, 6:7]

    def rows_of(f0, f1, ch, di):
        lanes = pl.ds((1 + di) * W + ch * CW, CW)
        return x3[f0:f1, :, lanes].reshape((f1 - f0) * C, CW)

    def partial(pi, f0, f1, ch):
        base = pi * 8 * Q
        k = slice(f0 * C, f1 * C)
        mid = jnp.dot(wf[base : base + C, k], rows_of(f0, f1, ch, 0), preferred_element_type=F32)
        edge = rows_of(f0, f1, ch, 1 if pi else -1)
        return mid + jnp.dot(wf[base + C : base + 2 * C, k], edge, preferred_element_type=F32)

    def result_copy(block):
        lines = pl.ds(block * H, H)
        return pltpu.make_async_copy(done.at[block], out.at[0, :, lines, :], loc_sem.at[1 + block])

    def static_when(condition):
        return lambda block: block() if condition else None

    def pipeline(step, carry):
        @static_when(step < NCH)
        def _():
            ch = step
            cells = pl.ds(ch * CW, CW)
            residual = fr[0, 2, :, cells].astype(F32) + gathered(1, ch)
            x3[2, quarter(0), lanes_of(ch)] = residual.astype(BF)
            own_z(0, ch).start()
            for d in (2, 1, 3):
                own_x(d, ch).start()

        @static_when((step >= LAG_K) and (step < NCH + LAG_K))
        def _():
            ch = step - LAG_K
            arrived(x3.at[0, quarter(0), lanes_of(ch)], zs_sem.at[0, ch], zr_sem.at[0, ch])
            for d in (1, 3):
                back_x(d, ch).start()

        @static_when((step >= LAG_P) and (step < NCH + LAG_P))
        def _():
            ch = step - LAG_P
            arrived(x3.at[2, quarter(2), lanes_of(ch)], as_sem.at[1, ch], ar_sem.at[1, ch])
            own_z(1, ch).start()
            for d in (1, 3):
                arrived(x3.at[2, quarter(4 - d), lanes_of(ch)], as_sem.at[d - 1, ch], ar_sem.at[d - 1, ch])
            for kind in range(3):
                for way in range(2):
                    ring_copy(1, kind, way, ch).wait_send()
            for d in (1, 2, 3):
                own_x(d, ch).wait_send()
            own_z(0, ch).wait_send()

        @static_when((step >= LAG_C) and (step < NCH + LAG_C))
        def _():
            ch = step - LAG_C
            for d in (1, 3):
                arrived(x3.at[0, quarter(4 - d), lanes_of(ch)], xs_sem.at[d // 2, ch], xr_sem.at[d // 2, ch])
            arrived(x3.at[0, quarter(2), lanes_of(ch)], zs_sem.at[1, ch], zr_sem.at[1, ch])
            across(ch).start()

        @static_when((step >= LAG_O) and (step < NCH + LAG_O))
        def _():
            ch = step - LAG_O
            for pi in range(2):
                y3[ch, pi] = partial(pi, 2, 3, ch)

        @static_when((step >= LAG_D) and (step < NCH + LAG_D))
        def _():
            ch = step - LAG_D
            for d in (1, 3):
                back_x(d, ch).wait_send()
            own_z(1, ch).wait_send()
            arrived(x3.at[1, :, lanes_of(ch)], bs_sem.at[ch], br_sem.at[ch])

        @static_when((step >= LAG_E) and (step < NCH + LAG_E))
        def _():
            ch = step - LAG_E
            for pi in range(2):
                y3[ch, pi] += partial(pi, 0, 2, ch)
                for h in range(2):
                    cells = slice(h * W, (h + 1) * W)
                    left = jnp.where(first, 0.0, pltpu.roll(y3[ch, pi, 0:Q, cells], 1, 1))
                    right = jnp.where(last, 0.0, pltpu.roll(y3[ch, pi, 3 * Q : 4 * Q, cells], W - 1, 1))
                    rows = slice((2 * h + pi) * Q, (2 * h + pi + 1) * Q)
                    both[rows, 0:W] = (y3[ch, pi, Q : 2 * Q, cells] + left + bias).astype(BF)
                    both[rows, W : 2 * W] = (y3[ch, pi, 2 * Q : 3 * Q, cells] + right + bias).astype(BF)
            spread = jnp.dot(both[...], perm[...], preferred_element_type=F32)
            for k in range(4):
                for g in range(2):
                    oscr[ch // 2, g, pl.ds((ch % 2) * 4 + k, Q, stride=H), :] = spread[k * Q : (k + 1) * Q, g * 128 : (g + 1) * 128]

            @static_when(ch % 2 == 1)
            def _():
                block = ch // 2
                for g in range(2):
                    lines = oscr[block, g].reshape(Q, H, 128)
                    done[block, :, :, g * 128 : (g + 1) * 128] = lines.astype(BF)
                result_copy(block).start()

        return carry

    for step in range(NCH + LAG_E):
        pipeline(step, 0)
    for ch in range(NCH):
        across(ch).wait_send()
    for block in range(2):
        result_copy(block).wait()


def on_device(nt, nc, *args):
    args = [a.reshape(1, Q) if a.ndim == 1 and a.dtype == F32 else a for a in args]
    anywhere = pl.BlockSpec(memory_space=pl.ANY)
    specs = [pl.BlockSpec(memory_space=pltpu.VMEM) if a.ndim == 2 else anywhere for a in args]
    specs[1] = pl.BlockSpec(memory_space=pltpu.SMEM)
    dma = pltpu.SemaphoreType.DMA
    scratch = [
        pltpu.VMEM((Q, H, W), BF),
        pltpu.VMEM((Q * H, W), F32),
        pltpu.VMEM((2, 3, Q, CELLS), BF),
        pltpu.VMEM((128, 128), F32),
        pltpu.VMEM((128, 128), F32),
        pltpu.VMEM((128, 128), F32),
        pltpu.VMEM((2, 8, 128), F32),
        pltpu.VMEM((2, len(OFFSETS), 8, 128), F32),
        pltpu.VMEM((3, KP, C), BF),
        pltpu.VMEM((3, KP, C), BF),
        pltpu.VMEM((3 * C, KP), BF),
        pltpu.VMEM((3 * C, KP), BF),
        pltpu.VMEM((3, 3, 3, C, 256), BF),
        pltpu.VMEM((9, 256, C), BF),
        pltpu.VMEM((16 * Q, 3 * C), BF),
        pltpu.VMEM((NCH + 2, KP, CW), BF),
        pltpu.VMEM((3 * C, CW), F32),
        pltpu.VMEM((2, NCH, 4, Q, CW), BF),
        pltpu.VMEM((2, NCH, 2, HQ, CW), BF),
        pltpu.VMEM((2, NCH, 3, 2, HQ, CW), BF),
        pltpu.VMEM((3, C, CELLS + 2 * W), BF),
        pltpu.VMEM((NCH, 2, C, CW), F32),
        pltpu.VMEM((C, 2 * W), BF),
        pltpu.VMEM((2 * W, 2 * W), BF),
        pltpu.VMEM((2, 2, Q * H, 128), F32),
        pltpu.VMEM((2, Q, H, 2 * W), BF),
        dma((3,)),
        dma((19,)),
        dma((2, 2, NCH)),
        dma((2, 2, NCH)),
        dma((2, len(OFFSETS))),
        dma((2, len(OFFSETS))),
        dma((2, 3, 2, NCH)),
        dma((2, 3, 2, NCH)),
        dma((3, NCH)),
        dma((3, NCH)),
        dma((2, NCH)),
        dma((2, NCH)),
        dma((2, NCH)),
        dma((2, NCH)),
        dma((NCH,)),
        dma((NCH,)),
    ]
    return pl.pallas_call(
        functools.partial(kernel, nt, nc),
        out_shape=jax.ShapeDtypeStruct((1, Q, 2 * H, 2 * W), BF),
        in_specs=specs,
        out_specs=pl.BlockSpec(memory_space=pl.ANY),
        scratch_shapes=scratch,
        compiler_params=pltpu.CompilerParams(
            collective_id=0, has_side_effects=True, vmem_limit_bytes=60 * 1024 * 1024
        ),
    )(*args)


def solution(mesh):
    in_specs = (
        P("tm", "chan", None, None),
        P(),
        P("chan"),
        P("chan"),
        P(None, None, None, "chan", None),
        P("chan"),
        P("chan"),
        P("chan"),
        P(None, None, None, "chan", None),
        P("chan"),
        P(),
        P("chan"),
    )
    return jax.shard_map(
        functools.partial(on_device, mesh.shape["tm"], mesh.shape["chan"]),
        mesh=mesh,
        in_specs=in_specs,
        out_specs=P("tm", "chan", None, None),
        check_vma=False,
    )
```
